512 devices in a mesh: gx: 8 (over z_lo, core), gy: 4 (over z_hi), gz: 16 (over x, y).
Axes of the slice: x: 4, y: 4, z: 16 (z_hi: 4, z_lo: 4; z = z_hi * 4 + z_lo), core: 2. Of those that a mesh axis runs over, the one named last changes fastest.
Arguments:
- particles: float32 [28, 1048576], P(None, ('gx', 'gy', 'gz')), may hold values from -3 to 3, as said below
- stencil_base: int32 [3, 1048576], P(None, ('gx', 'gy', 'gz')), may hold values from 0 to 32, as said below
- weights: float32 [8, 1048576], P(None, ('gx', 'gy', 'gz')), may hold values from 0.02 to 0.25
- gradients: float32 [3, 8, 1048576], P(None, None, ('gx', 'gy', 'gz')), may hold values from -4 to 4
- counts: int32 [512], P(('gx', 'gy', 'gz')), may hold values from 0 to 8, as said below
Outputs:
- migrated: float32 [28, 1572864], P(None, ('gx', 'gy', 'gz'))
- damage: float32 [64, 64, 512], P('gx', 'gy', 'gz')
The draws below stay inside these ranges and needn't reach their ends.
Inputs may be any that keep to these rules, and one draw needn't show every extreme that they name: `particles`: mass and volume in 0.5 to 2, deformation gradient entries within 0.1 of the identity's, damage in 0 to 0.5, history in 0.05 to 1. `stencil_base`: row 0 lies in 0 to 8, row 1 in 0 to 16, row 2 in 0 to 32. `counts`: some device hands exactly 8 bins.
All inputs are finite; a program needn't handle non-finite values.
Results may differ from the reference program's by a relative error of at most 0.0003.
Values sent between devices are 32-bit elements; how exact they have to be, the bound alone decides.
No kernel may reach another device: no remote copies, remote signals or barrier semaphores. Data moves between devices by JAX's collectives and lax.ppermute only.
A program may use at most 64 MiB of HBM per device.

```python
import math
import jax
import jax.numpy as jnp
from jax import lax

CX = 8
CY = 16
CZ = 32
NBIN = 16
BIN = 128
SUBSTEPS = 4
FIELDS = 28
MOST = 8
RANKS = 512
PARTICLES = 1048576
NX = 64
NY = 64
NZ = 512
N_GX = 8
N_GY = 4
N_GZ = 16


def draw_particles(key, part):
    keys = jax.random.split(key, 7)
    count = PARTICLES
    scales = jnp.exp(jax.random.uniform(keys[0], (2, count), jnp.float32, math.log(0.5), math.log(2.0)))
    velocity = jnp.clip(0.5 * jax.random.normal(keys[1], (3, count), jnp.float32), -2.0, 2.0)
    stress = jnp.clip(0.5 * jax.random.normal(keys[3], (9, count), jnp.float32), -3.0, 3.0)
    deform = jnp.eye(3, dtype=jnp.float32).reshape(9, 1) + jax.random.uniform(keys[2], (9, count), jnp.float32, -0.1, 0.1)
    damage = jax.random.uniform(keys[4], (1, count), jnp.float32, 0.0, 0.5)
    history = jnp.exp(jax.random.uniform(keys[5], (1, count), jnp.float32, math.log(0.05), 0.0))
    position = jax.random.uniform(keys[6], (3, count), jnp.float32, 0.0, 1.0)
    return jnp.concatenate([scales, velocity, deform, stress, damage, history, position], axis=0)


def draw_stencil_base(key, part):
    keys = jax.random.split(key, 3)
    row_x = jax.random.randint(keys[0], (PARTICLES,), 0, CX + 1)
    row_y = jax.random.randint(keys[1], (PARTICLES,), 0, CY + 1)
    row_z = jax.random.randint(keys[2], (PARTICLES,), 0, CZ + 1)
    return jnp.stack([row_x, row_y, row_z]).astype(jnp.int32)


def draw_counts(key, part):
    values = jax.random.randint(key, (RANKS,), 0, MOST + 1)
    chosen = jax.random.randint(jax.random.fold_in(key, 7), (), 0, RANKS)
    return values.at[chosen].set(MOST).astype(jnp.int32)


def level_of(key, shape, cuts, low, top_value):
    def one(axis_at, shards_of):
        draws = jax.random.uniform(jax.random.fold_in(jax.random.fold_in(key, 6), axis_at), (shards_of,), jnp.float32, low / len(cuts), top_value / len(cuts))
        return jnp.repeat(jnp.exp(draws), shape[axis_at] // shards_of).reshape((-1,) + (1,) * (len(shape) - axis_at - 1))

    level = one(*cuts[0])
    for cut in cuts[1:]:
        level = level * one(*cut)
    return level


def noise(key, dims, scale, most, shards=(), kind=jnp.bfloat16):
    result = scale * jax.random.normal(key, dims, jnp.float32)
    if shards:
        result = result * level_of(key, dims, shards, -0.22, 0.18)
    return jnp.clip(result, -most, most).astype(kind)


def setup_inputs(seed: int = 0) -> dict:
    splits = jax.random.split(jax.random.key(seed), 6)
    particles = draw_particles(jax.random.fold_in(splits[5], 71), 0)
    stencil_base = draw_stencil_base(jax.random.fold_in(splits[5], 71), 0)
    weights = jnp.clip(0.02 + 0.23 * jax.random.uniform(splits[2], (8, PARTICLES), jnp.float32) ** level_of(splits[2], (8, PARTICLES), ((1, 512),), -0.2, 0.2), 0.02, 0.25)
    gradients = noise(splits[3], (3, 8, PARTICLES), 1.0, 4.0, ((2, 512),), jnp.float32)
    counts = draw_counts(jax.random.fold_in(splits[5], 71), 0)
    return {"particles": particles, "stencil_base": stencil_base, "weights": weights, "gradients": gradients, "counts": counts}


time_step = 0.1
relax_rate = 0.2
length_sq = 0.6
shear_mod = 1.0
bulk_coef = 1.5
mass_floor = 0.5


def corner_offsets(corner):
    return (corner >> 2) & 1, (corner >> 1) & 1, corner & 1


def node_terms(particles, weights, gradients, corner):
    volume = particles[1]
    velocity = particles[2:5]
    stress = particles[14:23].reshape(3, 3, -1)
    share = particles[0] * weights[corner]
    slope = gradients[:, corner]
    force = -volume[None] * jnp.sum(stress * slope[None], axis=1)
    return jnp.concatenate([share[None], share[None] * velocity, force, (share * particles[23])[None], (share * particles[24])[None]], axis=0)


def relax(padded, drive):
    centre = padded[1:-1, 1:-1, 1:-1]
    laplace = (padded[2:, 1:-1, 1:-1] + padded[:-2, 1:-1, 1:-1] + padded[1:-1, 2:, 1:-1] + padded[1:-1, :-2, 1:-1] + padded[1:-1, 1:-1, 2:] + padded[1:-1, 1:-1, :-2]) - 6.0 * centre
    return centre + relax_rate * (length_sq * laplace - centre + 2.0 * (1.0 - centre) * drive)


def advance(particles, near_velocity, near_damage, weights, gradients):
    moved = [jnp.sum(weights * near_velocity[i], axis=0) for i in range(3)]
    velgrad = [[jnp.sum(near_velocity[i] * gradients[j], axis=0) for j in range(3)] for i in range(3)]
    damage_node = jnp.sum(weights * near_damage, axis=0)
    deform = [[particles[5 + 3 * i + j] for j in range(3)] for i in range(3)]
    stretch = [[(1.0 if i == j else 0.0) + time_step * velgrad[i][j] for j in range(3)] for i in range(3)]
    mapped = [[stretch[i][0] * deform[0][j] + stretch[i][1] * deform[1][j] + stretch[i][2] * deform[2][j] for j in range(3)] for i in range(3)]
    jacobian = (mapped[0][0] * (mapped[1][1] * mapped[2][2] - mapped[1][2] * mapped[2][1])
                - mapped[0][1] * (mapped[1][0] * mapped[2][2] - mapped[1][2] * mapped[2][0])
                + mapped[0][2] * (mapped[1][0] * mapped[2][1] - mapped[1][1] * mapped[2][0]))
    left = [[mapped[i][0] * mapped[j][0] + mapped[i][1] * mapped[j][1] + mapped[i][2] * mapped[j][2] for j in range(3)] for i in range(3)]
    damaged = jnp.maximum(particles[23], damage_node)
    degrade = (1.0 - damaged) ** 2
    rows_out = []
    for i in range(3):
        for j in range(3):
            term = shear_mod * (left[i][j] - (1.0 if i == j else 0.0))
            if i == j:
                term = term + bulk_coef * (jacobian - 1.0)
            rows_out.append(degrade * term)
    energy = 0.5 * shear_mod * (left[0][0] + left[1][1] + left[2][2] - 3.0) + 0.5 * bulk_coef * (jacobian - 1.0) ** 2
    history = jnp.maximum(particles[24], energy)
    position = particles[25:28] + time_step * jnp.stack(moved)
    flat_mapped = jnp.stack([mapped[i][j] for i in range(3) for j in range(3)])
    return jnp.concatenate([particles[0:2], jnp.stack(moved), flat_mapped, jnp.stack(rows_out), damaged[None], history[None], position], axis=0)


def assemble(own, tail, own_count, prior):
    buffer_all = jnp.concatenate([tail, own, jnp.zeros((own.shape[0], MOST * BIN), own.dtype)], axis=1)
    start = ((MOST - prior) * BIN).astype(jnp.int32)
    window = lax.dynamic_slice_in_dim(buffer_all, start, (NBIN + MOST) * BIN, 1)
    live = (NBIN - own_count + prior) * BIN
    slot = jnp.arange((NBIN + MOST) * BIN, dtype=jnp.int32)
    return jnp.where(slot[None, :] < live, window, jnp.zeros_like(window))


def reference(particles, stencil_base, weights, gradients, counts):
    per_device = NBIN * BIN
    span_y = NY + 2
    span_z = NZ + 2
    base = stencil_base.reshape(3, N_GX, N_GY, N_GZ, per_device)
    row_x = base[0] + (jnp.arange(N_GX, dtype=jnp.int32) * CX)[:, None, None, None]
    row_y = base[1] + (jnp.arange(N_GY, dtype=jnp.int32) * CY)[None, :, None, None]
    row_z = base[2] + (jnp.arange(N_GZ, dtype=jnp.int32) * CZ)[None, None, :, None]
    flats = []
    terms = []
    for corner in range(8):
        offset_x, offset_y, offset_z = corner_offsets(corner)
        flat_index = (((row_x + offset_x) * span_y + row_y + offset_y) * span_z + row_z + offset_z).reshape(-1).astype(jnp.int32)
        flats.append(flat_index)
        terms.append(node_terms(particles, weights, gradients, corner))
    all_index = jnp.concatenate(flats)
    grid_sum = jnp.zeros((9, (NX + 2) * span_y * span_z), jnp.float32).at[:, all_index].add(jnp.concatenate(terms, axis=1))
    owned = grid_sum.reshape(9, NX + 2, span_y, span_z)[:, 1:-1, 1:-1, 1:-1]
    masses = jnp.maximum(owned[0], mass_floor)
    velocity = (owned[1:4] + time_step * owned[4:7]) / masses[None]
    damage = owned[7] / masses
    drive = owned[8] / masses
    for step in range(SUBSTEPS):
        damage = relax(jnp.pad(damage, 1), drive)
    fields = jnp.pad(jnp.concatenate([velocity, damage[None]], axis=0), ((0, 0), (1, 1), (1, 1), (1, 1))).reshape(4, -1)
    near = fields[:, all_index].reshape(4, 8, PARTICLES)
    updated = advance(particles, near[0:3], near[3], weights, gradients)
    lines = N_GX * N_GY
    grouped = updated.reshape(FIELDS, lines, N_GZ, per_device)
    earlier = jnp.roll(grouped, 1, axis=2)
    tails = earlier[..., (NBIN - MOST) * BIN:]
    count_grid = counts.reshape(lines, N_GZ)
    prior = jnp.roll(count_grid, 1, axis=1)
    owns = jnp.transpose(grouped, (1, 2, 0, 3)).reshape(lines * N_GZ, FIELDS, per_device)
    tail_rows = jnp.transpose(tails, (1, 2, 0, 3)).reshape(lines * N_GZ, FIELDS, MOST * BIN)
    placed = jax.vmap(assemble)(owns, tail_rows, count_grid.reshape(-1), prior.reshape(-1))
    migrated = jnp.transpose(placed, (1, 0, 2)).reshape(FIELDS, -1)
    return migrated, damage
```

```python
import jax
import jax.numpy as jnp
from jax import lax
from jax.experimental import pallas as pl
from jax.experimental.pallas import tpu as pltpu
from jax.sharding import PartitionSpec as P

CX = 8
CY = 16
CZ = 32
NBIN = 16
BIN = 128
SUBSTEPS = 4
FIELDS = 28
MOST = 8
COUNT = NBIN * BIN
TAIL = MOST * BIN
SLOTS = (NBIN + MOST) * BIN

time_step = 0.1
relax_rate = 0.2
length_sq = 0.6
shear_mod = 1.0
bulk_coef = 1.5
mass_floor = 0.5

EX = CX + 2
EY = CY + 2
WIDE = SUBSTEPS + 1
LAYERS = WIDE + 1
SX = CX + 2 * WIDE
SY = CY + 2 * WIDE
SZ = CZ + 2 * WIDE
OFF = WIDE - 1
PITCH = 32
AROWS = 176
GROWS = 200
GROUP = 40
ZROWS = 40
CHUNK = 256
F32 = jnp.float32
BF16 = jnp.bfloat16
VMEM = pltpu.VMEM
VMEM_LIMIT = 48 * 1024 * 1024


def shift_lanes(value, by):
    by = by % 128
    return value if by == 0 else pltpu.roll(value, by, 1)


def lane_index(rows):
    return lax.broadcasted_iota(jnp.int32, (rows, 128), 1)


def onehot_rows(base_ref, lanes):
    xy = base_ref[0:1, lanes] * EY + base_ref[1:2, lanes]
    rows = lax.broadcasted_iota(jnp.int32, (AROWS, CHUNK), 0)
    return jnp.where(rows == xy, 1.0, 0.0).astype(BF16)


def scatter_kernel(counts_ref, part_ref, base_ref, w_ref, g_ref, deep_ref, vel_ref, low_ref, high_ref, acc_ref, sum_ref):
    acc_ref[...] = jnp.zeros_like(acc_ref)

    def step(index, carry):
        lanes = pl.ds(pl.multiple_of(index * CHUNK, CHUNK), CHUNK)
        mass = part_ref[0:1, lanes]
        minus_vol = -time_step * part_ref[1:2, lanes]
        share = mass * w_ref[:, lanes]
        slope = [g_ref[j, :, lanes] for j in range(3)]
        terms = [share, share * part_ref[23:24, lanes], share * part_ref[24:25, lanes]]
        for i in range(3):
            row = 14 + 3 * i
            pull = (
                part_ref[row : row + 1, lanes] * slope[0]
                + part_ref[row + 1 : row + 2, lanes] * slope[1]
                + part_ref[row + 2 : row + 3, lanes] * slope[2]
            )
            terms.append(share * part_ref[2 + i : 3 + i, lanes] + minus_vol * pull)
        high = [t.astype(BF16).astype(F32) for t in terms]
        low = [t - h for t, h in zip(terms, high)]
        base_z = base_ref[2:3, lanes]
        sub = lax.broadcasted_iota(jnp.int32, (8, CHUNK), 0) - base_z
        blocks = {}
        for tile in range(16):
            masks = []
            for ch in range(3):
                first, last = SZ * ch + OFF, SZ * ch + OFF + CZ + 1
                if first <= 8 * tile + 7 and last >= 8 * tile:
                    masks.append((ch, sub == first - 8 * tile, sub == first + 1 - 8 * tile))
            for corner in range(4):
                for half in range(2):
                    for part, source in enumerate((high, low)):
                        value = jnp.zeros((8, CHUNK), F32)
                        for ch, at, after in masks:
                            rows = source[3 * half + ch]
                            value = jnp.where(at, rows[2 * corner : 2 * corner + 1], value)
                            value = jnp.where(after, rows[2 * corner + 1 : 2 * corner + 2], value)
                        blocks[corner, half, part, tile] = value
        onehot = onehot_rows(base_ref, lanes)
        for corner in range(4):
            for half in range(2):
                total = None
                for part in range(2):
                    rhs = jnp.concatenate([blocks[corner, half, part, t] for t in range(16)], axis=0).astype(BF16)
                    piece = lax.dot_general(onehot, rhs, (((1,), (1,)), ((), ())), preferred_element_type=F32)
                    total = piece if total is None else total + piece
                at = 128 * (2 * corner + half)
                acc_ref[:, at : at + 128] += total
        return carry

    lax.fori_loop(0, COUNT // CHUNK, step, 0)
    sum_ref[...] = jnp.zeros_like(sum_ref)
    for corner in range(4):
        shift = (corner >> 1) * EY + (corner & 1)
        sum_ref[shift : shift + AROWS, :] += acc_ref[:, 256 * corner : 256 * corner + 256]
    deep_ref[...] = sum_ref[:, 0:128]
    vel_ref[...] = sum_ref[:, 128:256]
    lane = lane_index(GROUP)
    low_msg = jnp.zeros((GROUP, 128), F32)
    high_msg = jnp.zeros((GROUP, 128), F32)
    for j in range(5):
        deep = sum_ref[GROUP * j : GROUP * (j + 1), 0:128]
        vel = sum_ref[GROUP * j : GROUP * (j + 1), 128:256]
        for ch in range(3):
            to = 24 * j + LAYERS * ch
            inside = (lane >= to) & (lane < to + LAYERS)
            low_msg = jnp.where(inside, shift_lanes(deep, to - (SZ * ch + OFF)), low_msg)
            high_msg = jnp.where(inside, shift_lanes(deep, to - (SZ * ch + CZ)), high_msg)
            to = 24 * j + 3 * LAYERS + 2 * ch
            inside = (lane >= to) & (lane < to + 2)
            low_msg = jnp.where(inside, shift_lanes(vel, to - (SZ * ch + OFF)), low_msg)
            high_msg = jnp.where(inside, shift_lanes(vel, to - (SZ * ch + OFF + CZ)), high_msg)
    low_ref[...] = low_msg
    high_ref[...] = jnp.where(lane >= 120, counts_ref[0].astype(F32), high_msg)


def join_z_kernel(place_ref, deep_ref, vel_ref, before_ref, after_ref, deep_out, vel_out, low_ref, high_ref):
    lane = lane_index(GROUP)
    before = jnp.where(place_ref[2] > 0, before_ref[...], 0.0)
    after = after_ref[...]
    for j in range(5):
        rows = slice(GROUP * j, GROUP * (j + 1))
        deep = jnp.zeros((GROUP, 128), F32)
        vel = jnp.zeros((GROUP, 128), F32)
        for ch in range(3):
            source = 24 * j + LAYERS * ch
            to = SZ * ch
            inside = (lane >= to) & (lane < to + LAYERS)
            deep = jnp.where(inside, shift_lanes(before, to - source), deep)
            to = SZ * ch + OFF + CZ
            inside = (lane >= to) & (lane < to + LAYERS)
            deep = jnp.where(inside, shift_lanes(after, to - source), deep)
            source = 24 * j + 3 * LAYERS + 2 * ch
            to = SZ * ch + OFF
            inside = (lane >= to) & (lane < to + 2)
            vel = jnp.where(inside, shift_lanes(before, to - source), vel)
            to = SZ * ch + OFF + CZ
            inside = (lane >= to) & (lane < to + 2)
            vel = jnp.where(inside, shift_lanes(after, to - source), vel)
        deep_out[rows, :] = deep_ref[rows, :] + deep
        vel_out[rows, :] = vel_ref[rows, :] + vel
    for x in range(EX):
        row = EY * x
        low_ref[LAYERS * x : LAYERS * (x + 1), :] = deep_out[row : row + LAYERS, :]
        high_ref[LAYERS * x : LAYERS * (x + 1), :] = deep_out[row + EY - LAYERS : row + EY, :]
        at = LAYERS * EX + 2 * x
        low_ref[at : at + 2, :] = vel_out[row : row + 2, :]
        high_ref[at : at + 2, :] = vel_out[row + EY - 2 : row + EY, :]


def join_y_kernel(deep_ref, vel_ref, before_ref, after_ref, deep_out, vel_out, low_ref, high_ref):
    deep_out[...] = jnp.zeros_like(deep_out)
    vel_out[...] = jnp.zeros_like(vel_out)
    for x in range(EX):
        row = EY * x
        deep_out[x, OFF : OFF + EY, :] = deep_ref[row : row + EY, :]
        deep_out[x, 0:LAYERS, :] += before_ref[LAYERS * x : LAYERS * (x + 1), :]
        deep_out[x, OFF + CY : OFF + CY + LAYERS, :] += after_ref[LAYERS * x : LAYERS * (x + 1), :]
        at = LAYERS * EX + 2 * x
        vel_out[x, OFF : OFF + EY, :] = vel_ref[row : row + EY, :]
        vel_out[x, OFF : OFF + 2, :] += before_ref[at : at + 2, :]
        vel_out[x, OFF + CY : OFF + CY + 2, :] += after_ref[at : at + 2, :]
    for x in range(LAYERS):
        low_ref[SY * x : SY * (x + 1), :] = deep_out[x, 0:SY, :]
        high_ref[SY * x : SY * (x + 1), :] = deep_out[EX - LAYERS + x, 0:SY, :]
    for x in range(2):
        at = SY * LAYERS + EY * x
        low_ref[at : at + EY, :] = vel_out[x, OFF : OFF + EY, :]
        high_ref[at : at + EY, :] = vel_out[EX - 2 + x, OFF : OFF + EY, :]


def gather_update(index, nodes_ref, part_ref, base_ref, w_ref, g_ref, out_ref, out_index):
    lanes = pl.ds(pl.multiple_of(index * CHUNK, CHUNK), CHUNK)
    to = pl.ds(pl.multiple_of(out_index * CHUNK, CHUNK), CHUNK)
    onehot = onehot_rows(base_ref, lanes)
    base_z = base_ref[2:3, lanes]
    rows = lax.broadcasted_iota(jnp.int32, (ZROWS, CHUNK), 0) - base_z
    at = rows == 0
    after = rows == 1

    def pick(mask, value):
        kept = jnp.where(mask, value, 0.0)
        total = kept[0:8]
        for t in range(1, ZROWS // 8):
            total = total + kept[8 * t : 8 * t + 8]
        return total

    moved = [jnp.zeros((8, CHUNK), F32) for _ in range(3)]
    velgrad = [[jnp.zeros((8, CHUNK), F32) for _ in range(3)] for _ in range(3)]
    damage_node = jnp.zeros((8, CHUNK), F32)
    rows_ab = 4 * ZROWS
    for corner in range(4):
        start = 2 * rows_ab * corner
        near = jnp.dot(nodes_ref[start : start + rows_ab, 0:AROWS], onehot, preferred_element_type=F32) + jnp.dot(
            nodes_ref[start + rows_ab : start + 2 * rows_ab, 0:AROWS], onehot, preferred_element_type=F32
        )
        for c, mask in enumerate((at, after)):
            k = 2 * corner + c
            weight = w_ref[k : k + 1, lanes]
            slope = [g_ref[j, k : k + 1, lanes] for j in range(3)]
            for i in range(3):
                value = pick(mask, near[ZROWS * i : ZROWS * (i + 1)])
                moved[i] = moved[i] + value * weight
                for j in range(3):
                    velgrad[i][j] = velgrad[i][j] + value * slope[j]
            damage_node = damage_node + pick(mask, near[3 * ZROWS : 4 * ZROWS]) * weight
    moved = [jnp.sum(v, axis=0, keepdims=True) for v in moved]
    velgrad = [[jnp.sum(v, axis=0, keepdims=True) for v in row] for row in velgrad]
    damage_node = jnp.sum(damage_node, axis=0, keepdims=True)

    def field(i):
        return part_ref[i : i + 1, lanes]

    deform = [[field(5 + 3 * i + j) for j in range(3)] for i in range(3)]
    stretch = [[(1.0 if i == j else 0.0) + time_step * velgrad[i][j] for j in range(3)] for i in range(3)]
    mapped = [
        [
            stretch[i][0] * deform[0][j] + stretch[i][1] * deform[1][j] + stretch[i][2] * deform[2][j]
            for j in range(3)
        ]
        for i in range(3)
    ]
    jacobian = (
        mapped[0][0] * (mapped[1][1] * mapped[2][2] - mapped[1][2] * mapped[2][1])
        - mapped[0][1] * (mapped[1][0] * mapped[2][2] - mapped[1][2] * mapped[2][0])
        + mapped[0][2] * (mapped[1][0] * mapped[2][1] - mapped[1][1] * mapped[2][0])
    )
    left = {}
    for i in range(3):
        for j in range(i, 3):
            left[i, j] = left[j, i] = (
                mapped[i][0] * mapped[j][0] + mapped[i][1] * mapped[j][1] + mapped[i][2] * mapped[j][2]
            )
    damaged = jnp.maximum(field(23), damage_node)
    degrade = (1.0 - damaged) ** 2
    pressure = bulk_coef * (jacobian - 1.0)
    energy = (
        0.5 * shear_mod * (left[0, 0] + left[1, 1] + left[2, 2] - 3.0) + 0.5 * bulk_coef * (jacobian - 1.0) ** 2
    )
    out_ref[0:2, to] = part_ref[0:2, lanes]
    for i in range(3):
        out_ref[2 + i : 3 + i, to] = moved[i]
        out_ref[25 + i : 26 + i, to] = field(25 + i) + time_step * moved[i]
        for j in range(3):
            out_ref[5 + 3 * i + j : 6 + 3 * i + j, to] = mapped[i][j]
            term = shear_mod * (left[i, j] - (1.0 if i == j else 0.0))
            if i == j:
                term = term + pressure
            out_ref[14 + 3 * i + j : 15 + 3 * i + j, to] = degrade * term
    out_ref[23:24, to] = damaged
    out_ref[24:25, to] = jnp.maximum(field(24), energy)


def relax_kernel(
    axis_sizes,
    place_ref,
    deep_ref,
    vel_ref,
    before_ref,
    after_ref,
    part_ref,
    base_ref,
    w_ref,
    g_ref,
    damage_ref,
    nodes_ref,
    tail_ref,
    one_ref,
    two_ref,
    keep_ref,
    add_ref,
    inverse_ref,
    fv_ref,
    fd_ref,
):
    count_x, count_y, count_z = axis_sizes
    lane = lane_index(PITCH)
    row = lax.broadcasted_iota(jnp.int32, (PITCH, 128), 0)
    pos_y = place_ref[1] * CY + row - WIDE
    pos_z = place_ref[2] * CZ + lane - WIDE
    inside_yz = (
        (lane < SZ) & (pos_y >= 0) & (pos_y < count_y * CY) & (pos_z >= 0) & (pos_z < count_z * CZ)
    ).astype(F32)

    def inside(xd):
        pos = place_ref[0] * CX + xd - WIDE
        flag = jnp.where((pos >= 0) & (pos < count_x * CX), 1.0, 0.0).astype(F32)
        return inside_yz * flag

    one_ref[...] = jnp.zeros_like(one_ref)
    for xd in range(SX):
        if OFF <= xd < OFF + EX:
            one_ref[xd] = deep_ref[xd - OFF]
        if xd < LAYERS:
            one_ref[xd, 0:SY, :] += before_ref[SY * xd : SY * (xd + 1), :]
        if xd >= SX - LAYERS:
            at = SY * (xd - SX + LAYERS)
            one_ref[xd, 0:SY, :] += after_ref[at : at + SY, :]
    for xd in range(SX):
        sums = one_ref[xd]
        mask = inside(xd)
        inverse = mask / jnp.maximum(sums, mass_floor)
        drive = shift_lanes(sums, -2 * SZ) * inverse
        keep_ref[xd] = (1.0 - relax_rate * (1.0 + 6.0 * length_sq)) * mask - 2.0 * relax_rate * drive
        add_ref[xd] = 2.0 * relax_rate * drive
        one_ref[xd] = shift_lanes(sums, -SZ) * inverse
        if OFF <= xd < OFF + EX:
            inverse_ref[xd - OFF] = inverse
    source, target = one_ref, two_ref
    for step in range(SUBSTEPS):
        for xd in range(step + 1, SX - 1 - step):
            centre = source[xd]
            around = (
                source[xd - 1]
                + source[xd + 1]
                + pltpu.roll(centre, 1, 0)
                + pltpu.roll(centre, PITCH - 1, 0)
                + shift_lanes(centre, 1)
                + shift_lanes(centre, -1)
            )
            target[xd] = centre * keep_ref[xd] + add_ref[xd] + (relax_rate * length_sq) * inside(xd) * around
        source, target = target, source
    for x in range(CX):
        damage_ref[x] = shift_lanes(source[x + WIDE], -WIDE)[WIDE : WIDE + CY, 0:CZ]
    fv_ref[...] = jnp.zeros_like(fv_ref)
    fd_ref[...] = jnp.zeros_like(fd_ref)
    vel_at = SY * LAYERS
    for x in range(EX):
        vel = vel_ref[x, OFF : OFF + EY, :]
        if x < 2:
            vel = vel + before_ref[vel_at + EY * x : vel_at + EY * (x + 1), :]
        if x >= EX - 2:
            at = vel_at + EY * (x - EX + 2)
            vel = vel + after_ref[at : at + EY, :]
        inverse = inverse_ref[x, OFF : OFF + EY, :]
        vel = vel * (inverse + shift_lanes(inverse, SZ) + shift_lanes(inverse, 2 * SZ))
        lanes = lane_index(EY)
        vel = jnp.where(
            lanes < ZROWS,
            shift_lanes(vel, -OFF),
            jnp.where(
                lanes < 2 * ZROWS,
                shift_lanes(vel, ZROWS - SZ - OFF),
                shift_lanes(vel, 2 * (ZROWS - SZ) - OFF),
            ),
        )
        fv_ref[EY * x : EY * (x + 1), :] = vel
        fd_ref[EY * x : EY * (x + 1), :] = shift_lanes(source[x + OFF], -OFF)[OFF : OFF + EY, :]
    nodes = jnp.concatenate([fv_ref[...].T[0 : 3 * ZROWS], fd_ref[...].T[0:ZROWS]], axis=0)
    for corner in range(4):
        shift = (corner >> 1) * EY + (corner & 1)
        value = nodes if shift == 0 else pltpu.roll(nodes, 256 - shift, 1)
        high = value.astype(BF16)
        low = (value - high.astype(F32)).astype(BF16)
        start = 8 * ZROWS * corner
        nodes_ref[start : start + 4 * ZROWS, :] = high
        nodes_ref[start + 4 * ZROWS : start + 8 * ZROWS, :] = low

    def step(index, carry):
        gather_update((COUNT - TAIL) // CHUNK + index, nodes_ref, part_ref, base_ref, w_ref, g_ref, tail_ref, index)
        return carry

    lax.fori_loop(0, TAIL // CHUNK, step, 0)


def head_kernel(nodes_ref, part_ref, base_ref, w_ref, g_ref, head_ref):
    def step(index, carry):
        gather_update(index, nodes_ref, part_ref, base_ref, w_ref, g_ref, head_ref, index)
        return carry

    lax.fori_loop(0, (COUNT - TAIL) // CHUNK, step, 0)


def assemble_kernel(counts_ref, prior_ref, recv_ref, head_ref, tail_ref, out_ref, line_ref):
    line_ref[:, 0:TAIL] = recv_ref[...]
    line_ref[:, TAIL:COUNT] = head_ref[...]
    line_ref[:, COUNT : COUNT + TAIL] = tail_ref[...]
    prior = prior_ref[0, 120].astype(jnp.int32)
    live = NBIN - counts_ref[0] + prior
    for slot in range(NBIN + MOST):
        source = jnp.minimum(MOST - prior + slot, NBIN + MOST - 1)
        value = line_ref[:, pl.ds(pl.multiple_of(source * BIN, BIN), BIN)]
        out_ref[:, slot * BIN : (slot + 1) * BIN] = jnp.where(slot < live, value, 0.0)


def shape(*dims, kind=F32):
    return jax.ShapeDtypeStruct(dims, kind)


def smem():
    return pl.BlockSpec(memory_space=pltpu.SMEM)


def vmem(n):
    return [pl.BlockSpec(memory_space=VMEM)] * n


def call(kernel, out_shape, n_smem, args, scratch=(), flops=0):
    return pl.pallas_call(
        kernel,
        out_shape=out_shape,
        in_specs=[smem()] * n_smem + vmem(len(args) - n_smem),
        out_specs=jax.tree.map(lambda _: pl.BlockSpec(memory_space=VMEM), out_shape),
        scratch_shapes=list(scratch),
        compiler_params=pltpu.CompilerParams(vmem_limit_bytes=VMEM_LIMIT),
        cost_estimate=pl.CostEstimate(flops=flops, bytes_accessed=2000000, transcendentals=0),
    )(*args)


def exchange(low, high, axis, ring=False):
    count = lax.axis_size(axis)
    up = [(i, (i + 1) % count) for i in range(count if ring else count - 1)]
    down = [(i + 1, i) for i in range(count - 1)]
    return lax.ppermute(high, axis, up), lax.ppermute(low, axis, down)


def per_device(particles, stencil_base, weights, gradients, counts):
    axes = ("gx", "gy", "gz")
    place = jnp.stack([lax.axis_index(a) for a in axes]).astype(jnp.int32)
    sizes = tuple(lax.axis_size(a) for a in axes)
    ring = [(i, (i + 1) % sizes[2]) for i in range(sizes[2])]
    inputs = (particles, stencil_base, weights, gradients)
    deep, vel, low, high = call(
        scatter_kernel,
        (shape(GROWS, 128), shape(GROWS, 128), shape(GROUP, 128), shape(GROUP, 128)),
        1,
        (counts,) + inputs,
        [VMEM((AROWS, 1024), F32), VMEM((GROWS, 256), F32)],
    )
    before_z, after_z = exchange(low, high, "gz", ring=True)
    message = LAYERS * EX + 2 * EX
    deep, vel, low, high = call(
        join_z_kernel,
        (shape(GROWS, 128), shape(GROWS, 128), shape(message, 128), shape(message, 128)),
        1,
        (place, deep, vel, before_z, after_z),
    )
    before, after = exchange(low, high, "gy")
    message = LAYERS * SY + 2 * EY
    deep, vel, low, high = call(
        join_y_kernel,
        (shape(EX, PITCH, 128), shape(EX, PITCH, 128), shape(message, 128), shape(message, 128)),
        0,
        (deep, vel, before, after),
    )
    before, after = exchange(low, high, "gx")

    def relax(*refs):
        relax_kernel(sizes, *refs)

    damage, nodes, tail = call(
        relax,
        (shape(CX, CY, CZ), shape(32 * ZROWS, 256, kind=BF16), shape(FIELDS, TAIL)),
        1,
        (place, deep, vel, before, after) + inputs,
        [VMEM((SX, PITCH, 128), F32)] * 4 + [VMEM((EX, PITCH, 128), F32)] + [VMEM((256, 128), F32)] * 2,
    )
    recv = lax.ppermute(tail, "gz", ring)
    head = call(head_kernel, shape(FIELDS, COUNT - TAIL), 0, (nodes,) + inputs, flops=2 * 1280 * 256 * 1024)
    migrated = call(
        assemble_kernel,
        shape(FIELDS, SLOTS),
        2,
        (counts, before_z[0:8], recv, head, tail),
        [VMEM((FIELDS, COUNT + TAIL), F32)],
    )
    return (migrated, damage)


def solution(mesh):
    return jax.shard_map(
        per_device,
        mesh=mesh,
        in_specs=(
            P(None, ("gx", "gy", "gz")),
            P(None, ("gx", "gy", "gz")),
            P(None, ("gx", "gy", "gz")),
            P(None, None, ("gx", "gy", "gz")),
            P(("gx", "gy", "gz")),
        ),
        out_specs=(P(None, ("gx", "gy", "gz")), P("gx", "gy", "gz")),
        check_vma=False,
    )
```

```python
import jax
import jax.numpy as jnp
from jax import lax
from jax.experimental import pallas as pl
from jax.experimental.pallas import tpu as pltpu
from jax.sharding import PartitionSpec as P

CX = 8
CY = 16
CZ = 32
NBIN = 16
BIN = 128
SUBSTEPS = 4
FIELDS = 28
MOST = 8
COUNT = NBIN * BIN
TAIL = MOST * BIN
SLOTS = (NBIN + MOST) * BIN

time_step = 0.1
relax_rate = 0.2
length_sq = 0.6
shear_mod = 1.0
bulk_coef = 1.5
mass_floor = 0.5

EX = CX + 2
EY = CY + 2
EZ = CZ + 2
WIDE = SUBSTEPS + 1
LAYERS = WIDE + 1
SX = CX + 2 * WIDE
SY = CY + 2 * WIDE
SZ = CZ + 2 * WIDE
OFF = WIDE - 1
PITCH = 32
AROWS = 176
GROWS = 200
GROUP = 40
HALF = 104
PACK = SX // 3
ZROWS = 40
CHUNK = 256
F32 = jnp.float32
BF16 = jnp.bfloat16
SCATTER_KIB = 56000
VMEM = pltpu.VMEM


def shift_lanes(value, by):
    by = by % 128
    return value if by == 0 else pltpu.roll(value, by, 1)


def channel_lane(lane):
    return jnp.where(
        lane < SZ, lane, jnp.where(lane < 2 * SZ, lane - SZ, jnp.where(lane < 3 * SZ, lane - 2 * SZ, 1000))
    )


def three(lane, width, a, b, c):
    return jnp.where(lane < width, a, jnp.where(lane < 2 * width, b, c))


def lane_index(rows):
    return lax.broadcasted_iota(jnp.int32, (rows, 128), 1)


def onehot_rows(base_ref, lanes):
    xy = base_ref[0:1, lanes] * EY + base_ref[1:2, lanes]
    rows = lax.broadcasted_iota(jnp.int32, (AROWS, CHUNK), 0)
    return jnp.where(rows == xy, 1.0, 0.0).astype(BF16)


def scatter_kernel(
    counts_ref,
    part_hbm,
    base_hbm,
    w_hbm,
    g_hbm,
    deep_ref,
    vel_ref,
    low_ref,
    high_ref,
    part_ref,
    base_ref,
    w_ref,
    g_ref,
    acc_ref,
    wide_ref,
    term_ref,
    rows_ref,
    onehot_ref,
    sems,
):
    moves = [
        pltpu.make_async_copy(source, target, sems.at[i])
        for i, (source, target) in enumerate(
            ((base_hbm, base_ref), (part_hbm, part_ref), (w_hbm, w_ref), (g_hbm, g_ref))
        )
    ]
    for move in moves:
        move.start()
    acc_ref[...] = jnp.zeros_like(acc_ref)
    wide_ref[...] = jnp.zeros_like(wide_ref)
    moves[0].wait()
    for index in range(COUNT // CHUNK):
        lanes = slice(index * CHUNK, (index + 1) * CHUNK)
        onehot_ref[:, lanes] = onehot_rows(base_ref, lanes)
    for move in moves[1:]:
        move.wait()
    for index in range(COUNT // CHUNK):
        lanes = slice(index * CHUNK, (index + 1) * CHUNK)
        minus_vol = -time_step * part_ref[1:2, lanes]
        share = part_ref[0:1, lanes] * w_ref[:, lanes]
        slope = [g_ref[j, :, lanes] for j in range(3)]
        terms = [share, share * part_ref[23:24, lanes], share * part_ref[24:25, lanes]]
        for i in range(3):
            row = 14 + 3 * i
            pull = (
                part_ref[row : row + 1, lanes] * slope[0]
                + part_ref[row + 1 : row + 2, lanes] * slope[1]
                + part_ref[row + 2 : row + 3, lanes] * slope[2]
            )
            terms.append(share * part_ref[2 + i : 3 + i, lanes] + minus_vol * pull)
        for ch, term in enumerate(terms):
            high = term.astype(BF16).astype(F32)
            term_ref[0, ch, :, lanes] = high
            term_ref[1, ch, :, lanes] = term - high
    nt = (((1,), (1,)), ((), ()))
    for corner in range(4):
        k = 2 * corner
        for index in range(COUNT // CHUNK):
            lanes = slice(index * CHUNK, (index + 1) * CHUNK)
            sub = lax.broadcasted_iota(jnp.int32, (8, CHUNK), 0) - base_ref[2:3, lanes]
            for part in range(2):
                tiles = {}
                for tile in range(HALF // 8):
                    first = [(ch, EZ * ch - 8 * tile) for ch in range(3) if EZ * ch < 8 * tile + 8 and EZ * (ch + 1) > 8 * tile]
                    for half in range(2):
                        value = jnp.zeros((8, CHUNK), F32)
                        for ch, at in first:
                            value = jnp.where(sub == at, term_ref[part, 3 * half + ch, k : k + 1, lanes], value)
                            value = jnp.where(sub == at + 1, term_ref[part, 3 * half + ch, k + 1 : k + 2, lanes], value)
                        tiles[half * (HALF // 8) + tile] = value
                to = slice(part * COUNT + index * CHUNK, part * COUNT + (index + 1) * CHUNK)
                for pair in range(HALF // 8):
                    row = 2 * HALF * corner + 16 * pair
                    rows_ref[row : row + 16, to] = jnp.concatenate([tiles[2 * pair], tiles[2 * pair + 1]], axis=0).astype(BF16)
        rows = slice(2 * HALF * corner, 2 * HALF * (corner + 1))
        piece = lax.dot_general(rows_ref[rows, 0:COUNT], onehot_ref[...], nt, preferred_element_type=F32)
        piece = piece + lax.dot_general(rows_ref[rows, COUNT:], onehot_ref[...], nt, preferred_element_type=F32)
        acc_ref[corner, :, 0:AROWS] = piece
    total = acc_ref[0]
    for corner in range(1, 4):
        total = total + pltpu.roll(acc_ref[corner], (corner >> 1) * EY + (corner & 1), 1)
    for half in range(2):
        for ch in range(3):
            row = half * HALF + EZ * ch
            to = half * 128 + SZ * ch + OFF
            wide_ref[to : to + EZ, :] = total[row : row + EZ]
    deep_ref[...] = wide_ref[0:128, :].T[0:GROWS]
    vel_ref[...] = wide_ref[128:256, :].T[0:GROWS]
    lane = lane_index(GROUP)
    place = channel_lane(lane)
    low_msg = jnp.zeros((GROUP, 128), F32)
    high_msg = jnp.zeros((GROUP, 128), F32)
    for j in range(5):
        rows = slice(GROUP * j, GROUP * (j + 1))
        deep = deep_ref[rows, :]
        vel = vel_ref[rows, :]
        inside = (place >= 8 * j) & (place < 8 * j + LAYERS)
        low_msg = jnp.where(inside, shift_lanes(deep, 8 * j - OFF), low_msg)
        high_msg = jnp.where(inside, shift_lanes(deep, 8 * j - CZ), high_msg)
        inside = (place >= 8 * j + LAYERS) & (place < 8 * j + LAYERS + 2)
        low_msg = jnp.where(inside, shift_lanes(vel, 8 * j + LAYERS - OFF), low_msg)
        high_msg = jnp.where(inside, shift_lanes(vel, 8 * j + LAYERS - OFF - CZ), high_msg)
    low_ref[...] = low_msg
    high_ref[...] = jnp.where(lane >= 3 * SZ, counts_ref[0].astype(F32), high_msg)


def join_z_kernel(place_ref, deep_ref, vel_ref, before_ref, after_ref, deep_out, vel_out, low_ref, high_ref):
    place = channel_lane(lane_index(GROUP))
    before = jnp.where(place_ref[2] > 0, before_ref[...], 0.0)
    after = after_ref[...]
    deep_low, deep_high = place < LAYERS, (place >= SZ - LAYERS) & (place < SZ)
    vel_low = (place >= OFF) & (place < OFF + 2)
    vel_high = (place >= OFF + CZ) & (place < OFF + CZ + 2)
    for j in range(5):
        rows = slice(GROUP * j, GROUP * (j + 1))
        deep = jnp.where(
            deep_low,
            shift_lanes(before, -8 * j),
            jnp.where(deep_high, shift_lanes(after, SZ - LAYERS - 8 * j), 0.0),
        )
        vel = jnp.where(
            vel_low,
            shift_lanes(before, OFF - 8 * j - LAYERS),
            jnp.where(vel_high, shift_lanes(after, OFF + CZ - 8 * j - LAYERS), 0.0),
        )
        deep_out[rows, :] = deep_ref[rows, :] + deep
        vel_out[rows, :] = vel_ref[rows, :] + vel
    for x in range(EX):
        row = EY * x
        low_ref[LAYERS * x : LAYERS * (x + 1), :] = deep_out[row : row + LAYERS, :]
        high_ref[LAYERS * x : LAYERS * (x + 1), :] = deep_out[row + EY - LAYERS : row + EY, :]
        at = LAYERS * EX + 2 * x
        low_ref[at : at + 2, :] = vel_out[row : row + 2, :]
        high_ref[at : at + 2, :] = vel_out[row + EY - 2 : row + EY, :]


def join_y_kernel(deep_ref, vel_ref, before_ref, after_ref, deep_out, vel_out, low_ref, high_ref):
    deep_out[...] = jnp.zeros_like(deep_out)
    vel_out[...] = jnp.zeros_like(vel_out)
    for x in range(EX):
        row = EY * x
        deep_out[x, OFF : OFF + EY, :] = deep_ref[row : row + EY, :]
        deep_out[x, 0:LAYERS, :] += before_ref[LAYERS * x : LAYERS * (x + 1), :]
        deep_out[x, OFF + CY : OFF + CY + LAYERS, :] += after_ref[LAYERS * x : LAYERS * (x + 1), :]
        at = LAYERS * EX + 2 * x
        vel_out[x, OFF : OFF + EY, :] = vel_ref[row : row + EY, :]
        vel_out[x, OFF : OFF + 2, :] += before_ref[at : at + 2, :]
        vel_out[x, OFF + CY : OFF + CY + 2, :] += after_ref[at : at + 2, :]
    for x in range(LAYERS):
        low_ref[SY * x : SY * (x + 1), :] = deep_out[x, 0:SY, :]
        high_ref[SY * x : SY * (x + 1), :] = deep_out[EX - LAYERS + x, 0:SY, :]
    for x in range(2):
        at = SY * LAYERS + EY * x
        low_ref[at : at + EY, :] = vel_out[x, OFF : OFF + EY, :]
        high_ref[at : at + EY, :] = vel_out[EX - 2 + x, OFF : OFF + EY, :]


def gather_update(index, nodes_ref, part_ref, base_ref, w_ref, g_ref, out_ref, out_index):
    lanes = slice(index * CHUNK, (index + 1) * CHUNK)
    to = slice(out_index * CHUNK, (out_index + 1) * CHUNK)
    onehot = onehot_rows(base_ref, lanes)
    base_z = base_ref[2:3, lanes]
    rows = lax.broadcasted_iota(jnp.int32, (ZROWS, CHUNK), 0) - base_z
    at = rows == 0
    after = rows == 1

    def pick(mask, value):
        kept = jnp.where(mask, value, 0.0)
        total = kept[0:8]
        for t in range(1, ZROWS // 8):
            total = total + kept[8 * t : 8 * t + 8]
        return total

    moved = [jnp.zeros((8, CHUNK), F32) for _ in range(3)]
    velgrad = [[jnp.zeros((8, CHUNK), F32) for _ in range(3)] for _ in range(3)]
    damage_node = jnp.zeros((8, CHUNK), F32)
    rows_ab = 4 * ZROWS
    for corner in range(4):
        start = 2 * rows_ab * corner
        near = jnp.dot(nodes_ref[start : start + rows_ab, 0:AROWS], onehot, preferred_element_type=F32) + jnp.dot(
            nodes_ref[start + rows_ab : start + 2 * rows_ab, 0:AROWS], onehot, preferred_element_type=F32
        )
        for c, mask in enumerate((at, after)):
            k = 2 * corner + c
            weight = w_ref[k : k + 1, lanes]
            slope = [g_ref[j, k : k + 1, lanes] for j in range(3)]
            for i in range(3):
                value = pick(mask, near[ZROWS * i : ZROWS * (i + 1)])
                moved[i] = moved[i] + value * weight
                for j in range(3):
                    velgrad[i][j] = velgrad[i][j] + value * slope[j]
            damage_node = damage_node + pick(mask, near[3 * ZROWS : 4 * ZROWS]) * weight
    moved = [jnp.sum(v, axis=0, keepdims=True) for v in moved]
    velgrad = [[jnp.sum(v, axis=0, keepdims=True) for v in row] for row in velgrad]
    damage_node = jnp.sum(damage_node, axis=0, keepdims=True)

    def field(i):
        return part_ref[i : i + 1, lanes]

    deform = [[field(5 + 3 * i + j) for j in range(3)] for i in range(3)]
    stretch = [[(1.0 if i == j else 0.0) + time_step * velgrad[i][j] for j in range(3)] for i in range(3)]
    mapped = [
        [
            stretch[i][0] * deform[0][j] + stretch[i][1] * deform[1][j] + stretch[i][2] * deform[2][j]
            for j in range(3)
        ]
        for i in range(3)
    ]
    jacobian = (
        mapped[0][0] * (mapped[1][1] * mapped[2][2] - mapped[1][2] * mapped[2][1])
        - mapped[0][1] * (mapped[1][0] * mapped[2][2] - mapped[1][2] * mapped[2][0])
        + mapped[0][2] * (mapped[1][0] * mapped[2][1] - mapped[1][1] * mapped[2][0])
    )
    left = {}
    for i in range(3):
        for j in range(i, 3):
            left[i, j] = left[j, i] = (
                mapped[i][0] * mapped[j][0] + mapped[i][1] * mapped[j][1] + mapped[i][2] * mapped[j][2]
            )
    damaged = jnp.maximum(field(23), damage_node)
    degrade = (1.0 - damaged) ** 2
    pressure = bulk_coef * (jacobian - 1.0)
    energy = (
        0.5 * shear_mod * (left[0, 0] + left[1, 1] + left[2, 2] - 3.0) + 0.5 * bulk_coef * (jacobian - 1.0) ** 2
    )
    out_ref[0:2, to] = part_ref[0:2, lanes]
    for i in range(3):
        out_ref[2 + i : 3 + i, to] = moved[i]
        out_ref[25 + i : 26 + i, to] = field(25 + i) + time_step * moved[i]
        for j in range(3):
            out_ref[5 + 3 * i + j : 6 + 3 * i + j, to] = mapped[i][j]
            term = shear_mod * (left[i, j] - (1.0 if i == j else 0.0))
            if i == j:
                term = term + pressure
            out_ref[14 + 3 * i + j : 15 + 3 * i + j, to] = degrade * term
    out_ref[23:24, to] = damaged
    out_ref[24:25, to] = jnp.maximum(field(24), energy)


def relax_kernel(
    axis_sizes,
    place_ref,
    deep_ref,
    vel_ref,
    before_ref,
    after_ref,
    part_ref,
    base_ref,
    w_ref,
    g_ref,
    damage_hbm,
    nodes_ref,
    tail_ref,
    sums_ref,
    one_ref,
    two_ref,
    keep_ref,
    add_ref,
    spread_ref,
    inverse_ref,
    fv_ref,
    fd_ref,
    damage_ref,
    sem,
):
    count_x, count_y, count_z = axis_sizes
    sums_ref[...] = jnp.zeros_like(sums_ref)
    for xd in range(SX):
        if OFF <= xd < OFF + EX:
            sums_ref[xd] = deep_ref[xd - OFF]
        if xd < LAYERS:
            sums_ref[xd, 0:SY, :] += before_ref[SY * xd : SY * (xd + 1), :]
        if xd >= SX - LAYERS:
            at = SY * (xd - SX + LAYERS)
            sums_ref[xd, 0:SY, :] += after_ref[at : at + SY, :]
    lane = lane_index(PITCH)
    pos_x = place_ref[0] * CX - WIDE + three(lane, SZ, 0, PACK, 2 * PACK)
    pos_y = place_ref[1] * CY - WIDE + lax.broadcasted_iota(jnp.int32, (PITCH, 128), 0)
    pos_z = place_ref[2] * CZ - WIDE + lane - three(lane, SZ, 0, SZ, 2 * SZ)
    inside_yz = (
        (lane < 3 * SZ) & (pos_y >= 0) & (pos_y < count_y * CY) & (pos_z >= 0) & (pos_z < count_z * CZ)
    )
    for j in range(PACK):
        first, second, third = sums_ref[j], sums_ref[j + PACK], sums_ref[j + 2 * PACK]
        mass = three(lane, SZ, first, shift_lanes(second, SZ), shift_lanes(third, 2 * SZ))
        damage = three(lane, SZ, shift_lanes(first, -SZ), second, shift_lanes(third, SZ))
        drive = three(lane, SZ, shift_lanes(first, -2 * SZ), shift_lanes(second, -SZ), third)
        mask = (inside_yz & (pos_x + j >= 0) & (pos_x + j < count_x * CX)).astype(F32)
        inverse = mask / jnp.maximum(mass, mass_floor)
        drive = (2.0 * relax_rate) * (drive * inverse)
        keep_ref[j] = (1.0 - relax_rate * (1.0 + 6.0 * length_sq)) * mask - drive
        add_ref[j] = drive
        spread_ref[j] = (relax_rate * length_sq) * mask
        one_ref[j] = damage * inverse
        inverse_ref[j] = inverse
    source, target = one_ref, two_ref
    for _ in range(SUBSTEPS):
        for j in range(PACK):
            centre = source[j]
            lower = source[j - 1] if j > 0 else shift_lanes(source[PACK - 1], SZ)
            upper = source[j + 1] if j < PACK - 1 else shift_lanes(source[0], -SZ)
            around = (
                (lower + upper)
                + (pltpu.roll(centre, 1, 0) + pltpu.roll(centre, PITCH - 1, 0))
                + (shift_lanes(centre, 1) + shift_lanes(centre, -1))
            )
            target[j] = (centre * keep_ref[j] + add_ref[j]) + spread_ref[j] * around
        source, target = target, source
    for x in range(CX):
        xd = x + WIDE
        value = shift_lanes(source[xd % PACK], -SZ * (xd // PACK) - WIDE)
        damage_ref[x] = value[WIDE : WIDE + CY, 0:CZ]
    move = pltpu.make_async_copy(damage_ref, damage_hbm, sem)
    move.start()
    fv_ref[...] = jnp.zeros_like(fv_ref)
    fd_ref[...] = jnp.zeros_like(fd_ref)
    vel_at = SY * LAYERS
    lane = lane_index(EY)
    for x in range(EX):
        vel = vel_ref[x, OFF : OFF + EY, :]
        if x < 2:
            vel = vel + before_ref[vel_at + EY * x : vel_at + EY * (x + 1), :]
        if x >= EX - 2:
            at = vel_at + EY * (x - EX + 2)
            vel = vel + after_ref[at : at + EY, :]
        slot, group = (x + OFF) % PACK, (x + OFF) // PACK
        inverse = inverse_ref[slot, OFF : OFF + EY, :]
        vel = three(lane, ZROWS, *(shift_lanes(vel, (ZROWS - SZ) * ch - OFF) for ch in range(3)))
        inverse = three(lane, ZROWS, *(shift_lanes(inverse, ZROWS * ch - SZ * group - OFF) for ch in range(3)))
        fv_ref[EY * x : EY * (x + 1), :] = vel * inverse
        fd_ref[EY * x : EY * (x + 1), :] = shift_lanes(source[slot], -SZ * group - OFF)[OFF : OFF + EY, :]
    nodes = jnp.concatenate([fv_ref[...].T[0 : 3 * ZROWS], fd_ref[...].T[0:ZROWS]], axis=0)
    for corner in range(4):
        shift = (corner >> 1) * EY + (corner & 1)
        value = nodes if shift == 0 else pltpu.roll(nodes, 256 - shift, 1)
        high = value.astype(BF16)
        low = (value - high.astype(F32)).astype(BF16)
        start = 8 * ZROWS * corner
        nodes_ref[start : start + 4 * ZROWS, :] = high
        nodes_ref[start + 4 * ZROWS : start + 8 * ZROWS, :] = low
    for index in range(TAIL // CHUNK):
        gather_update((COUNT - TAIL) // CHUNK + index, nodes_ref, part_ref, base_ref, w_ref, g_ref, tail_ref, index)
    move.wait()


def head_kernel(
    counts_ref, prior_ref, nodes_ref, tail_ref, part_ref, base_ref, w_ref, g_ref, out_hbm, head_ref, left_ref, zero_ref, sems
):
    prior = prior_ref[0, 3 * SZ].astype(jnp.int32)
    left = MOST - counts_ref[0]
    zero_ref[...] = jnp.zeros_like(zero_ref)
    blanks = []
    for i in range(MOST):
        to = pl.ds(pl.multiple_of((NBIN + MOST - 1 - i) * BIN, BIN), BIN)
        blanks.append((i < MOST - prior, pltpu.make_async_copy(zero_ref, out_hbm.at[:, to], sems.at[2 + i])))
    for wanted, move in blanks:
        pl.when(wanted)(move.start)
    for i in range(MOST):
        bins = slice(i * BIN, (i + 1) * BIN)
        left_ref[:, bins] = jnp.where(i < left, tail_ref[:, bins], 0.0)
    to = pl.ds(pl.multiple_of((prior + NBIN - MOST) * BIN, BIN), TAIL)
    own = pltpu.make_async_copy(left_ref, out_hbm.at[:, to], sems.at[0])
    own.start()
    for index in range((COUNT - TAIL) // CHUNK):
        gather_update(index, nodes_ref, part_ref, base_ref, w_ref, g_ref, head_ref, index)
    to = pl.ds(pl.multiple_of(prior * BIN, BIN), COUNT - TAIL)
    stay = pltpu.make_async_copy(head_ref, out_hbm.at[:, to], sems.at[1])
    stay.start()
    for wanted, move in blanks:
        pl.when(wanted)(move.wait)
    own.wait()
    stay.wait()


def arrive_kernel(prior_ref, recv_ref, partial_hbm, out_hbm, sems):
    prior = prior_ref[0, 3 * SZ].astype(jnp.int32)
    moves = []
    for slot in range(MOST):
        source = pl.ds(pl.multiple_of(jnp.minimum(MOST - prior + slot, MOST - 1) * BIN, BIN), BIN)
        moves.append(
            (
                slot < prior,
                pltpu.make_async_copy(recv_ref.at[:, source], out_hbm.at[:, slot * BIN : (slot + 1) * BIN], sems.at[slot]),
            )
        )
    for wanted, move in moves:
        pl.when(wanted)(move.start)
    for wanted, move in moves:
        pl.when(wanted)(move.wait)


def shape(*dims, kind=F32):
    return jax.ShapeDtypeStruct(dims, kind)


SMEM = pltpu.SMEM
HBM = pltpu.HBM


def call(kernel, out_shape, spaces, args, out_spaces=None, scratch=(), flops=0, aliases=None, limit=None):
    leaves = jax.tree.leaves(out_shape)
    out_spaces = out_spaces or [VMEM] * len(leaves)
    out_specs = [pl.BlockSpec(memory_space=s) for s in out_spaces]
    return pl.pallas_call(
        kernel,
        out_shape=out_shape,
        in_specs=[pl.BlockSpec(memory_space=s) for s in spaces],
        out_specs=tuple(out_specs) if isinstance(out_shape, tuple) else out_specs[0],
        scratch_shapes=list(scratch),
        input_output_aliases=aliases or {},
        compiler_params=pltpu.CompilerParams(vmem_limit_bytes=(limit or 48 * 1024) * 1024),
        cost_estimate=pl.CostEstimate(flops=flops, bytes_accessed=2000000, transcendentals=0),
    )(*args)


def exchange(low, high, axis, ring=False):
    count = lax.axis_size(axis)
    up = [(i, (i + 1) % count) for i in range(count if ring else count - 1)]
    down = [(i + 1, i) for i in range(count - 1)]
    return lax.ppermute(high, axis, up), lax.ppermute(low, axis, down)


def per_device(particles, stencil_base, weights, gradients, counts):
    axes = ("gx", "gy", "gz")
    place = jnp.stack([lax.axis_index(a) for a in axes]).astype(jnp.int32)
    sizes = tuple(lax.axis_size(a) for a in axes)
    ring = [(i, (i + 1) % sizes[2]) for i in range(sizes[2])]
    inputs = (particles, stencil_base, weights, gradients)
    deep, vel, low, high = call(
        scatter_kernel,
        (VMEM((GROWS, 128), F32), VMEM((GROWS, 128), F32), VMEM((GROUP, 128), F32), VMEM((GROUP, 128), F32)),
        [SMEM] + [HBM] * 4,
        (counts,) + inputs,
        scratch=[
            VMEM((FIELDS, COUNT), F32),
            VMEM((3, COUNT), jnp.int32),
            VMEM((8, COUNT), F32),
            VMEM((3, 8, COUNT), F32),
            VMEM((4, 2 * HALF, 256), F32),
            VMEM((256, 256), F32),
            VMEM((2, 6, 8, COUNT), F32),
            VMEM((8 * HALF, 2 * COUNT), BF16),
            VMEM((AROWS, COUNT), BF16),
            pltpu.SemaphoreType.DMA((4,)),
        ],
        limit=SCATTER_KIB,
    )
    before_z, after_z = exchange(low, high, "gz", ring=True)
    message = LAYERS * EX + 2 * EX
    deep, vel, low, high = call(
        join_z_kernel,
        (shape(GROWS, 128), shape(GROWS, 128), shape(message, 128), shape(message, 128)),
        [SMEM] + [VMEM] * 4,
        (place, deep, vel, before_z, after_z),
    )
    before, after = exchange(low, high, "gy")
    message = LAYERS * SY + 2 * EY
    deep, vel, low, high = call(
        join_y_kernel,
        (shape(EX, PITCH, 128), shape(EX, PITCH, 128), shape(message, 128), shape(message, 128)),
        [VMEM] * 4,
        (deep, vel, before, after),
    )
    before, after = exchange(low, high, "gx")

    def relax(*refs):
        relax_kernel(sizes, *refs)

    damage, nodes, tail = call(
        relax,
        (shape(CX, CY, CZ), shape(32 * ZROWS, 256, kind=BF16), shape(FIELDS, TAIL)),
        [SMEM] + [VMEM] * 8,
        (place, deep, vel, before, after) + inputs,
        out_spaces=[HBM, VMEM, VMEM],
        scratch=[VMEM((SX, PITCH, 128), F32)]
        + [VMEM((PACK, PITCH, 128), F32)] * 6
        + [VMEM((256, 128), F32)] * 2
        + [VMEM((CX, CY, CZ), F32), pltpu.SemaphoreType.DMA],
    )
    recv = lax.ppermute(tail, "gz", ring)
    prior = before_z[0:8]
    own = call(
        head_kernel,
        shape(FIELDS, SLOTS),
        [SMEM] + [VMEM] * 7,
        (counts, prior, nodes, tail) + inputs,
        out_spaces=[HBM],
        scratch=[
            VMEM((FIELDS, COUNT - TAIL), F32),
            VMEM((FIELDS, TAIL), F32),
            VMEM((FIELDS, BIN), F32),
            pltpu.SemaphoreType.DMA((2 + MOST,)),
        ],
        flops=2 * 1280 * 256 * 1024,
    )
    migrated = call(
        arrive_kernel,
        shape(FIELDS, SLOTS),
        [VMEM, VMEM, HBM],
        (prior, recv, own),
        out_spaces=[HBM],
        scratch=[pltpu.SemaphoreType.DMA((MOST,))],
        aliases={2: 0},
    )
    return (migrated, damage)


def solution(mesh):
    return jax.shard_map(
        per_device,
        mesh=mesh,
        in_specs=(
            P(None, ("gx", "gy", "gz")),
            P(None, ("gx", "gy", "gz")),
            P(None, ("gx", "gy", "gz")),
            P(None, None, ("gx", "gy", "gz")),
            P(("gx", "gy", "gz")),
        ),
        out_specs=(P(None, ("gx", "gy", "gz")), P("gx", "gy", "gz")),
        check_vma=False,
    )
```

```python
import jax
import jax.numpy as jnp
from jax import lax
from jax.experimental import pallas as pl
from jax.experimental.pallas import tpu as pltpu
from jax.sharding import PartitionSpec as P

CX = 8
CY = 16
CZ = 32
NBIN = 16
BIN = 128
SUBSTEPS = 4
FIELDS = 28
MOST = 8
COUNT = NBIN * BIN
TAIL = MOST * BIN
SLOTS = (NBIN + MOST) * BIN

time_step = 0.1
relax_rate = 0.2
length_sq = 0.6
shear_mod = 1.0
bulk_coef = 1.5
mass_floor = 0.5

EX = CX + 2
EY = CY + 2
EZ = CZ + 2
WIDE = SUBSTEPS + 1
LAYERS = WIDE + 1
SX = CX + 2 * WIDE
SY = CY + 2 * WIDE
SZ = CZ + 2 * WIDE
OFF = WIDE - 1
PITCH = 32
AROWS = 176
GROWS = 200
GROUP = 40
HALF = 104
PACK = SX // 3
ZROWS = 40
CHUNK = 256
F32 = jnp.float32
BF16 = jnp.bfloat16
SCATTER_KIB = 56000
VMEM = pltpu.VMEM


def shift_lanes(value, by):
    by = by % 128
    return value if by == 0 else pltpu.roll(value, by, 1)


def channel_lane(lane):
    return jnp.where(
        lane < SZ, lane, jnp.where(lane < 2 * SZ, lane - SZ, jnp.where(lane < 3 * SZ, lane - 2 * SZ, 1000))
    )


def three(lane, width, a, b, c):
    return jnp.where(lane < width, a, jnp.where(lane < 2 * width, b, c))


def lane_index(rows):
    return lax.broadcasted_iota(jnp.int32, (rows, 128), 1)


def onehot_rows(base_ref, lanes):
    xy = base_ref[0:1, lanes] * EY + base_ref[1:2, lanes]
    rows = lax.broadcasted_iota(jnp.int32, (AROWS, CHUNK), 0)
    return jnp.where(rows == xy, 1.0, 0.0).astype(BF16)


def scatter_kernel(
    counts_ref,
    part_hbm,
    base_hbm,
    w_hbm,
    g_hbm,
    deep_ref,
    vel_ref,
    low_ref,
    high_ref,
    part_ref,
    base_ref,
    w_ref,
    g_ref,
    acc_ref,
    wide_ref,
    term_ref,
    rows_ref,
    onehot_ref,
    sems,
):
    moves = [
        pltpu.make_async_copy(source, target, sems.at[i])
        for i, (source, target) in enumerate(
            ((base_hbm, base_ref), (part_hbm, part_ref), (w_hbm, w_ref), (g_hbm, g_ref))
        )
    ]
    for move in moves:
        move.start()
    acc_ref[...] = jnp.zeros_like(acc_ref)
    wide_ref[...] = jnp.zeros_like(wide_ref)
    moves[0].wait()
    for index in range(COUNT // CHUNK):
        lanes = slice(index * CHUNK, (index + 1) * CHUNK)
        onehot_ref[:, lanes] = onehot_rows(base_ref, lanes)
    for move in moves[1:]:
        move.wait()
    for index in range(COUNT // CHUNK):
        lanes = slice(index * CHUNK, (index + 1) * CHUNK)
        minus_vol = -time_step * part_ref[1:2, lanes]
        share = part_ref[0:1, lanes] * w_ref[:, lanes]
        slope = [g_ref[j, :, lanes] for j in range(3)]
        terms = [share, share * part_ref[23:24, lanes], share * part_ref[24:25, lanes]]
        for i in range(3):
            row = 14 + 3 * i
            pull = (
                part_ref[row : row + 1, lanes] * slope[0]
                + part_ref[row + 1 : row + 2, lanes] * slope[1]
                + part_ref[row + 2 : row + 3, lanes] * slope[2]
            )
            terms.append(share * part_ref[2 + i : 3 + i, lanes] + minus_vol * pull)
        for ch, term in enumerate(terms):
            high = term.astype(BF16).astype(F32)
            term_ref[0, ch, :, lanes] = high
            term_ref[1, ch, :, lanes] = term - high
    nt = (((1,), (1,)), ((), ()))
    for corner in range(4):
        k = 2 * corner
        for index in range(COUNT // CHUNK):
            lanes = slice(index * CHUNK, (index + 1) * CHUNK)
            sub = lax.broadcasted_iota(jnp.int32, (8, CHUNK), 0) - base_ref[2:3, lanes]
            for part in range(2):
                tiles = {}
                for tile in range(HALF // 8):
                    first = [(ch, EZ * ch - 8 * tile) for ch in range(3) if EZ * ch < 8 * tile + 8 and EZ * (ch + 1) > 8 * tile]
                    for half in range(2):
                        value = jnp.zeros((8, CHUNK), F32)
                        for ch, at in first:
                            value = jnp.where(sub == at, term_ref[part, 3 * half + ch, k : k + 1, lanes], value)
                            value = jnp.where(sub == at + 1, term_ref[part, 3 * half + ch, k + 1 : k + 2, lanes], value)
                        tiles[half * (HALF // 8) + tile] = value
                to = slice(part * COUNT + index * CHUNK, part * COUNT + (index + 1) * CHUNK)
                for pair in range(HALF // 8):
                    row = 2 * HALF * corner + 16 * pair
                    rows_ref[row : row + 16, to] = jnp.concatenate([tiles[2 * pair], tiles[2 * pair + 1]], axis=0).astype(BF16)
        rows = slice(2 * HALF * corner, 2 * HALF * (corner + 1))
        piece = lax.dot_general(rows_ref[rows, 0:COUNT], onehot_ref[...], nt, preferred_element_type=F32)
        piece = piece + lax.dot_general(rows_ref[rows, COUNT:], onehot_ref[...], nt, preferred_element_type=F32)
        acc_ref[corner, :, 0:AROWS] = piece
    total = acc_ref[0]
    for corner in range(1, 4):
        total = total + pltpu.roll(acc_ref[corner], (corner >> 1) * EY + (corner & 1), 1)
    for half in range(2):
        for ch in range(3):
            row = half * HALF + EZ * ch
            to = half * 128 + SZ * ch + OFF
            wide_ref[to : to + EZ, :] = total[row : row + EZ]
    deep_ref[...] = wide_ref[0:128, :].T[0:GROWS]
    vel_ref[...] = wide_ref[128:256, :].T[0:GROWS]
    lane = lane_index(GROUP)
    place = channel_lane(lane)
    low_msg = jnp.zeros((GROUP, 128), F32)
    high_msg = jnp.zeros((GROUP, 128), F32)
    for j in range(5):
        rows = slice(GROUP * j, GROUP * (j + 1))
        deep = deep_ref[rows, :]
        vel = vel_ref[rows, :]
        inside = (place >= 8 * j) & (place < 8 * j + LAYERS)
        low_msg = jnp.where(inside, shift_lanes(deep, 8 * j - OFF), low_msg)
        high_msg = jnp.where(inside, shift_lanes(deep, 8 * j - CZ), high_msg)
        inside = (place >= 8 * j + LAYERS) & (place < 8 * j + LAYERS + 2)
        low_msg = jnp.where(inside, shift_lanes(vel, 8 * j + LAYERS - OFF), low_msg)
        high_msg = jnp.where(inside, shift_lanes(vel, 8 * j + LAYERS - OFF - CZ), high_msg)
    low_ref[...] = low_msg
    high_ref[...] = jnp.where(lane >= 3 * SZ, counts_ref[0].astype(F32), high_msg)


def join_z_kernel(place_ref, deep_ref, vel_ref, before_ref, after_ref, deep_out, vel_out, low_ref, high_ref):
    place = channel_lane(lane_index(GROUP))
    before = jnp.where(place_ref[2] > 0, before_ref[...], 0.0)
    after = after_ref[...]
    deep_low, deep_high = place < LAYERS, (place >= SZ - LAYERS) & (place < SZ)
    vel_low = (place >= OFF) & (place < OFF + 2)
    vel_high = (place >= OFF + CZ) & (place < OFF + CZ + 2)
    for j in range(5):
        rows = slice(GROUP * j, GROUP * (j + 1))
        deep = jnp.where(
            deep_low,
            shift_lanes(before, -8 * j),
            jnp.where(deep_high, shift_lanes(after, SZ - LAYERS - 8 * j), 0.0),
        )
        vel = jnp.where(
            vel_low,
            shift_lanes(before, OFF - 8 * j - LAYERS),
            jnp.where(vel_high, shift_lanes(after, OFF + CZ - 8 * j - LAYERS), 0.0),
        )
        deep_out[rows, :] = deep_ref[rows, :] + deep
        vel_out[rows, :] = vel_ref[rows, :] + vel
    for x in range(EX):
        row = EY * x
        low_ref[LAYERS * x : LAYERS * (x + 1), :] = deep_out[row : row + LAYERS, :]
        high_ref[LAYERS * x : LAYERS * (x + 1), :] = deep_out[row + EY - LAYERS : row + EY, :]
        at = LAYERS * EX + 2 * x
        low_ref[at : at + 2, :] = vel_out[row : row + 2, :]
        high_ref[at : at + 2, :] = vel_out[row + EY - 2 : row + EY, :]


def join_y_kernel(deep_ref, vel_ref, after_ref, before_ref, deep_out, vel_out, low_ref, high_ref):
    deep_out[...] = jnp.zeros_like(deep_out)
    vel_out[...] = jnp.zeros_like(vel_out)
    for x in range(EX):
        row = EY * x
        deep_out[x, OFF : OFF + EY, :] = deep_ref[row : row + EY, :]
        deep_out[x, 0:LAYERS, :] += before_ref[LAYERS * x : LAYERS * (x + 1), :]
        deep_out[x, OFF + CY : OFF + CY + LAYERS, :] += after_ref[LAYERS * x : LAYERS * (x + 1), :]
        at = LAYERS * EX + 2 * x
        vel_out[x, OFF : OFF + EY, :] = vel_ref[row : row + EY, :]
        vel_out[x, OFF : OFF + 2, :] += before_ref[at : at + 2, :]
        vel_out[x, OFF + CY : OFF + CY + 2, :] += after_ref[at : at + 2, :]
    for x in range(LAYERS):
        low_ref[SY * x : SY * (x + 1), :] = deep_out[x, 0:SY, :]
        high_ref[SY * x : SY * (x + 1), :] = deep_out[EX - LAYERS + x, 0:SY, :]
    for x in range(2):
        at = SY * LAYERS + EY * x
        low_ref[at : at + EY, :] = vel_out[x, OFF : OFF + EY, :]
        high_ref[at : at + EY, :] = vel_out[EX - 2 + x, OFF : OFF + EY, :]


def gather_update(index, nodes_ref, part_ref, base_ref, w_ref, g_ref, out_ref, out_index):
    lanes = slice(index * CHUNK, (index + 1) * CHUNK)
    to = slice(out_index * CHUNK, (out_index + 1) * CHUNK)
    onehot = onehot_rows(base_ref, lanes)
    base_z = base_ref[2:3, lanes]
    rows = lax.broadcasted_iota(jnp.int32, (ZROWS, CHUNK), 0) - base_z
    at = rows == 0
    after = rows == 1

    def pick(mask, value):
        kept = jnp.where(mask, value, 0.0)
        total = kept[0:8]
        for t in range(1, ZROWS // 8):
            total = total + kept[8 * t : 8 * t + 8]
        return total

    moved = [jnp.zeros((8, CHUNK), F32) for _ in range(3)]
    velgrad = [[jnp.zeros((8, CHUNK), F32) for _ in range(3)] for _ in range(3)]
    damage_node = jnp.zeros((8, CHUNK), F32)
    rows_ab = 4 * ZROWS
    for corner in range(4):
        start = 2 * rows_ab * corner
        near = jnp.dot(nodes_ref[start : start + rows_ab, 0:AROWS], onehot, preferred_element_type=F32) + jnp.dot(
            nodes_ref[start + rows_ab : start + 2 * rows_ab, 0:AROWS], onehot, preferred_element_type=F32
        )
        for c, mask in enumerate((at, after)):
            k = 2 * corner + c
            weight = w_ref[k : k + 1, lanes]
            slope = [g_ref[j, k : k + 1, lanes] for j in range(3)]
            for i in range(3):
                value = pick(mask, near[ZROWS * i : ZROWS * (i + 1)])
                moved[i] = moved[i] + value * weight
                for j in range(3):
                    velgrad[i][j] = velgrad[i][j] + value * slope[j]
            damage_node = damage_node + pick(mask, near[3 * ZROWS : 4 * ZROWS]) * weight
    moved = [jnp.sum(v, axis=0, keepdims=True) for v in moved]
    velgrad = [[jnp.sum(v, axis=0, keepdims=True) for v in row] for row in velgrad]
    damage_node = jnp.sum(damage_node, axis=0, keepdims=True)

    def field(i):
        return part_ref[i : i + 1, lanes]

    deform = [[field(5 + 3 * i + j) for j in range(3)] for i in range(3)]
    stretch = [[(1.0 if i == j else 0.0) + time_step * velgrad[i][j] for j in range(3)] for i in range(3)]
    mapped = [
        [
            stretch[i][0] * deform[0][j] + stretch[i][1] * deform[1][j] + stretch[i][2] * deform[2][j]
            for j in range(3)
        ]
        for i in range(3)
    ]
    jacobian = (
        mapped[0][0] * (mapped[1][1] * mapped[2][2] - mapped[1][2] * mapped[2][1])
        - mapped[0][1] * (mapped[1][0] * mapped[2][2] - mapped[1][2] * mapped[2][0])
        + mapped[0][2] * (mapped[1][0] * mapped[2][1] - mapped[1][1] * mapped[2][0])
    )
    left = {}
    for i in range(3):
        for j in range(i, 3):
            left[i, j] = left[j, i] = (
                mapped[i][0] * mapped[j][0] + mapped[i][1] * mapped[j][1] + mapped[i][2] * mapped[j][2]
            )
    damaged = jnp.maximum(field(23), damage_node)
    degrade = (1.0 - damaged) ** 2
    pressure = bulk_coef * (jacobian - 1.0)
    energy = (
        0.5 * shear_mod * (left[0, 0] + left[1, 1] + left[2, 2] - 3.0) + 0.5 * bulk_coef * (jacobian - 1.0) ** 2
    )
    out_ref[0:2, to] = part_ref[0:2, lanes]
    for i in range(3):
        out_ref[2 + i : 3 + i, to] = moved[i]
        out_ref[25 + i : 26 + i, to] = field(25 + i) + time_step * moved[i]
        for j in range(3):
            out_ref[5 + 3 * i + j : 6 + 3 * i + j, to] = mapped[i][j]
            term = shear_mod * (left[i, j] - (1.0 if i == j else 0.0))
            if i == j:
                term = term + pressure
            out_ref[14 + 3 * i + j : 15 + 3 * i + j, to] = degrade * term
    out_ref[23:24, to] = damaged
    out_ref[24:25, to] = jnp.maximum(field(24), energy)


def relax_kernel(
    axis_sizes,
    place_ref,
    deep_ref,
    vel_ref,
    after_ref,
    before_ref,
    part_ref,
    base_ref,
    w_ref,
    g_ref,
    damage_hbm,
    nodes_ref,
    tail_ref,
    sums_ref,
    one_ref,
    two_ref,
    keep_ref,
    add_ref,
    spread_ref,
    inverse_ref,
    fv_ref,
    fd_ref,
    damage_ref,
    sem,
):
    count_x, count_y, count_z = axis_sizes
    sums_ref[...] = jnp.zeros_like(sums_ref)
    for xd in range(SX):
        if OFF <= xd < OFF + EX:
            sums_ref[xd] = deep_ref[xd - OFF]
        if xd < LAYERS:
            sums_ref[xd, 0:SY, :] += before_ref[SY * xd : SY * (xd + 1), :]
        if xd >= SX - LAYERS:
            at = SY * (xd - SX + LAYERS)
            sums_ref[xd, 0:SY, :] += after_ref[at : at + SY, :]
    lane = lane_index(PITCH)
    pos_x = place_ref[0] * CX - WIDE + three(lane, SZ, 0, PACK, 2 * PACK)
    pos_y = place_ref[1] * CY - WIDE + lax.broadcasted_iota(jnp.int32, (PITCH, 128), 0)
    pos_z = place_ref[2] * CZ - WIDE + lane - three(lane, SZ, 0, SZ, 2 * SZ)
    inside_yz = (
        (lane < 3 * SZ) & (pos_y >= 0) & (pos_y < count_y * CY) & (pos_z >= 0) & (pos_z < count_z * CZ)
    )
    for j in range(PACK):
        first, second, third = sums_ref[j], sums_ref[j + PACK], sums_ref[j + 2 * PACK]
        mass = three(lane, SZ, first, shift_lanes(second, SZ), shift_lanes(third, 2 * SZ))
        damage = three(lane, SZ, shift_lanes(first, -SZ), second, shift_lanes(third, SZ))
        drive = three(lane, SZ, shift_lanes(first, -2 * SZ), shift_lanes(second, -SZ), third)
        mask = (inside_yz & (pos_x + j >= 0) & (pos_x + j < count_x * CX)).astype(F32)
        inverse = mask / jnp.maximum(mass, mass_floor)
        drive = (2.0 * relax_rate) * (drive * inverse)
        keep_ref[j] = (1.0 - relax_rate * (1.0 + 6.0 * length_sq)) * mask - drive
        add_ref[j] = drive
        spread_ref[j] = (relax_rate * length_sq) * mask
        one_ref[j] = damage * inverse
        inverse_ref[j] = inverse
    source, target = one_ref, two_ref
    for _ in range(SUBSTEPS):
        for j in range(PACK):
            centre = source[j]
            lower = source[j - 1] if j > 0 else shift_lanes(source[PACK - 1], SZ)
            upper = source[j + 1] if j < PACK - 1 else shift_lanes(source[0], -SZ)
            around = (
                (lower + upper)
                + (pltpu.roll(centre, 1, 0) + pltpu.roll(centre, PITCH - 1, 0))
                + (shift_lanes(centre, 1) + shift_lanes(centre, -1))
            )
            target[j] = (centre * keep_ref[j] + add_ref[j]) + spread_ref[j] * around
        source, target = target, source
    for x in range(CX):
        xd = x + WIDE
        value = shift_lanes(source[xd % PACK], -SZ * (xd // PACK) - WIDE)
        damage_ref[x] = value[WIDE : WIDE + CY, 0:CZ]
    move = pltpu.make_async_copy(damage_ref, damage_hbm, sem)
    move.start()
    fv_ref[...] = jnp.zeros_like(fv_ref)
    fd_ref[...] = jnp.zeros_like(fd_ref)
    vel_at = SY * LAYERS
    lane = lane_index(EY)
    for x in range(EX):
        vel = vel_ref[x, OFF : OFF + EY, :]
        if x < 2:
            vel = vel + before_ref[vel_at + EY * x : vel_at + EY * (x + 1), :]
        if x >= EX - 2:
            at = vel_at + EY * (x - EX + 2)
            vel = vel + after_ref[at : at + EY, :]
        slot, group = (x + OFF) % PACK, (x + OFF) // PACK
        inverse = inverse_ref[slot, OFF : OFF + EY, :]
        vel = three(lane, ZROWS, *(shift_lanes(vel, (ZROWS - SZ) * ch - OFF) for ch in range(3)))
        inverse = three(lane, ZROWS, *(shift_lanes(inverse, ZROWS * ch - SZ * group - OFF) for ch in range(3)))
        fv_ref[EY * x : EY * (x + 1), :] = vel * inverse
        fd_ref[EY * x : EY * (x + 1), :] = shift_lanes(source[slot], -SZ * group - OFF)[OFF : OFF + EY, :]
    nodes = jnp.concatenate([fv_ref[...].T[0 : 3 * ZROWS], fd_ref[...].T[0:ZROWS]], axis=0)
    for corner in range(4):
        shift = (corner >> 1) * EY + (corner & 1)
        value = nodes if shift == 0 else pltpu.roll(nodes, 256 - shift, 1)
        high = value.astype(BF16)
        low = (value - high.astype(F32)).astype(BF16)
        start = 8 * ZROWS * corner
        nodes_ref[start : start + 4 * ZROWS, :] = high
        nodes_ref[start + 4 * ZROWS : start + 8 * ZROWS, :] = low
    for index in range(TAIL // CHUNK):
        gather_update((COUNT - TAIL) // CHUNK + index, nodes_ref, part_ref, base_ref, w_ref, g_ref, tail_ref, index)
    move.wait()


def head_kernel(
    counts_ref, prior_ref, nodes_ref, tail_ref, part_ref, base_ref, w_ref, g_ref, out_hbm, head_ref, left_ref, zero_ref, sems
):
    prior = prior_ref[0, 3 * SZ].astype(jnp.int32)
    left = MOST - counts_ref[0]
    zero_ref[...] = jnp.zeros_like(zero_ref)
    blanks = []
    for i in range(MOST):
        to = pl.ds(pl.multiple_of((NBIN + MOST - 1 - i) * BIN, BIN), BIN)
        blanks.append((i < MOST - prior, pltpu.make_async_copy(zero_ref, out_hbm.at[:, to], sems.at[2 + i])))
    for wanted, move in blanks:
        pl.when(wanted)(move.start)
    for i in range(MOST):
        bins = slice(i * BIN, (i + 1) * BIN)
        left_ref[:, bins] = jnp.where(i < left, tail_ref[:, bins], 0.0)
    to = pl.ds(pl.multiple_of((prior + NBIN - MOST) * BIN, BIN), TAIL)
    own = pltpu.make_async_copy(left_ref, out_hbm.at[:, to], sems.at[0])
    own.start()
    for index in range((COUNT - TAIL) // CHUNK):
        gather_update(index, nodes_ref, part_ref, base_ref, w_ref, g_ref, head_ref, index)
    to = pl.ds(pl.multiple_of(prior * BIN, BIN), COUNT - TAIL)
    stay = pltpu.make_async_copy(head_ref, out_hbm.at[:, to], sems.at[1])
    stay.start()
    for wanted, move in blanks:
        pl.when(wanted)(move.wait)
    own.wait()
    stay.wait()


def arrive_kernel(prior_ref, recv_ref, partial_hbm, out_hbm, sems):
    prior = prior_ref[0, 3 * SZ].astype(jnp.int32)
    moves = []
    for slot in range(MOST):
        source = pl.ds(pl.multiple_of(jnp.minimum(MOST - prior + slot, MOST - 1) * BIN, BIN), BIN)
        moves.append(
            (
                slot < prior,
                pltpu.make_async_copy(recv_ref.at[:, source], out_hbm.at[:, slot * BIN : (slot + 1) * BIN], sems.at[slot]),
            )
        )
    for wanted, move in moves:
        pl.when(wanted)(move.start)
    for wanted, move in moves:
        pl.when(wanted)(move.wait)


def shape(*dims, kind=F32):
    return jax.ShapeDtypeStruct(dims, kind)


SMEM = pltpu.SMEM
HBM = pltpu.HBM


def call(kernel, out_shape, spaces, args, out_spaces=None, scratch=(), flops=0, aliases=None, limit=None):
    leaves = jax.tree.leaves(out_shape)
    out_spaces = out_spaces or [VMEM] * len(leaves)
    out_specs = [pl.BlockSpec(memory_space=s) for s in out_spaces]
    return pl.pallas_call(
        kernel,
        out_shape=out_shape,
        in_specs=[pl.BlockSpec(memory_space=s) for s in spaces],
        out_specs=tuple(out_specs) if isinstance(out_shape, tuple) else out_specs[0],
        scratch_shapes=list(scratch),
        input_output_aliases=aliases or {},
        compiler_params=pltpu.CompilerParams(vmem_limit_bytes=(limit or 48 * 1024) * 1024),
        cost_estimate=pl.CostEstimate(flops=flops, bytes_accessed=2000000, transcendentals=0),
    )(*args)


def exchange(low, high, axis, ring=False):
    count = lax.axis_size(axis)
    up = [(i, (i + 1) % count) for i in range(count if ring else count - 1)]
    down = [(i + 1, i) for i in range(count - 1)]
    after = lax.ppermute(low, axis, down)
    return lax.ppermute(high, axis, up), after


def per_device(particles, stencil_base, weights, gradients, counts):
    axes = ("gx", "gy", "gz")
    place = jnp.stack([lax.axis_index(a) for a in axes]).astype(jnp.int32)
    sizes = tuple(lax.axis_size(a) for a in axes)
    ring = [(i, (i + 1) % sizes[2]) for i in range(sizes[2])]
    inputs = (particles, stencil_base, weights, gradients)
    deep, vel, low, high = call(
        scatter_kernel,
        (VMEM((GROWS, 128), F32), VMEM((GROWS, 128), F32), VMEM((GROUP, 128), F32), VMEM((GROUP, 128), F32)),
        [SMEM] + [HBM] * 4,
        (counts,) + inputs,
        scratch=[
            VMEM((FIELDS, COUNT), F32),
            VMEM((3, COUNT), jnp.int32),
            VMEM((8, COUNT), F32),
            VMEM((3, 8, COUNT), F32),
            VMEM((4, 2 * HALF, 256), F32),
            VMEM((256, 256), F32),
            VMEM((2, 6, 8, COUNT), F32),
            VMEM((8 * HALF, 2 * COUNT), BF16),
            VMEM((AROWS, COUNT), BF16),
            pltpu.SemaphoreType.DMA((4,)),
        ],
        limit=SCATTER_KIB,
    )
    before_z, after_z = exchange(low, high, "gz", ring=True)
    message = LAYERS * EX + 2 * EX
    deep, vel, low, high = call(
        join_z_kernel,
        (shape(GROWS, 128), shape(GROWS, 128), shape(message, 128), shape(message, 128)),
        [SMEM] + [VMEM] * 4,
        (place, deep, vel, before_z, after_z),
    )
    before, after = exchange(low, high, "gy")
    message = LAYERS * SY + 2 * EY
    deep, vel, low, high = call(
        join_y_kernel,
        (shape(EX, PITCH, 128), shape(EX, PITCH, 128), shape(message, 128), shape(message, 128)),
        [VMEM] * 4,
        (deep, vel, after, before),
    )
    before, after = exchange(low, high, "gx")

    def relax(*refs):
        relax_kernel(sizes, *refs)

    damage, nodes, tail = call(
        relax,
        (shape(CX, CY, CZ), shape(32 * ZROWS, 256, kind=BF16), shape(FIELDS, TAIL)),
        [SMEM] + [VMEM] * 8,
        (place, deep, vel, after, before) + inputs,
        out_spaces=[HBM, VMEM, VMEM],
        scratch=[VMEM((SX, PITCH, 128), F32)]
        + [VMEM((PACK, PITCH, 128), F32)] * 6
        + [VMEM((256, 128), F32)] * 2
        + [VMEM((CX, CY, CZ), F32), pltpu.SemaphoreType.DMA],
    )
    recv = lax.ppermute(tail, "gz", ring)
    prior = before_z[0:8]
    own = call(
        head_kernel,
        shape(FIELDS, SLOTS),
        [SMEM] + [VMEM] * 7,
        (counts, prior, nodes, tail) + inputs,
        out_spaces=[HBM],
        scratch=[
            VMEM((FIELDS, COUNT - TAIL), F32),
            VMEM((FIELDS, TAIL), F32),
            VMEM((FIELDS, BIN), F32),
            pltpu.SemaphoreType.DMA((2 + MOST,)),
        ],
        flops=2 * 1280 * 256 * 1024,
    )
    migrated = call(
        arrive_kernel,
        shape(FIELDS, SLOTS),
        [VMEM, VMEM, HBM],
        (prior, recv, own),
        out_spaces=[HBM],
        scratch=[pltpu.SemaphoreType.DMA((MOST,))],
        aliases={2: 0},
    )
    return (migrated, damage)


def solution(mesh):
    return jax.shard_map(
        per_device,
        mesh=mesh,
        in_specs=(
            P(None, ("gx", "gy", "gz")),
            P(None, ("gx", "gy", "gz")),
            P(None, ("gx", "gy", "gz")),
            P(None, None, ("gx", "gy", "gz")),
            P(("gx", "gy", "gz")),
        ),
        out_specs=(P(None, ("gx", "gy", "gz")), P("gx", "gy", "gz")),
        check_vma=False,
    )
```

```python
import jax
import jax.numpy as jnp
from jax import lax
from jax.experimental import pallas as pl
from jax.experimental.pallas import tpu as pltpu
from jax.sharding import PartitionSpec as P

CX = 8
CY = 16
CZ = 32
NBIN = 16
BIN = 128
SUBSTEPS = 4
FIELDS = 28
MOST = 8
COUNT = NBIN * BIN
TAIL = MOST * BIN
SLOTS = (NBIN + MOST) * BIN

time_step = 0.1
relax_rate = 0.2
length_sq = 0.6
shear_mod = 1.0
bulk_coef = 1.5
mass_floor = 0.5

EX = CX + 2
EY = CY + 2
EZ = CZ + 2
WIDE = SUBSTEPS + 1
LAYERS = WIDE + 1
SX = CX + 2 * WIDE
SY = CY + 2 * WIDE
SZ = CZ + 2 * WIDE
OFF = WIDE - 1
PITCH = 32
AROWS = 176
GROWS = 200
GROUP = 40
HALF = 104
PACK = SX // 3
ZROWS = 40
CHUNK = 256
SENT = tuple(range(14)) + tuple(range(23, FIELDS))
AXES = ("gx", "gy", "gz")
F32 = jnp.float32
BF16 = jnp.bfloat16
SCATTER_KIB = 56000
VMEM = pltpu.VMEM


def shift_lanes(value, by):
    by = by % 128
    return value if by == 0 else pltpu.roll(value, by, 1)


def channel_lane(lane):
    return jnp.where(
        lane < SZ, lane, jnp.where(lane < 2 * SZ, lane - SZ, jnp.where(lane < 3 * SZ, lane - 2 * SZ, 1000))
    )


def three(lane, width, a, b, c):
    return jnp.where(lane < width, a, jnp.where(lane < 2 * width, b, c))


def lane_index(rows):
    return lax.broadcasted_iota(jnp.int32, (rows, 128), 1)


def onehot_rows(base_ref, lanes):
    xy = base_ref[0:1, lanes] * EY + base_ref[1:2, lanes]
    rows = lax.broadcasted_iota(jnp.int32, (AROWS, CHUNK), 0)
    return jnp.where(rows == xy, 1.0, 0.0).astype(BF16)


def scatter_kernel(
    counts_ref,
    part_hbm,
    base_hbm,
    w_hbm,
    g_hbm,
    deep_ref,
    vel_ref,
    odd_ref,
    even_ref,
    part_ref,
    base_ref,
    w_ref,
    g_ref,
    acc_ref,
    wide_ref,
    term_ref,
    rows_ref,
    onehot_ref,
    sems,
):
    moves = [
        pltpu.make_async_copy(source, target, sems.at[i])
        for i, (source, target) in enumerate(
            ((base_hbm, base_ref), (part_hbm, part_ref), (w_hbm, w_ref), (g_hbm, g_ref))
        )
    ]
    for move in moves:
        move.start()
    acc_ref[...] = jnp.zeros_like(acc_ref)
    wide_ref[...] = jnp.zeros_like(wide_ref)
    moves[0].wait()
    for index in range(COUNT // CHUNK):
        lanes = slice(index * CHUNK, (index + 1) * CHUNK)
        onehot_ref[:, lanes] = onehot_rows(base_ref, lanes)
    for move in moves[1:]:
        move.wait()
    for index in range(COUNT // CHUNK):
        lanes = slice(index * CHUNK, (index + 1) * CHUNK)
        minus_vol = -time_step * part_ref[1:2, lanes]
        share = part_ref[0:1, lanes] * w_ref[:, lanes]
        slope = [g_ref[j, :, lanes] for j in range(3)]
        terms = [share, share * part_ref[23:24, lanes], share * part_ref[24:25, lanes]]
        for i in range(3):
            row = 14 + 3 * i
            pull = (
                part_ref[row : row + 1, lanes] * slope[0]
                + part_ref[row + 1 : row + 2, lanes] * slope[1]
                + part_ref[row + 2 : row + 3, lanes] * slope[2]
            )
            terms.append(share * part_ref[2 + i : 3 + i, lanes] + minus_vol * pull)
        for ch, term in enumerate(terms):
            high = term.astype(BF16).astype(F32)
            term_ref[0, ch, :, lanes] = high
            term_ref[1, ch, :, lanes] = term - high
    nt = (((1,), (1,)), ((), ()))
    for corner in range(4):
        k = 2 * corner
        for index in range(COUNT // CHUNK):
            lanes = slice(index * CHUNK, (index + 1) * CHUNK)
            sub = lax.broadcasted_iota(jnp.int32, (8, CHUNK), 0) - base_ref[2:3, lanes]
            for part in range(2):
                tiles = {}
                for tile in range(HALF // 8):
                    first = [(ch, EZ * ch - 8 * tile) for ch in range(3) if EZ * ch < 8 * tile + 8 and EZ * (ch + 1) > 8 * tile]
                    for half in range(2):
                        value = jnp.zeros((8, CHUNK), F32)
                        for ch, at in first:
                            value = jnp.where(sub == at, term_ref[part, 3 * half + ch, k : k + 1, lanes], value)
                            value = jnp.where(sub == at + 1, term_ref[part, 3 * half + ch, k + 1 : k + 2, lanes], value)
                        tiles[half * (HALF // 8) + tile] = value
                to = slice(part * COUNT + index * CHUNK, part * COUNT + (index + 1) * CHUNK)
                for pair in range(HALF // 8):
                    row = 2 * HALF * corner + 16 * pair
                    rows_ref[row : row + 16, to] = jnp.concatenate([tiles[2 * pair], tiles[2 * pair + 1]], axis=0).astype(BF16)
        rows = slice(2 * HALF * corner, 2 * HALF * (corner + 1))
        piece = lax.dot_general(rows_ref[rows, 0:COUNT], onehot_ref[...], nt, preferred_element_type=F32)
        piece = piece + lax.dot_general(rows_ref[rows, COUNT:], onehot_ref[...], nt, preferred_element_type=F32)
        acc_ref[corner, :, 0:AROWS] = piece
    total = acc_ref[0]
    for corner in range(1, 4):
        total = total + pltpu.roll(acc_ref[corner], (corner >> 1) * EY + (corner & 1), 1)
    for half in range(2):
        for ch in range(3):
            row = half * HALF + EZ * ch
            to = half * 128 + SZ * ch + OFF
            wide_ref[to : to + EZ, :] = total[row : row + EZ]
    deep_ref[...] = wide_ref[0:128, :].T[0:GROWS]
    vel_ref[...] = wide_ref[128:256, :].T[0:GROWS]
    lane = lane_index(GROUP)
    place = channel_lane(lane)
    low_msg = jnp.zeros((GROUP, 128), F32)
    high_msg = jnp.zeros((GROUP, 128), F32)
    for j in range(5):
        rows = slice(GROUP * j, GROUP * (j + 1))
        deep = deep_ref[rows, :]
        vel = vel_ref[rows, :]
        inside = (place >= 8 * j) & (place < 8 * j + LAYERS)
        low_msg = jnp.where(inside, shift_lanes(deep, 8 * j - OFF), low_msg)
        high_msg = jnp.where(inside, shift_lanes(deep, 8 * j - CZ), high_msg)
        inside = (place >= 8 * j + LAYERS) & (place < 8 * j + LAYERS + 2)
        low_msg = jnp.where(inside, shift_lanes(vel, 8 * j + LAYERS - OFF), low_msg)
        high_msg = jnp.where(inside, shift_lanes(vel, 8 * j + LAYERS - OFF - CZ), high_msg)
    high_msg = jnp.where(lane >= 3 * SZ, counts_ref[0].astype(F32), high_msg)
    is_even = lax.rem(lax.axis_index(AXES[2]), 2) == 0
    odd_ref[...] = jnp.where(is_even, low_msg, high_msg)
    even_ref[...] = jnp.where(is_even, high_msg, low_msg)


def join_z_kernel(pairs, deep_ref, vel_ref, odd_ref, even_ref, deep_out, vel_out, prior_ref, *messages):
    place = channel_lane(lane_index(GROUP))
    is_even = lax.rem(lax.axis_index(AXES[2]), 2) == 0
    before = jnp.where(is_even, odd_ref[...], even_ref[...])
    after = jnp.where(is_even, even_ref[...], odd_ref[...])
    prior_ref[...] = before[0:8]
    before = jnp.where(lax.axis_index(AXES[2]) > 0, before, 0.0)
    deep_low, deep_high = place < LAYERS, (place >= SZ - LAYERS) & (place < SZ)
    vel_low = (place >= OFF) & (place < OFF + 2)
    vel_high = (place >= OFF + CZ) & (place < OFF + CZ + 2)
    for j in range(5):
        rows = slice(GROUP * j, GROUP * (j + 1))
        deep = jnp.where(
            deep_low,
            shift_lanes(before, -8 * j),
            jnp.where(deep_high, shift_lanes(after, SZ - LAYERS - 8 * j), 0.0),
        )
        vel = jnp.where(
            vel_low,
            shift_lanes(before, OFF - 8 * j - LAYERS),
            jnp.where(vel_high, shift_lanes(after, OFF + CZ - 8 * j - LAYERS), 0.0),
        )
        deep_out[rows, :] = deep_ref[rows, :] + deep
        vel_out[rows, :] = vel_ref[rows, :] + vel
    for i in range(pairs):
        is_lower = lax.axis_index(AXES[1]) == i
        for x in range(EX):
            row = EY * x
            messages[i][LAYERS * x : LAYERS * (x + 1), :] = jnp.where(
                is_lower, deep_out[row + EY - LAYERS : row + EY, :], deep_out[row : row + LAYERS, :]
            )
            at = LAYERS * EX + 2 * x
            messages[i][at : at + 2, :] = jnp.where(
                is_lower, vel_out[row + EY - 2 : row + EY, :], vel_out[row : row + 2, :]
            )


def join_y_kernel(pairs, deep_ref, vel_ref, *refs):
    received, (deep_out, vel_out, low_ref, high_ref, before_ref, after_ref) = refs[:pairs], refs[pairs:]
    before = jnp.zeros_like(before_ref)
    after = jnp.zeros_like(after_ref)
    for i in range(pairs):
        before = jnp.where(lax.axis_index(AXES[1]) == i + 1, received[i][...], before)
        after = jnp.where(lax.axis_index(AXES[1]) == i, received[i][...], after)
    before_ref[...] = before
    after_ref[...] = after
    deep_out[...] = jnp.zeros_like(deep_out)
    vel_out[...] = jnp.zeros_like(vel_out)
    for x in range(EX):
        row = EY * x
        deep_out[x, OFF : OFF + EY, :] = deep_ref[row : row + EY, :]
        deep_out[x, 0:LAYERS, :] += before_ref[LAYERS * x : LAYERS * (x + 1), :]
        deep_out[x, OFF + CY : OFF + CY + LAYERS, :] += after_ref[LAYERS * x : LAYERS * (x + 1), :]
        at = LAYERS * EX + 2 * x
        vel_out[x, OFF : OFF + EY, :] = vel_ref[row : row + EY, :]
        vel_out[x, OFF : OFF + 2, :] += before_ref[at : at + 2, :]
        vel_out[x, OFF + CY : OFF + CY + 2, :] += after_ref[at : at + 2, :]
    for x in range(LAYERS):
        low_ref[SY * x : SY * (x + 1), :] = deep_out[x, 0:SY, :]
        high_ref[SY * x : SY * (x + 1), :] = deep_out[EX - LAYERS + x, 0:SY, :]
    for x in range(2):
        at = SY * LAYERS + EY * x
        low_ref[at : at + EY, :] = vel_out[x, OFF : OFF + EY, :]
        high_ref[at : at + EY, :] = vel_out[EX - 2 + x, OFF : OFF + EY, :]


def determinant(m):
    return (
        m[0][0] * (m[1][1] * m[2][2] - m[1][2] * m[2][1])
        - m[0][1] * (m[1][0] * m[2][2] - m[1][2] * m[2][0])
        + m[0][2] * (m[1][0] * m[2][1] - m[1][1] * m[2][0])
    )


def left_product(m, i, j):
    return m[i][0] * m[j][0] + m[i][1] * m[j][1] + m[i][2] * m[j][2]


def stress_rows(mapped, damaged):
    degrade = (1.0 - damaged) ** 2
    pressure = bulk_coef * (determinant(mapped) - 1.0)
    rows = {}
    for i in range(3):
        for j in range(i, 3):
            term = shear_mod * (left_product(mapped, i, j) - (1.0 if i == j else 0.0))
            if i == j:
                term = term + pressure
            rows[14 + 3 * i + j] = rows[14 + 3 * j + i] = degrade * term
    return rows


def unpack(packed_ref, out_ref, left=None):
    rows = {f: packed_ref[MOST * at : MOST * (at + 1), :] for at, f in enumerate(SENT)}
    rows.update(stress_rows([[rows[5 + 3 * i + j] for j in range(3)] for i in range(3)], rows[23]))
    for f in range(FIELDS):
        value = rows[f]
        if left is not None:
            value = jnp.where(lax.broadcasted_iota(jnp.int32, (MOST, BIN), 0) < left, value, 0.0)
        for t in range(MOST):
            out_ref[f : f + 1, t * BIN : (t + 1) * BIN] = value[t : t + 1]


def gather_update(index, nodes_ref, part_ref, base_ref, w_ref, g_ref, out_ref, out_index, packed):
    lanes = slice(index * CHUNK, (index + 1) * CHUNK)
    to = slice(out_index * CHUNK, (out_index + 1) * CHUNK)
    onehot = onehot_rows(base_ref, lanes)
    base_z = base_ref[2:3, lanes]
    rows = lax.broadcasted_iota(jnp.int32, (ZROWS, CHUNK), 0) - base_z
    at = rows == 0
    after = rows == 1

    def pick(mask, value):
        kept = jnp.where(mask, value, 0.0)
        total = kept[0:8]
        for t in range(1, ZROWS // 8):
            total = total + kept[8 * t : 8 * t + 8]
        return total

    moved = [jnp.zeros((8, CHUNK), F32) for _ in range(3)]
    velgrad = [[jnp.zeros((8, CHUNK), F32) for _ in range(3)] for _ in range(3)]
    damage_node = jnp.zeros((8, CHUNK), F32)
    rows_ab = 4 * ZROWS
    for corner in range(4):
        start = 2 * rows_ab * corner
        near = jnp.dot(nodes_ref[start : start + rows_ab, 0:AROWS], onehot, preferred_element_type=F32) + jnp.dot(
            nodes_ref[start + rows_ab : start + 2 * rows_ab, 0:AROWS], onehot, preferred_element_type=F32
        )
        for c, mask in enumerate((at, after)):
            k = 2 * corner + c
            weight = w_ref[k : k + 1, lanes]
            slope = [g_ref[j, k : k + 1, lanes] for j in range(3)]
            for i in range(3):
                value = pick(mask, near[ZROWS * i : ZROWS * (i + 1)])
                moved[i] = moved[i] + value * weight
                for j in range(3):
                    velgrad[i][j] = velgrad[i][j] + value * slope[j]
            damage_node = damage_node + pick(mask, near[3 * ZROWS : 4 * ZROWS]) * weight
    moved = [jnp.sum(v, axis=0, keepdims=True) for v in moved]
    velgrad = [[jnp.sum(v, axis=0, keepdims=True) for v in row] for row in velgrad]
    damage_node = jnp.sum(damage_node, axis=0, keepdims=True)

    def field(i):
        return part_ref[i : i + 1, lanes]

    deform = [[field(5 + 3 * i + j) for j in range(3)] for i in range(3)]
    stretch = [[(1.0 if i == j else 0.0) + time_step * velgrad[i][j] for j in range(3)] for i in range(3)]
    mapped = [
        [
            stretch[i][0] * deform[0][j] + stretch[i][1] * deform[1][j] + stretch[i][2] * deform[2][j]
            for j in range(3)
        ]
        for i in range(3)
    ]
    damaged = jnp.maximum(field(23), damage_node)
    jacobian = determinant(mapped)
    trace = left_product(mapped, 0, 0) + left_product(mapped, 1, 1) + left_product(mapped, 2, 2)
    energy = 0.5 * shear_mod * (trace - 3.0) + 0.5 * bulk_coef * (jacobian - 1.0) ** 2
    rows = {f: field(f) for f in range(2)}
    for i in range(3):
        rows[2 + i] = moved[i]
        rows[25 + i] = field(25 + i) + time_step * moved[i]
        for j in range(3):
            rows[5 + 3 * i + j] = mapped[i][j]
    rows[23] = damaged
    rows[24] = jnp.maximum(field(24), energy)
    if packed:
        for at, f in enumerate(SENT):
            for t in range(CHUNK // BIN):
                row = MOST * (MOST * (at // MOST) + out_index * (CHUNK // BIN) + t) + at % MOST
                out_ref[row : row + 1, :] = rows[f][:, t * BIN : (t + 1) * BIN]
    else:
        rows.update(stress_rows(mapped, damaged))
        for f in range(FIELDS):
            out_ref[f : f + 1, to] = rows[f]


def relax_kernel(
    axis_sizes,
    deep_ref,
    vel_ref,
    after_ref,
    before_ref,
    part_ref,
    base_ref,
    w_ref,
    g_ref,
    damage_hbm,
    nodes_ref,
    tail_ref,
    sums_ref,
    one_ref,
    two_ref,
    keep_ref,
    add_ref,
    spread_ref,
    inverse_ref,
    fv_ref,
    fd_ref,
    damage_ref,
    rows_ref,
    sem,
):
    count_x, count_y, count_z = axis_sizes
    sums_ref[...] = jnp.zeros_like(sums_ref)
    for xd in range(SX):
        if OFF <= xd < OFF + EX:
            sums_ref[xd] = deep_ref[xd - OFF]
        if xd < LAYERS:
            sums_ref[xd, 0:SY, :] += before_ref[SY * xd : SY * (xd + 1), :]
        if xd >= SX - LAYERS:
            at = SY * (xd - SX + LAYERS)
            sums_ref[xd, 0:SY, :] += after_ref[at : at + SY, :]
    lane = lane_index(PITCH)
    pos_x = lax.axis_index(AXES[0]) * CX - WIDE + three(lane, SZ, 0, PACK, 2 * PACK)
    pos_y = lax.axis_index(AXES[1]) * CY - WIDE + lax.broadcasted_iota(jnp.int32, (PITCH, 128), 0)
    pos_z = lax.axis_index(AXES[2]) * CZ - WIDE + lane - three(lane, SZ, 0, SZ, 2 * SZ)
    inside_yz = (
        (lane < 3 * SZ) & (pos_y >= 0) & (pos_y < count_y * CY) & (pos_z >= 0) & (pos_z < count_z * CZ)
    )
    for j in range(PACK):
        first, second, third = sums_ref[j], sums_ref[j + PACK], sums_ref[j + 2 * PACK]
        mass = three(lane, SZ, first, shift_lanes(second, SZ), shift_lanes(third, 2 * SZ))
        damage = three(lane, SZ, shift_lanes(first, -SZ), second, shift_lanes(third, SZ))
        drive = three(lane, SZ, shift_lanes(first, -2 * SZ), shift_lanes(second, -SZ), third)
        mask = (inside_yz & (pos_x + j >= 0) & (pos_x + j < count_x * CX)).astype(F32)
        inverse = mask / jnp.maximum(mass, mass_floor)
        drive = (2.0 * relax_rate) * (drive * inverse)
        keep_ref[j] = (1.0 - relax_rate * (1.0 + 6.0 * length_sq)) * mask - drive
        add_ref[j] = drive
        spread_ref[j] = (relax_rate * length_sq) * mask
        one_ref[j] = damage * inverse
        inverse_ref[j] = inverse
    source, target = one_ref, two_ref
    for _ in range(SUBSTEPS):
        for j in range(PACK):
            centre = source[j]
            lower = source[j - 1] if j > 0 else shift_lanes(source[PACK - 1], SZ)
            upper = source[j + 1] if j < PACK - 1 else shift_lanes(source[0], -SZ)
            around = (
                (lower + upper)
                + (pltpu.roll(centre, 1, 0) + pltpu.roll(centre, PITCH - 1, 0))
                + (shift_lanes(centre, 1) + shift_lanes(centre, -1))
            )
            target[j] = (centre * keep_ref[j] + add_ref[j]) + spread_ref[j] * around
        source, target = target, source
    for x in range(CX):
        xd = x + WIDE
        value = shift_lanes(source[xd % PACK], -SZ * (xd // PACK) - WIDE)
        damage_ref[x] = value[WIDE : WIDE + CY, 0:CZ]
    move = pltpu.make_async_copy(damage_ref, damage_hbm, sem)
    move.start()
    fv_ref[...] = jnp.zeros_like(fv_ref)
    fd_ref[...] = jnp.zeros_like(fd_ref)
    vel_at = SY * LAYERS
    lane = lane_index(EY)
    for x in range(EX):
        vel = vel_ref[x, OFF : OFF + EY, :]
        if x < 2:
            vel = vel + before_ref[vel_at + EY * x : vel_at + EY * (x + 1), :]
        if x >= EX - 2:
            at = vel_at + EY * (x - EX + 2)
            vel = vel + after_ref[at : at + EY, :]
        slot, group = (x + OFF) % PACK, (x + OFF) // PACK
        inverse = inverse_ref[slot, OFF : OFF + EY, :]
        vel = three(lane, ZROWS, *(shift_lanes(vel, (ZROWS - SZ) * ch - OFF) for ch in range(3)))
        inverse = three(lane, ZROWS, *(shift_lanes(inverse, ZROWS * ch - SZ * group - OFF) for ch in range(3)))
        fv_ref[EY * x : EY * (x + 1), :] = vel * inverse
        fd_ref[EY * x : EY * (x + 1), :] = shift_lanes(source[slot], -SZ * group - OFF)[OFF : OFF + EY, :]
    nodes = jnp.concatenate([fv_ref[...].T[0 : 3 * ZROWS], fd_ref[...].T[0:ZROWS]], axis=0)
    for corner in range(4):
        shift = (corner >> 1) * EY + (corner & 1)
        value = nodes if shift == 0 else pltpu.roll(nodes, 256 - shift, 1)
        high = value.astype(BF16)
        low = (value - high.astype(F32)).astype(BF16)
        start = 8 * ZROWS * corner
        nodes_ref[start : start + 4 * ZROWS, :] = high
        nodes_ref[start + 4 * ZROWS : start + 8 * ZROWS, :] = low
    for index in range(TAIL // CHUNK):
        gather_update((COUNT - TAIL) // CHUNK + index, nodes_ref, part_ref, base_ref, w_ref, g_ref, rows_ref, index, True)
    for at in range(len(SENT)):
        first = MOST * MOST * (at // MOST) + at % MOST
        tail_ref[MOST * at : MOST * (at + 1), :] = rows_ref[pl.ds(first, MOST, stride=MOST), :]
    move.wait()


def head_kernel(
    counts_ref, prior_ref, nodes_ref, tail_ref, part_ref, base_ref, w_ref, g_ref, out_hbm, head_ref, left_ref, zero_ref, sems
):
    prior = prior_ref[0, 3 * SZ].astype(jnp.int32)
    left = MOST - counts_ref[0]
    zero_ref[...] = jnp.zeros_like(zero_ref)
    blanks = []
    for i in range(MOST):
        to = pl.ds(pl.multiple_of((NBIN + MOST - 1 - i) * BIN, BIN), BIN)
        blanks.append((i < MOST - prior, pltpu.make_async_copy(zero_ref, out_hbm.at[:, to], sems.at[2 + i])))
    for wanted, move in blanks:
        pl.when(wanted)(move.start)
    unpack(tail_ref, left_ref, left)
    to = pl.ds(pl.multiple_of((prior + NBIN - MOST) * BIN, BIN), TAIL)
    own = pltpu.make_async_copy(left_ref, out_hbm.at[:, to], sems.at[0])
    own.start()
    for index in range((COUNT - TAIL) // CHUNK):
        gather_update(index, nodes_ref, part_ref, base_ref, w_ref, g_ref, head_ref, index, False)
    to = pl.ds(pl.multiple_of(prior * BIN, BIN), COUNT - TAIL)
    stay = pltpu.make_async_copy(head_ref, out_hbm.at[:, to], sems.at[1])
    stay.start()
    for wanted, move in blanks:
        pl.when(wanted)(move.wait)
    own.wait()
    stay.wait()


def arrive_kernel(prior_ref, packed_ref, partial_hbm, out_hbm, recv_ref, sems):
    prior = prior_ref[0, 3 * SZ].astype(jnp.int32)
    unpack(packed_ref, recv_ref)
    moves = []
    for slot in range(MOST):
        source = pl.ds(pl.multiple_of(jnp.minimum(MOST - prior + slot, MOST - 1) * BIN, BIN), BIN)
        moves.append(
            (
                slot < prior,
                pltpu.make_async_copy(recv_ref.at[:, source], out_hbm.at[:, slot * BIN : (slot + 1) * BIN], sems.at[slot]),
            )
        )
    for wanted, move in moves:
        pl.when(wanted)(move.start)
    for wanted, move in moves:
        pl.when(wanted)(move.wait)


def shape(*dims, kind=F32):
    return jax.ShapeDtypeStruct(dims, kind)


SMEM = pltpu.SMEM
HBM = pltpu.HBM


def call(kernel, out_shape, spaces, args, out_spaces=None, scratch=(), flops=0, aliases=None, limit=None):
    leaves = jax.tree.leaves(out_shape)
    out_spaces = out_spaces or [VMEM] * len(leaves)
    out_specs = [pl.BlockSpec(memory_space=s) for s in out_spaces]
    return pl.pallas_call(
        kernel,
        out_shape=out_shape,
        in_specs=[pl.BlockSpec(memory_space=s) for s in spaces],
        out_specs=tuple(out_specs) if isinstance(out_shape, tuple) else out_specs[0],
        scratch_shapes=list(scratch),
        input_output_aliases=aliases or {},
        compiler_params=pltpu.CompilerParams(vmem_limit_bytes=(limit or 48 * 1024) * 1024),
        cost_estimate=pl.CostEstimate(flops=flops, bytes_accessed=2000000, transcendentals=0),
    )(*args)


def exchange(low, high, axis):
    down = [(i + 1, i) for i in range(lax.axis_size(axis) - 1)]
    after = lax.ppermute(low, axis, down)
    return lax.ppermute(high, axis, [(j, i) for i, j in down]), after


def per_device(particles, stencil_base, weights, gradients, counts):
    sizes = tuple(lax.axis_size(a) for a in AXES)
    ring = [(i, (i + 1) % sizes[2]) for i in range(sizes[2])]
    inputs = (particles, stencil_base, weights, gradients)
    deep, vel, odd, even = call(
        scatter_kernel,
        (VMEM((GROWS, 128), F32), VMEM((GROWS, 128), F32), VMEM((GROUP, 128), F32), VMEM((GROUP, 128), F32)),
        [SMEM] + [HBM] * 4,
        (counts,) + inputs,
        scratch=[
            VMEM((FIELDS, COUNT), F32),
            VMEM((3, COUNT), jnp.int32),
            VMEM((8, COUNT), F32),
            VMEM((3, 8, COUNT), F32),
            VMEM((4, 2 * HALF, 256), F32),
            VMEM((256, 256), F32),
            VMEM((2, 6, 8, COUNT), F32),
            VMEM((8 * HALF, 2 * COUNT), BF16),
            VMEM((AROWS, COUNT), BF16),
            pltpu.SemaphoreType.DMA((4,)),
        ],
        limit=SCATTER_KIB,
    )
    count_z = sizes[2]
    odd_pairs = [(i, i + 1) for i in range(1, count_z - 1, 2)]
    even_pairs = [(i, i + 1) for i in range(0, count_z, 2)]
    from_odd = lax.ppermute(odd, "gz", odd_pairs + [(j, i) for i, j in odd_pairs] + [(count_z - 1, 0)])
    from_even = lax.ppermute(even, "gz", even_pairs + [(j, i) for i, j in even_pairs])
    message = LAYERS * EX + 2 * EX
    pairs = sizes[1] - 1
    deep, vel, prior, *messages = call(
        lambda *refs: join_z_kernel(pairs, *refs),
        (shape(GROWS, 128), shape(GROWS, 128), shape(8, 128)) + (shape(message, 128),) * pairs,
        [VMEM] * 4,
        (deep, vel, from_odd, from_even),
    )
    received = [lax.ppermute(messages[i], "gy", [(i, i + 1), (i + 1, i)]) for i in range(pairs)]
    wide_message = LAYERS * SY + 2 * EY
    deep, vel, low, high = call(
        lambda *refs: join_y_kernel(pairs, *refs),
        (shape(EX, PITCH, 128), shape(EX, PITCH, 128), shape(wide_message, 128), shape(wide_message, 128)),
        [VMEM] * (2 + pairs),
        (deep, vel, *received),
        scratch=[VMEM((message, 128), F32)] * 2,
    )
    before, after = exchange(low, high, "gx")

    def relax(*refs):
        relax_kernel(sizes, *refs)

    damage, nodes, tail = call(
        relax,
        (shape(CX, CY, CZ), shape(32 * ZROWS, 256, kind=BF16), shape(len(SENT) * MOST, BIN)),
        [VMEM] * 8,
        (deep, vel, after, before) + inputs,
        out_spaces=[HBM, VMEM, VMEM],
        scratch=[VMEM((SX, PITCH, 128), F32)]
        + [VMEM((PACK, PITCH, 128), F32)] * 6
        + [VMEM((256, 128), F32)] * 2
        + [VMEM((CX, CY, CZ), F32), VMEM((3 * MOST * MOST, BIN), F32), pltpu.SemaphoreType.DMA],
    )
    recv = lax.ppermute(tail, "gz", ring)
    own = call(
        head_kernel,
        shape(FIELDS, SLOTS),
        [SMEM] + [VMEM] * 7,
        (counts, prior, nodes, tail) + inputs,
        out_spaces=[HBM],
        scratch=[
            VMEM((FIELDS, COUNT - TAIL), F32),
            VMEM((FIELDS, TAIL), F32),
            VMEM((FIELDS, BIN), F32),
            pltpu.SemaphoreType.DMA((2 + MOST,)),
        ],
        flops=2 * 1280 * 256 * 1024,
    )
    migrated = call(
        arrive_kernel,
        shape(FIELDS, SLOTS),
        [VMEM, VMEM, HBM],
        (prior, recv, own),
        out_spaces=[HBM],
        scratch=[VMEM((FIELDS, TAIL), F32), pltpu.SemaphoreType.DMA((MOST,))],
        aliases={2: 0},
    )
    return (migrated, damage)


def solution(mesh):
    return jax.shard_map(
        per_device,
        mesh=mesh,
        in_specs=(
            P(None, ("gx", "gy", "gz")),
            P(None, ("gx", "gy", "gz")),
            P(None, ("gx", "gy", "gz")),
            P(None, None, ("gx", "gy", "gz")),
            P(("gx", "gy", "gz")),
        ),
        out_specs=(P(None, ("gx", "gy", "gz")), P("gx", "gy", "gz")),
        check_vma=False,
    )
```

```python
import jax
import jax.numpy as jnp
from jax import lax
from jax.experimental import pallas as pl
from jax.experimental.pallas import tpu as pltpu
from jax.sharding import PartitionSpec as P

CX = 8
CY = 16
CZ = 32
NBIN = 16
BIN = 128
SUBSTEPS = 4
FIELDS = 28
MOST = 8
COUNT = NBIN * BIN
TAIL = MOST * BIN
SLOTS = (NBIN + MOST) * BIN

time_step = 0.1
relax_rate = 0.2
length_sq = 0.6
shear_mod = 1.0
bulk_coef = 1.5
mass_floor = 0.5

EX = CX + 2
EY = CY + 2
EZ = CZ + 2
WIDE = SUBSTEPS + 1
LAYERS = WIDE + 1
SX = CX + 2 * WIDE
SY = CY + 2 * WIDE
SZ = CZ + 2 * WIDE
OFF = WIDE - 1
PITCH = 32
AROWS = 176
GROWS = 200
GROUP = 40
HALF = 104
PACK = SX // 3
ZROWS = 40
CHUNK = 256
FAR = 4
SENT = tuple(range(14)) + tuple(range(23, FIELDS))
AXES = ("gx", "gy", "gz")
F32 = jnp.float32
BF16 = jnp.bfloat16
SCATTER_KIB = 56000
VMEM = pltpu.VMEM


def shift_lanes(value, by):
    by = by % 128
    return value if by == 0 else pltpu.roll(value, by, 1)


def channel_lane(lane):
    return jnp.where(
        lane < SZ, lane, jnp.where(lane < 2 * SZ, lane - SZ, jnp.where(lane < 3 * SZ, lane - 2 * SZ, 1000))
    )


def three(lane, width, a, b, c):
    return jnp.where(lane < width, a, jnp.where(lane < 2 * width, b, c))


def lane_index(rows):
    return lax.broadcasted_iota(jnp.int32, (rows, 128), 1)


def onehot_rows(base_ref, lanes):
    xy = base_ref[0:1, lanes] * EY + base_ref[1:2, lanes]
    rows = lax.broadcasted_iota(jnp.int32, (AROWS, CHUNK), 0)
    return jnp.where(rows == xy, 1.0, 0.0).astype(BF16)


def scatter_kernel(
    counts_ref,
    part_hbm,
    base_hbm,
    w_hbm,
    g_hbm,
    deep_ref,
    vel_ref,
    odd_ref,
    even_ref,
    part_ref,
    base_ref,
    w_ref,
    g_ref,
    acc_ref,
    wide_ref,
    term_ref,
    rows_ref,
    onehot_ref,
    sems,
):
    moves = [
        pltpu.make_async_copy(source, target, sems.at[i])
        for i, (source, target) in enumerate(
            ((base_hbm, base_ref), (part_hbm, part_ref), (w_hbm, w_ref), (g_hbm, g_ref))
        )
    ]
    for move in moves:
        move.start()
    acc_ref[...] = jnp.zeros_like(acc_ref)
    wide_ref[...] = jnp.zeros_like(wide_ref)
    moves[0].wait()
    for index in range(COUNT // CHUNK):
        lanes = slice(index * CHUNK, (index + 1) * CHUNK)
        onehot_ref[:, lanes] = onehot_rows(base_ref, lanes)
    for move in moves[1:]:
        move.wait()
    for index in range(COUNT // CHUNK):
        lanes = slice(index * CHUNK, (index + 1) * CHUNK)
        minus_vol = -time_step * part_ref[1:2, lanes]
        share = part_ref[0:1, lanes] * w_ref[:, lanes]
        slope = [g_ref[j, :, lanes] for j in range(3)]
        terms = [share, share * part_ref[23:24, lanes], share * part_ref[24:25, lanes]]
        for i in range(3):
            row = 14 + 3 * i
            pull = (
                part_ref[row : row + 1, lanes] * slope[0]
                + part_ref[row + 1 : row + 2, lanes] * slope[1]
                + part_ref[row + 2 : row + 3, lanes] * slope[2]
            )
            terms.append(share * part_ref[2 + i : 3 + i, lanes] + minus_vol * pull)
        for ch, term in enumerate(terms):
            high = term.astype(BF16).astype(F32)
            term_ref[0, ch, :, lanes] = high
            term_ref[1, ch, :, lanes] = term - high
    nt = (((1,), (1,)), ((), ()))
    for corner in range(4):
        k = 2 * corner
        for index in range(COUNT // CHUNK):
            lanes = slice(index * CHUNK, (index + 1) * CHUNK)
            sub = lax.broadcasted_iota(jnp.int32, (8, CHUNK), 0) - base_ref[2:3, lanes]
            for part in range(2):
                tiles = {}
                for tile in range(HALF // 8):
                    first = [(ch, EZ * ch - 8 * tile) for ch in range(3) if EZ * ch < 8 * tile + 8 and EZ * (ch + 1) > 8 * tile]
                    for half in range(2):
                        value = jnp.zeros((8, CHUNK), F32)
                        for ch, at in first:
                            value = jnp.where(sub == at, term_ref[part, 3 * half + ch, k : k + 1, lanes], value)
                            value = jnp.where(sub == at + 1, term_ref[part, 3 * half + ch, k + 1 : k + 2, lanes], value)
                        tiles[half * (HALF // 8) + tile] = value
                to = slice(part * COUNT + index * CHUNK, part * COUNT + (index + 1) * CHUNK)
                for pair in range(HALF // 8):
                    row = 2 * HALF * corner + 16 * pair
                    rows_ref[row : row + 16, to] = jnp.concatenate([tiles[2 * pair], tiles[2 * pair + 1]], axis=0).astype(BF16)
        rows = slice(2 * HALF * corner, 2 * HALF * (corner + 1))
        piece = lax.dot_general(rows_ref[rows, 0:COUNT], onehot_ref[...], nt, preferred_element_type=F32)
        piece = piece + lax.dot_general(rows_ref[rows, COUNT:], onehot_ref[...], nt, preferred_element_type=F32)
        acc_ref[corner, :, 0:AROWS] = piece
    total = acc_ref[0]
    for corner in range(1, 4):
        total = total + pltpu.roll(acc_ref[corner], (corner >> 1) * EY + (corner & 1), 1)
    for half in range(2):
        for ch in range(3):
            row = half * HALF + EZ * ch
            to = half * 128 + SZ * ch + OFF
            wide_ref[to : to + EZ, :] = total[row : row + EZ]
    deep_ref[...] = wide_ref[0:128, :].T[0:GROWS]
    vel_ref[...] = wide_ref[128:256, :].T[0:GROWS]
    lane = lane_index(GROUP)
    place = channel_lane(lane)
    low_msg = jnp.zeros((GROUP, 128), F32)
    high_msg = jnp.zeros((GROUP, 128), F32)
    for j in range(5):
        rows = slice(GROUP * j, GROUP * (j + 1))
        deep = deep_ref[rows, :]
        vel = vel_ref[rows, :]
        inside = (place >= 8 * j) & (place < 8 * j + LAYERS)
        low_msg = jnp.where(inside, shift_lanes(deep, 8 * j - OFF), low_msg)
        high_msg = jnp.where(inside, shift_lanes(deep, 8 * j - CZ), high_msg)
        inside = (place >= 8 * j + LAYERS) & (place < 8 * j + LAYERS + 2)
        low_msg = jnp.where(inside, shift_lanes(vel, 8 * j + LAYERS - OFF), low_msg)
        high_msg = jnp.where(inside, shift_lanes(vel, 8 * j + LAYERS - OFF - CZ), high_msg)
    high_msg = jnp.where(lane >= 3 * SZ, counts_ref[0].astype(F32), high_msg)
    is_even = lax.rem(lax.axis_index(AXES[2]), 2) == 0
    odd_ref[...] = jnp.where(is_even, low_msg, high_msg)
    even_ref[...] = jnp.where(is_even, high_msg, low_msg)


def join_z_kernel(pairs, deep_ref, vel_ref, odd_ref, even_ref, deep_out, vel_out, prior_ref, *messages):
    place = channel_lane(lane_index(GROUP))
    is_even = lax.rem(lax.axis_index(AXES[2]), 2) == 0
    before = jnp.where(is_even, odd_ref[...], even_ref[...])
    after = jnp.where(is_even, even_ref[...], odd_ref[...])
    prior_ref[...] = before[0:8]
    before = jnp.where(lax.axis_index(AXES[2]) > 0, before, 0.0)
    deep_low, deep_high = place < LAYERS, (place >= SZ - LAYERS) & (place < SZ)
    vel_low = (place >= OFF) & (place < OFF + 2)
    vel_high = (place >= OFF + CZ) & (place < OFF + CZ + 2)
    for j in range(5):
        rows = slice(GROUP * j, GROUP * (j + 1))
        deep = jnp.where(
            deep_low,
            shift_lanes(before, -8 * j),
            jnp.where(deep_high, shift_lanes(after, SZ - LAYERS - 8 * j), 0.0),
        )
        vel = jnp.where(
            vel_low,
            shift_lanes(before, OFF - 8 * j - LAYERS),
            jnp.where(vel_high, shift_lanes(after, OFF + CZ - 8 * j - LAYERS), 0.0),
        )
        deep_out[rows, :] = deep_ref[rows, :] + deep
        vel_out[rows, :] = vel_ref[rows, :] + vel
    for i in range(pairs):
        is_lower = lax.axis_index(AXES[1]) == i
        for x in range(EX):
            row = EY * x
            messages[i][LAYERS * x : LAYERS * (x + 1), :] = jnp.where(
                is_lower, deep_out[row + EY - LAYERS : row + EY, :], deep_out[row : row + LAYERS, :]
            )
            at = LAYERS * EX + 2 * x
            messages[i][at : at + 2, :] = jnp.where(
                is_lower, vel_out[row + EY - 2 : row + EY, :], vel_out[row : row + 2, :]
            )


def join_y_kernel(pairs, deep_ref, vel_ref, *refs):
    received, (deep_out, vel_out, low_ref, high_ref, before_ref, after_ref) = refs[:pairs], refs[pairs:]
    before = jnp.zeros_like(before_ref)
    after = jnp.zeros_like(after_ref)
    for i in range(pairs):
        before = jnp.where(lax.axis_index(AXES[1]) == i + 1, received[i][...], before)
        after = jnp.where(lax.axis_index(AXES[1]) == i, received[i][...], after)
    before_ref[...] = before
    after_ref[...] = after
    deep_out[...] = jnp.zeros_like(deep_out)
    vel_out[...] = jnp.zeros_like(vel_out)
    for x in range(EX):
        row = EY * x
        deep_out[x, OFF : OFF + EY, :] = deep_ref[row : row + EY, :]
        deep_out[x, 0:LAYERS, :] += before_ref[LAYERS * x : LAYERS * (x + 1), :]
        deep_out[x, OFF + CY : OFF + CY + LAYERS, :] += after_ref[LAYERS * x : LAYERS * (x + 1), :]
        at = LAYERS * EX + 2 * x
        vel_out[x, OFF : OFF + EY, :] = vel_ref[row : row + EY, :]
        vel_out[x, OFF : OFF + 2, :] += before_ref[at : at + 2, :]
        vel_out[x, OFF + CY : OFF + CY + 2, :] += after_ref[at : at + 2, :]
    for x in range(LAYERS):
        low_ref[SY * x : SY * (x + 1), :] = deep_out[x, 0:SY, :]
        high_ref[SY * x : SY * (x + 1), :] = deep_out[EX - LAYERS + x, 0:SY, :]
    for x in range(2):
        at = SY * LAYERS + EY * x
        low_ref[at : at + EY, :] = vel_out[x, OFF : OFF + EY, :]
        high_ref[at : at + EY, :] = vel_out[EX - 2 + x, OFF : OFF + EY, :]


def determinant(m):
    return (
        m[0][0] * (m[1][1] * m[2][2] - m[1][2] * m[2][1])
        - m[0][1] * (m[1][0] * m[2][2] - m[1][2] * m[2][0])
        + m[0][2] * (m[1][0] * m[2][1] - m[1][1] * m[2][0])
    )


def left_product(m, i, j):
    return m[i][0] * m[j][0] + m[i][1] * m[j][1] + m[i][2] * m[j][2]


def stress_rows(mapped, damaged):
    degrade = (1.0 - damaged) ** 2
    pressure = bulk_coef * (determinant(mapped) - 1.0)
    rows = {}
    for i in range(3):
        for j in range(i, 3):
            term = shear_mod * (left_product(mapped, i, j) - (1.0 if i == j else 0.0))
            if i == j:
                term = term + pressure
            rows[14 + 3 * i + j] = rows[14 + 3 * j + i] = degrade * term
    return rows


def unpack(packed_ref, out_ref, left=None):
    rows = {f: packed_ref[MOST * at : MOST * (at + 1), :] for at, f in enumerate(SENT)}
    rows.update(stress_rows([[rows[5 + 3 * i + j] for j in range(3)] for i in range(3)], rows[23]))
    for f in range(FIELDS):
        value = rows[f]
        if left is not None:
            value = jnp.where(lax.broadcasted_iota(jnp.int32, (MOST, BIN), 0) < left, value, 0.0)
        for t in range(MOST):
            out_ref[f : f + 1, t * BIN : (t + 1) * BIN] = value[t : t + 1]


def gather_update(index, nodes_ref, part_ref, base_ref, w_ref, g_ref, out_ref, out_index, packed):
    lanes = slice(index * CHUNK, (index + 1) * CHUNK)
    to = slice(out_index * CHUNK, (out_index + 1) * CHUNK)
    onehot = onehot_rows(base_ref, lanes)
    base_z = base_ref[2:3, lanes]
    rows = lax.broadcasted_iota(jnp.int32, (ZROWS, CHUNK), 0) - base_z
    at = rows == 0
    after = rows == 1

    def pick(mask, value):
        kept = jnp.where(mask, value, 0.0)
        total = kept[0:8]
        for t in range(1, ZROWS // 8):
            total = total + kept[8 * t : 8 * t + 8]
        return total

    moved = [jnp.zeros((8, CHUNK), F32) for _ in range(3)]
    velgrad = [[jnp.zeros((8, CHUNK), F32) for _ in range(3)] for _ in range(3)]
    damage_node = jnp.zeros((8, CHUNK), F32)
    rows_ab = 4 * ZROWS
    for corner in range(4):
        start = 2 * rows_ab * corner
        near = jnp.dot(nodes_ref[start : start + rows_ab, 0:AROWS], onehot, preferred_element_type=F32) + jnp.dot(
            nodes_ref[start + rows_ab : start + 2 * rows_ab, 0:AROWS], onehot, preferred_element_type=F32
        )
        for c, mask in enumerate((at, after)):
            k = 2 * corner + c
            weight = w_ref[k : k + 1, lanes]
            slope = [g_ref[j, k : k + 1, lanes] for j in range(3)]
            for i in range(3):
                value = pick(mask, near[ZROWS * i : ZROWS * (i + 1)])
                moved[i] = moved[i] + value * weight
                for j in range(3):
                    velgrad[i][j] = velgrad[i][j] + value * slope[j]
            damage_node = damage_node + pick(mask, near[3 * ZROWS : 4 * ZROWS]) * weight
    moved = [jnp.sum(v, axis=0, keepdims=True) for v in moved]
    velgrad = [[jnp.sum(v, axis=0, keepdims=True) for v in row] for row in velgrad]
    damage_node = jnp.sum(damage_node, axis=0, keepdims=True)

    def field(i):
        return part_ref[i : i + 1, lanes]

    deform = [[field(5 + 3 * i + j) for j in range(3)] for i in range(3)]
    stretch = [[(1.0 if i == j else 0.0) + time_step * velgrad[i][j] for j in range(3)] for i in range(3)]
    mapped = [
        [
            stretch[i][0] * deform[0][j] + stretch[i][1] * deform[1][j] + stretch[i][2] * deform[2][j]
            for j in range(3)
        ]
        for i in range(3)
    ]
    damaged = jnp.maximum(field(23), damage_node)
    jacobian = determinant(mapped)
    trace = left_product(mapped, 0, 0) + left_product(mapped, 1, 1) + left_product(mapped, 2, 2)
    energy = 0.5 * shear_mod * (trace - 3.0) + 0.5 * bulk_coef * (jacobian - 1.0) ** 2
    rows = {f: field(f) for f in range(2)}
    for i in range(3):
        rows[2 + i] = moved[i]
        rows[25 + i] = field(25 + i) + time_step * moved[i]
        for j in range(3):
            rows[5 + 3 * i + j] = mapped[i][j]
    rows[23] = damaged
    rows[24] = jnp.maximum(field(24), energy)
    if packed:
        for at, f in enumerate(SENT):
            for t in range(CHUNK // BIN):
                row = MOST * (MOST * (at // MOST) + out_index * (CHUNK // BIN) + t) + at % MOST
                out_ref[row : row + 1, :] = rows[f][:, t * BIN : (t + 1) * BIN]
    else:
        rows.update(stress_rows(mapped, damaged))
        for f in range(FIELDS):
            out_ref[f : f + 1, to] = rows[f]


def relax_kernel(turn, axis_sizes, *refs):
    tail_before = refs[10]
    refs = refs if turn == 0 else refs[:8] + refs[11:]
    is_far = lax.rem(lax.axis_index(AXES[2]), FAR) == 0

    @pl.when(is_far if turn else jnp.logical_not(is_far))
    def _():
        relax_body(axis_sizes, *refs)

    if turn:

        @pl.when(jnp.logical_not(is_far))
        def _():
            refs[10][...] = tail_before[...]


def relax_body(
    axis_sizes,
    deep_ref,
    vel_ref,
    after_ref,
    before_ref,
    part_ref,
    base_ref,
    w_ref,
    g_ref,
    damage_hbm,
    nodes_ref,
    tail_ref,
    sums_ref,
    one_ref,
    two_ref,
    keep_ref,
    add_ref,
    spread_ref,
    inverse_ref,
    fv_ref,
    fd_ref,
    damage_ref,
    rows_ref,
    sem,
):
    count_x, count_y, count_z = axis_sizes
    sums_ref[...] = jnp.zeros_like(sums_ref)
    for xd in range(SX):
        if OFF <= xd < OFF + EX:
            sums_ref[xd] = deep_ref[xd - OFF]
        if xd < LAYERS:
            sums_ref[xd, 0:SY, :] += before_ref[SY * xd : SY * (xd + 1), :]
        if xd >= SX - LAYERS:
            at = SY * (xd - SX + LAYERS)
            sums_ref[xd, 0:SY, :] += after_ref[at : at + SY, :]
    lane = lane_index(PITCH)
    pos_x = lax.axis_index(AXES[0]) * CX - WIDE + three(lane, SZ, 0, PACK, 2 * PACK)
    pos_y = lax.axis_index(AXES[1]) * CY - WIDE + lax.broadcasted_iota(jnp.int32, (PITCH, 128), 0)
    pos_z = lax.axis_index(AXES[2]) * CZ - WIDE + lane - three(lane, SZ, 0, SZ, 2 * SZ)
    inside_yz = (
        (lane < 3 * SZ) & (pos_y >= 0) & (pos_y < count_y * CY) & (pos_z >= 0) & (pos_z < count_z * CZ)
    )
    for j in range(PACK):
        first, second, third = sums_ref[j], sums_ref[j + PACK], sums_ref[j + 2 * PACK]
        mass = three(lane, SZ, first, shift_lanes(second, SZ), shift_lanes(third, 2 * SZ))
        damage = three(lane, SZ, shift_lanes(first, -SZ), second, shift_lanes(third, SZ))
        drive = three(lane, SZ, shift_lanes(first, -2 * SZ), shift_lanes(second, -SZ), third)
        mask = (inside_yz & (pos_x + j >= 0) & (pos_x + j < count_x * CX)).astype(F32)
        inverse = mask / jnp.maximum(mass, mass_floor)
        drive = (2.0 * relax_rate) * (drive * inverse)
        keep_ref[j] = (1.0 - relax_rate * (1.0 + 6.0 * length_sq)) * mask - drive
        add_ref[j] = drive
        spread_ref[j] = (relax_rate * length_sq) * mask
        one_ref[j] = damage * inverse
        inverse_ref[j] = inverse
    source, target = one_ref, two_ref
    for _ in range(SUBSTEPS):
        for j in range(PACK):
            centre = source[j]
            lower = source[j - 1] if j > 0 else shift_lanes(source[PACK - 1], SZ)
            upper = source[j + 1] if j < PACK - 1 else shift_lanes(source[0], -SZ)
            around = (
                (lower + upper)
                + (pltpu.roll(centre, 1, 0) + pltpu.roll(centre, PITCH - 1, 0))
                + (shift_lanes(centre, 1) + shift_lanes(centre, -1))
            )
            target[j] = (centre * keep_ref[j] + add_ref[j]) + spread_ref[j] * around
        source, target = target, source
    for x in range(CX):
        xd = x + WIDE
        value = shift_lanes(source[xd % PACK], -SZ * (xd // PACK) - WIDE)
        damage_ref[x] = value[WIDE : WIDE + CY, 0:CZ]
    move = pltpu.make_async_copy(damage_ref, damage_hbm, sem)
    move.start()
    fv_ref[...] = jnp.zeros_like(fv_ref)
    fd_ref[...] = jnp.zeros_like(fd_ref)
    vel_at = SY * LAYERS
    lane = lane_index(EY)
    for x in range(EX):
        vel = vel_ref[x, OFF : OFF + EY, :]
        if x < 2:
            vel = vel + before_ref[vel_at + EY * x : vel_at + EY * (x + 1), :]
        if x >= EX - 2:
            at = vel_at + EY * (x - EX + 2)
            vel = vel + after_ref[at : at + EY, :]
        slot, group = (x + OFF) % PACK, (x + OFF) // PACK
        inverse = inverse_ref[slot, OFF : OFF + EY, :]
        vel = three(lane, ZROWS, *(shift_lanes(vel, (ZROWS - SZ) * ch - OFF) for ch in range(3)))
        inverse = three(lane, ZROWS, *(shift_lanes(inverse, ZROWS * ch - SZ * group - OFF) for ch in range(3)))
        fv_ref[EY * x : EY * (x + 1), :] = vel * inverse
        fd_ref[EY * x : EY * (x + 1), :] = shift_lanes(source[slot], -SZ * group - OFF)[OFF : OFF + EY, :]
    nodes = jnp.concatenate([fv_ref[...].T[0 : 3 * ZROWS], fd_ref[...].T[0:ZROWS]], axis=0)
    for corner in range(4):
        shift = (corner >> 1) * EY + (corner & 1)
        value = nodes if shift == 0 else pltpu.roll(nodes, 256 - shift, 1)
        high = value.astype(BF16)
        low = (value - high.astype(F32)).astype(BF16)
        start = 8 * ZROWS * corner
        nodes_ref[start : start + 4 * ZROWS, :] = high
        nodes_ref[start + 4 * ZROWS : start + 8 * ZROWS, :] = low
    for index in range(TAIL // CHUNK):
        gather_update((COUNT - TAIL) // CHUNK + index, nodes_ref, part_ref, base_ref, w_ref, g_ref, rows_ref, index, True)
    for at in range(len(SENT)):
        first = MOST * MOST * (at // MOST) + at % MOST
        tail_ref[MOST * at : MOST * (at + 1), :] = rows_ref[pl.ds(first, MOST, stride=MOST), :]
    move.wait()


def head_kernel(
    counts_ref, prior_ref, nodes_ref, tail_ref, part_ref, base_ref, w_ref, g_ref, out_hbm, head_ref, left_ref, zero_ref, sems
):
    prior = prior_ref[0, 3 * SZ].astype(jnp.int32)
    left = MOST - counts_ref[0]
    zero_ref[...] = jnp.zeros_like(zero_ref)
    blanks = []
    for i in range(MOST):
        to = pl.ds(pl.multiple_of((NBIN + MOST - 1 - i) * BIN, BIN), BIN)
        blanks.append((i < MOST - prior, pltpu.make_async_copy(zero_ref, out_hbm.at[:, to], sems.at[2 + i])))
    for wanted, move in blanks:
        pl.when(wanted)(move.start)
    unpack(tail_ref, left_ref, left)
    to = pl.ds(pl.multiple_of((prior + NBIN - MOST) * BIN, BIN), TAIL)
    own = pltpu.make_async_copy(left_ref, out_hbm.at[:, to], sems.at[0])
    own.start()
    for index in range((COUNT - TAIL) // CHUNK):
        gather_update(index, nodes_ref, part_ref, base_ref, w_ref, g_ref, head_ref, index, False)
    to = pl.ds(pl.multiple_of(prior * BIN, BIN), COUNT - TAIL)
    stay = pltpu.make_async_copy(head_ref, out_hbm.at[:, to], sems.at[1])
    stay.start()
    for wanted, move in blanks:
        pl.when(wanted)(move.wait)
    own.wait()
    stay.wait()


def arrive_kernel(turn, prior_ref, packed_ref, partial_hbm, out_hbm, recv_ref, sems):
    is_far = lax.rem(lax.axis_index(AXES[2]), FAR) == 0

    @pl.when(jnp.logical_not(is_far) if turn else is_far)
    def _():
        prior = prior_ref[0, 3 * SZ].astype(jnp.int32)
        unpack(packed_ref, recv_ref)
        moves = []
        for slot in range(MOST):
            source = pl.ds(pl.multiple_of(jnp.minimum(MOST - prior + slot, MOST - 1) * BIN, BIN), BIN)
            target = out_hbm.at[:, slot * BIN : (slot + 1) * BIN]
            moves.append((slot < prior, pltpu.make_async_copy(recv_ref.at[:, source], target, sems.at[slot])))
        for wanted, move in moves:
            pl.when(wanted)(move.start)
        for wanted, move in moves:
            pl.when(wanted)(move.wait)


def shape(*dims, kind=F32):
    return jax.ShapeDtypeStruct(dims, kind)


SMEM = pltpu.SMEM
HBM = pltpu.HBM


def call(kernel, out_shape, spaces, args, out_spaces=None, scratch=(), flops=0, aliases=None, limit=None):
    leaves = jax.tree.leaves(out_shape)
    out_spaces = out_spaces or [VMEM] * len(leaves)
    out_specs = [pl.BlockSpec(memory_space=s) for s in out_spaces]
    return pl.pallas_call(
        kernel,
        out_shape=out_shape,
        in_specs=[pl.BlockSpec(memory_space=s) for s in spaces],
        out_specs=tuple(out_specs) if isinstance(out_shape, tuple) else out_specs[0],
        scratch_shapes=list(scratch),
        input_output_aliases=aliases or {},
        compiler_params=pltpu.CompilerParams(vmem_limit_bytes=(limit or 48 * 1024) * 1024),
        cost_estimate=pl.CostEstimate(flops=flops, bytes_accessed=2000000, transcendentals=0),
    )(*args)


def exchange(low, high, axis):
    down = [(i + 1, i) for i in range(lax.axis_size(axis) - 1)]
    after = lax.ppermute(low, axis, down)
    return lax.ppermute(high, axis, [(j, i) for i, j in down]), after


def per_device(particles, stencil_base, weights, gradients, counts):
    sizes = tuple(lax.axis_size(a) for a in AXES)
    inputs = (particles, stencil_base, weights, gradients)
    deep, vel, odd, even = call(
        scatter_kernel,
        (VMEM((GROWS, 128), F32), VMEM((GROWS, 128), F32), VMEM((GROUP, 128), F32), VMEM((GROUP, 128), F32)),
        [SMEM] + [HBM] * 4,
        (counts,) + inputs,
        scratch=[
            VMEM((FIELDS, COUNT), F32),
            VMEM((3, COUNT), jnp.int32),
            VMEM((8, COUNT), F32),
            VMEM((3, 8, COUNT), F32),
            VMEM((4, 2 * HALF, 256), F32),
            VMEM((256, 256), F32),
            VMEM((2, 6, 8, COUNT), F32),
            VMEM((8 * HALF, 2 * COUNT), BF16),
            VMEM((AROWS, COUNT), BF16),
            pltpu.SemaphoreType.DMA((4,)),
        ],
        limit=SCATTER_KIB,
    )
    count_z = sizes[2]
    odd_pairs = [(i, i + 1) for i in range(1, count_z - 1, 2)]
    even_pairs = [(i, i + 1) for i in range(0, count_z, 2)]
    from_odd = lax.ppermute(odd, "gz", odd_pairs + [(j, i) for i, j in odd_pairs] + [(count_z - 1, 0)])
    from_even = lax.ppermute(even, "gz", even_pairs + [(j, i) for i, j in even_pairs])
    message = LAYERS * EX + 2 * EX
    pairs = sizes[1] - 1
    deep, vel, prior, *messages = call(
        lambda *refs: join_z_kernel(pairs, *refs),
        (shape(GROWS, 128), shape(GROWS, 128), shape(8, 128)) + (shape(message, 128),) * pairs,
        [VMEM] * 4,
        (deep, vel, from_odd, from_even),
    )
    received = [lax.ppermute(messages[i], "gy", [(i, i + 1), (i + 1, i)]) for i in range(pairs)]
    wide_message = LAYERS * SY + 2 * EY
    deep, vel, low, high = call(
        lambda *refs: join_y_kernel(pairs, *refs),
        (shape(EX, PITCH, 128), shape(EX, PITCH, 128), shape(wide_message, 128), shape(wide_message, 128)),
        [VMEM] * (2 + pairs),
        (deep, vel, *received),
        scratch=[VMEM((message, 128), F32)] * 2,
    )
    before, after = exchange(low, high, "gx")

    ring = [(i, (i + 1) % count_z) for i in range(count_z)]
    far = [edge for edge in ring if edge[1] % FAR == 0]
    near = [edge for edge in ring if edge[1] % FAR != 0]
    results = ()
    for turn in range(2):
        results = call(
            lambda *refs, turn=turn: relax_kernel(turn, sizes, *refs),
            (shape(CX, CY, CZ), VMEM((32 * ZROWS, 256), BF16), VMEM((len(SENT) * MOST, BIN), F32)),
            [VMEM] * 8 + [HBM, VMEM, VMEM][: len(results)],
            (deep, vel, after, before) + inputs + tuple(results),
            out_spaces=[HBM, VMEM, VMEM],
            scratch=[VMEM((SX, PITCH, 128), F32)]
            + [VMEM((PACK, PITCH, 128), F32)] * 6
            + [VMEM((256, 128), F32)] * 2
            + [VMEM((CX, CY, CZ), F32), VMEM((3 * MOST * MOST, BIN), F32), pltpu.SemaphoreType.DMA],
            aliases={8: 0, 9: 1} if turn else {},
        )
        if turn == 0:
            recv_far = lax.ppermute(results[2], "gz", far)
    damage, nodes, tail = results
    recv_near = lax.ppermute(tail, "gz", near)
    own = call(
        head_kernel,
        shape(FIELDS, SLOTS),
        [SMEM] + [VMEM] * 7,
        (counts, prior, nodes, tail) + inputs,
        out_spaces=[HBM],
        scratch=[
            VMEM((FIELDS, COUNT - TAIL), F32),
            VMEM((FIELDS, TAIL), F32),
            VMEM((FIELDS, BIN), F32),
            pltpu.SemaphoreType.DMA((2 + MOST,)),
        ],
        flops=2 * 1280 * 256 * 1024,
    )
    migrated = own
    for turn, recv in enumerate((recv_far, recv_near)):
        migrated = call(
            lambda *refs, turn=turn: arrive_kernel(turn, *refs),
            shape(FIELDS, SLOTS),
            [VMEM, VMEM, HBM],
            (prior, recv, migrated),
            out_spaces=[HBM],
            scratch=[VMEM((FIELDS, TAIL), F32), pltpu.SemaphoreType.DMA((MOST,))],
            aliases={2: 0},
        )
    return (migrated, damage)


def solution(mesh):
    return jax.shard_map(
        per_device,
        mesh=mesh,
        in_specs=(
            P(None, ("gx", "gy", "gz")),
            P(None, ("gx", "gy", "gz")),
            P(None, ("gx", "gy", "gz")),
            P(None, None, ("gx", "gy", "gz")),
            P(("gx", "gy", "gz")),
        ),
        out_specs=(P(None, ("gx", "gy", "gz")), P("gx", "gy", "gz")),
        check_vma=False,
    )
```

```python
import jax
import jax.numpy as jnp
from jax import lax
from jax.experimental import pallas as pl
from jax.experimental.pallas import tpu as pltpu
from jax.sharding import PartitionSpec as P

CX = 8
CY = 16
CZ = 32
NBIN = 16
BIN = 128
SUBSTEPS = 4
FIELDS = 28
MOST = 8
COUNT = NBIN * BIN
TAIL = MOST * BIN
SLOTS = (NBIN + MOST) * BIN

time_step = 0.1
relax_rate = 0.2
length_sq = 0.6
shear_mod = 1.0
bulk_coef = 1.5
mass_floor = 0.5

EX = CX + 2
EY = CY + 2
EZ = CZ + 2
WIDE = SUBSTEPS + 1
LAYERS = WIDE + 1
SX = CX + 2 * WIDE
SY = CY + 2 * WIDE
SZ = CZ + 2 * WIDE
OFF = WIDE - 1
PITCH = 32
AROWS = 176
GROWS = 200
GROUP = 40
HALF = 104
PACK = SX // 3
ZROWS = 40
CHUNK = 256
FAR = 4
SENT = tuple(range(14)) + tuple(range(23, FIELDS))
AXES = ("gx", "gy", "gz")
F32 = jnp.float32
BF16 = jnp.bfloat16
SCATTER_KIB = 56000
VMEM = pltpu.VMEM


def shift_lanes(value, by):
    by = by % 128
    return value if by == 0 else pltpu.roll(value, by, 1)


def channel_lane(lane):
    return jnp.where(
        lane < SZ, lane, jnp.where(lane < 2 * SZ, lane - SZ, jnp.where(lane < 3 * SZ, lane - 2 * SZ, 1000))
    )


def three(lane, width, a, b, c):
    return jnp.where(lane < width, a, jnp.where(lane < 2 * width, b, c))


def lane_index(rows):
    return lax.broadcasted_iota(jnp.int32, (rows, 128), 1)


def onehot_rows(base_ref, lanes):
    xy = base_ref[0:1, lanes] * EY + base_ref[1:2, lanes]
    rows = lax.broadcasted_iota(jnp.int32, (AROWS, CHUNK), 0)
    return jnp.where(rows == xy, 1.0, 0.0).astype(BF16)


def scatter_kernel(
    counts_ref,
    part_hbm,
    base_hbm,
    w_hbm,
    g_hbm,
    deep_ref,
    vel_ref,
    odd_ref,
    even_ref,
    part_ref,
    base_ref,
    w_ref,
    g_ref,
    acc_ref,
    wide_ref,
    term_ref,
    rows_ref,
    onehot_ref,
    sems,
):
    moves = [
        pltpu.make_async_copy(source, target, sems.at[i])
        for i, (source, target) in enumerate(
            ((base_hbm, base_ref), (part_hbm, part_ref), (w_hbm, w_ref), (g_hbm, g_ref))
        )
    ]
    for move in moves:
        move.start()
    acc_ref[...] = jnp.zeros_like(acc_ref)
    wide_ref[...] = jnp.zeros_like(wide_ref)
    moves[0].wait()
    for index in range(COUNT // CHUNK):
        lanes = slice(index * CHUNK, (index + 1) * CHUNK)
        onehot_ref[:, lanes] = onehot_rows(base_ref, lanes)
    for move in moves[1:]:
        move.wait()
    for index in range(COUNT // CHUNK):
        lanes = slice(index * CHUNK, (index + 1) * CHUNK)
        minus_vol = -time_step * part_ref[1:2, lanes]
        share = part_ref[0:1, lanes] * w_ref[:, lanes]
        slope = [g_ref[j, :, lanes] for j in range(3)]
        terms = [share, share * part_ref[23:24, lanes], share * part_ref[24:25, lanes]]
        for i in range(3):
            row = 14 + 3 * i
            pull = (
                part_ref[row : row + 1, lanes] * slope[0]
                + part_ref[row + 1 : row + 2, lanes] * slope[1]
                + part_ref[row + 2 : row + 3, lanes] * slope[2]
            )
            terms.append(share * part_ref[2 + i : 3 + i, lanes] + minus_vol * pull)
        for ch, term in enumerate(terms):
            high = term.astype(BF16).astype(F32)
            term_ref[0, ch, :, lanes] = high
            term_ref[1, ch, :, lanes] = term - high
    nt = (((1,), (1,)), ((), ()))
    for corner in range(4):
        k = 2 * corner
        for index in range(COUNT // CHUNK):
            lanes = slice(index * CHUNK, (index + 1) * CHUNK)
            sub = lax.broadcasted_iota(jnp.int32, (8, CHUNK), 0) - base_ref[2:3, lanes]
            for part in range(2):
                tiles = {}
                for tile in range(HALF // 8):
                    first = [(ch, EZ * ch - 8 * tile) for ch in range(3) if EZ * ch < 8 * tile + 8 and EZ * (ch + 1) > 8 * tile]
                    for half in range(2):
                        value = jnp.zeros((8, CHUNK), F32)
                        for ch, at in first:
                            value = jnp.where(sub == at, term_ref[part, 3 * half + ch, k : k + 1, lanes], value)
                            value = jnp.where(sub == at + 1, term_ref[part, 3 * half + ch, k + 1 : k + 2, lanes], value)
                        tiles[half * (HALF // 8) + tile] = value
                to = slice(part * COUNT + index * CHUNK, part * COUNT + (index + 1) * CHUNK)
                for pair in range(HALF // 8):
                    row = 2 * HALF * corner + 16 * pair
                    rows_ref[row : row + 16, to] = jnp.concatenate([tiles[2 * pair], tiles[2 * pair + 1]], axis=0).astype(BF16)
        rows = slice(2 * HALF * corner, 2 * HALF * (corner + 1))
        piece = lax.dot_general(rows_ref[rows, 0:COUNT], onehot_ref[...], nt, preferred_element_type=F32)
        piece = piece + lax.dot_general(rows_ref[rows, COUNT:], onehot_ref[...], nt, preferred_element_type=F32)
        acc_ref[corner, :, 0:AROWS] = piece
    total = acc_ref[0]
    for corner in range(1, 4):
        total = total + pltpu.roll(acc_ref[corner], (corner >> 1) * EY + (corner & 1), 1)
    for half in range(2):
        for ch in range(3):
            row = half * HALF + EZ * ch
            to = half * 128 + SZ * ch + OFF
            wide_ref[to : to + EZ, :] = total[row : row + EZ]
    deep_ref[...] = wide_ref[0:128, :].T[0:GROWS]
    vel_ref[...] = wide_ref[128:256, :].T[0:GROWS]
    lane = lane_index(GROUP)
    place = channel_lane(lane)
    low_msg = jnp.zeros((GROUP, 128), F32)
    high_msg = jnp.zeros((GROUP, 128), F32)
    for j in range(5):
        rows = slice(GROUP * j, GROUP * (j + 1))
        deep = deep_ref[rows, :]
        vel = vel_ref[rows, :]
        inside = (place >= 8 * j) & (place < 8 * j + LAYERS)
        low_msg = jnp.where(inside, shift_lanes(deep, 8 * j - OFF), low_msg)
        high_msg = jnp.where(inside, shift_lanes(deep, 8 * j - CZ), high_msg)
        inside = (place >= 8 * j + LAYERS) & (place < 8 * j + LAYERS + 2)
        low_msg = jnp.where(inside, shift_lanes(vel, 8 * j + LAYERS - OFF), low_msg)
        high_msg = jnp.where(inside, shift_lanes(vel, 8 * j + LAYERS - OFF - CZ), high_msg)
    high_msg = jnp.where(lane >= 3 * SZ, counts_ref[0].astype(F32), high_msg)
    is_even = lax.rem(lax.axis_index(AXES[2]), 2) == 0
    odd_ref[...] = jnp.where(is_even, low_msg, high_msg)
    even_ref[...] = jnp.where(is_even, high_msg, low_msg)


def join_z_kernel(pairs, deep_ref, vel_ref, odd_ref, even_ref, deep_out, vel_out, prior_ref, *messages):
    place = channel_lane(lane_index(GROUP))
    is_even = lax.rem(lax.axis_index(AXES[2]), 2) == 0
    before = jnp.where(is_even, odd_ref[...], even_ref[...])
    after = jnp.where(is_even, even_ref[...], odd_ref[...])
    prior_ref[...] = before[0:8]
    before = jnp.where(lax.axis_index(AXES[2]) > 0, before, 0.0)
    deep_low, deep_high = place < LAYERS, (place >= SZ - LAYERS) & (place < SZ)
    vel_low = (place >= OFF) & (place < OFF + 2)
    vel_high = (place >= OFF + CZ) & (place < OFF + CZ + 2)
    for j in range(5):
        rows = slice(GROUP * j, GROUP * (j + 1))
        deep = jnp.where(
            deep_low,
            shift_lanes(before, -8 * j),
            jnp.where(deep_high, shift_lanes(after, SZ - LAYERS - 8 * j), 0.0),
        )
        vel = jnp.where(
            vel_low,
            shift_lanes(before, OFF - 8 * j - LAYERS),
            jnp.where(vel_high, shift_lanes(after, OFF + CZ - 8 * j - LAYERS), 0.0),
        )
        deep_out[rows, :] = deep_ref[rows, :] + deep
        vel_out[rows, :] = vel_ref[rows, :] + vel
    for i in range(pairs):
        is_lower = lax.axis_index(AXES[1]) == i
        for x in range(EX):
            row = EY * x
            messages[i][LAYERS * x : LAYERS * (x + 1), :] = jnp.where(
                is_lower, deep_out[row + EY - LAYERS : row + EY, :], deep_out[row : row + LAYERS, :]
            )
            at = LAYERS * EX + 2 * x
            messages[i][at : at + 2, :] = jnp.where(
                is_lower, vel_out[row + EY - 2 : row + EY, :], vel_out[row : row + 2, :]
            )


def join_y_kernel(pairs, deep_ref, vel_ref, *refs):
    received, (deep_out, vel_out, odd_ref, even_ref, before_ref, after_ref) = refs[:pairs], refs[pairs:]
    before = jnp.zeros_like(before_ref)
    after = jnp.zeros_like(after_ref)
    for i in range(pairs):
        before = jnp.where(lax.axis_index(AXES[1]) == i + 1, received[i][...], before)
        after = jnp.where(lax.axis_index(AXES[1]) == i, received[i][...], after)
    before_ref[...] = before
    after_ref[...] = after
    deep_out[...] = jnp.zeros_like(deep_out)
    vel_out[...] = jnp.zeros_like(vel_out)
    for x in range(EX):
        row = EY * x
        deep_out[x, OFF : OFF + EY, :] = deep_ref[row : row + EY, :]
        deep_out[x, 0:LAYERS, :] += before_ref[LAYERS * x : LAYERS * (x + 1), :]
        deep_out[x, OFF + CY : OFF + CY + LAYERS, :] += after_ref[LAYERS * x : LAYERS * (x + 1), :]
        at = LAYERS * EX + 2 * x
        vel_out[x, OFF : OFF + EY, :] = vel_ref[row : row + EY, :]
        vel_out[x, OFF : OFF + 2, :] += before_ref[at : at + 2, :]
        vel_out[x, OFF + CY : OFF + CY + 2, :] += after_ref[at : at + 2, :]
    is_even = lax.rem(lax.axis_index(AXES[0]), 2) == 0

    def put(rows, low, high):
        odd_ref[rows, :] = jnp.where(is_even, low, high)
        even_ref[rows, :] = jnp.where(is_even, high, low)

    for x in range(LAYERS):
        put(slice(SY * x, SY * (x + 1)), deep_out[x, 0:SY, :], deep_out[EX - LAYERS + x, 0:SY, :])
    for x in range(2):
        at = SY * LAYERS + EY * x
        put(slice(at, at + EY), vel_out[x, OFF : OFF + EY, :], vel_out[EX - 2 + x, OFF : OFF + EY, :])


def determinant(m):
    return (
        m[0][0] * (m[1][1] * m[2][2] - m[1][2] * m[2][1])
        - m[0][1] * (m[1][0] * m[2][2] - m[1][2] * m[2][0])
        + m[0][2] * (m[1][0] * m[2][1] - m[1][1] * m[2][0])
    )


def left_product(m, i, j):
    return m[i][0] * m[j][0] + m[i][1] * m[j][1] + m[i][2] * m[j][2]


def stress_rows(mapped, damaged):
    degrade = (1.0 - damaged) ** 2
    pressure = bulk_coef * (determinant(mapped) - 1.0)
    rows = {}
    for i in range(3):
        for j in range(i, 3):
            term = shear_mod * (left_product(mapped, i, j) - (1.0 if i == j else 0.0))
            if i == j:
                term = term + pressure
            rows[14 + 3 * i + j] = rows[14 + 3 * j + i] = degrade * term
    return rows


def unpack(packed_ref, out_ref, left=None):
    rows = {f: packed_ref[MOST * at : MOST * (at + 1), :] for at, f in enumerate(SENT)}
    rows.update(stress_rows([[rows[5 + 3 * i + j] for j in range(3)] for i in range(3)], rows[23]))
    for f in range(FIELDS):
        value = rows[f]
        if left is not None:
            value = jnp.where(lax.broadcasted_iota(jnp.int32, (MOST, BIN), 0) < left, value, 0.0)
        for t in range(MOST):
            out_ref[f : f + 1, t * BIN : (t + 1) * BIN] = value[t : t + 1]


def gather_update(index, nodes_ref, part_ref, base_ref, w_ref, g_ref, out_ref, out_index, packed):
    lanes = slice(index * CHUNK, (index + 1) * CHUNK)
    to = slice(out_index * CHUNK, (out_index + 1) * CHUNK)
    onehot = onehot_rows(base_ref, lanes)
    base_z = base_ref[2:3, lanes]
    rows = lax.broadcasted_iota(jnp.int32, (ZROWS, CHUNK), 0) - base_z
    at = rows == 0
    after = rows == 1

    def pick(mask, value):
        kept = jnp.where(mask, value, 0.0)
        total = kept[0:8]
        for t in range(1, ZROWS // 8):
            total = total + kept[8 * t : 8 * t + 8]
        return total

    moved = [jnp.zeros((8, CHUNK), F32) for _ in range(3)]
    velgrad = [[jnp.zeros((8, CHUNK), F32) for _ in range(3)] for _ in range(3)]
    damage_node = jnp.zeros((8, CHUNK), F32)
    rows_ab = 4 * ZROWS
    for corner in range(4):
        start = 2 * rows_ab * corner
        near = jnp.dot(nodes_ref[start : start + rows_ab, 0:AROWS], onehot, preferred_element_type=F32) + jnp.dot(
            nodes_ref[start + rows_ab : start + 2 * rows_ab, 0:AROWS], onehot, preferred_element_type=F32
        )
        for c, mask in enumerate((at, after)):
            k = 2 * corner + c
            weight = w_ref[k : k + 1, lanes]
            slope = [g_ref[j, k : k + 1, lanes] for j in range(3)]
            for i in range(3):
                value = pick(mask, near[ZROWS * i : ZROWS * (i + 1)])
                moved[i] = moved[i] + value * weight
                for j in range(3):
                    velgrad[i][j] = velgrad[i][j] + value * slope[j]
            damage_node = damage_node + pick(mask, near[3 * ZROWS : 4 * ZROWS]) * weight
    moved = [jnp.sum(v, axis=0, keepdims=True) for v in moved]
    velgrad = [[jnp.sum(v, axis=0, keepdims=True) for v in row] for row in velgrad]
    damage_node = jnp.sum(damage_node, axis=0, keepdims=True)

    def field(i):
        return part_ref[i : i + 1, lanes]

    deform = [[field(5 + 3 * i + j) for j in range(3)] for i in range(3)]
    stretch = [[(1.0 if i == j else 0.0) + time_step * velgrad[i][j] for j in range(3)] for i in range(3)]
    mapped = [
        [
            stretch[i][0] * deform[0][j] + stretch[i][1] * deform[1][j] + stretch[i][2] * deform[2][j]
            for j in range(3)
        ]
        for i in range(3)
    ]
    damaged = jnp.maximum(field(23), damage_node)
    jacobian = determinant(mapped)
    trace = left_product(mapped, 0, 0) + left_product(mapped, 1, 1) + left_product(mapped, 2, 2)
    energy = 0.5 * shear_mod * (trace - 3.0) + 0.5 * bulk_coef * (jacobian - 1.0) ** 2
    rows = {f: field(f) for f in range(2)}
    for i in range(3):
        rows[2 + i] = moved[i]
        rows[25 + i] = field(25 + i) + time_step * moved[i]
        for j in range(3):
            rows[5 + 3 * i + j] = mapped[i][j]
    rows[23] = damaged
    rows[24] = jnp.maximum(field(24), energy)
    if packed:
        for at, f in enumerate(SENT):
            for t in range(CHUNK // BIN):
                row = MOST * (MOST * (at // MOST) + out_index * (CHUNK // BIN) + t) + at % MOST
                out_ref[row : row + 1, :] = rows[f][:, t * BIN : (t + 1) * BIN]
    else:
        rows.update(stress_rows(mapped, damaged))
        for f in range(FIELDS):
            out_ref[f : f + 1, to] = rows[f]


def relax_kernel(turn, axis_sizes, *refs):
    tail_before = refs[10]
    refs = refs if turn == 0 else refs[:8] + refs[11:]
    is_far = lax.rem(lax.axis_index(AXES[2]), FAR) == 0

    @pl.when(is_far if turn else jnp.logical_not(is_far))
    def _():
        relax_body(axis_sizes, *refs)

    if turn:

        @pl.when(jnp.logical_not(is_far))
        def _():
            refs[10][...] = tail_before[...]


def relax_body(
    axis_sizes,
    deep_ref,
    vel_ref,
    odd_ref,
    even_ref,
    part_ref,
    base_ref,
    w_ref,
    g_ref,
    damage_hbm,
    nodes_ref,
    tail_ref,
    sums_ref,
    one_ref,
    two_ref,
    keep_ref,
    add_ref,
    spread_ref,
    inverse_ref,
    fv_ref,
    fd_ref,
    damage_ref,
    rows_ref,
    before_ref,
    after_ref,
    sem,
):
    is_even = lax.rem(lax.axis_index(AXES[0]), 2) == 0
    before_ref[...] = jnp.where(is_even, odd_ref[...], even_ref[...])
    after_ref[...] = jnp.where(is_even, even_ref[...], odd_ref[...])
    count_x, count_y, count_z = axis_sizes
    sums_ref[...] = jnp.zeros_like(sums_ref)
    for xd in range(SX):
        if OFF <= xd < OFF + EX:
            sums_ref[xd] = deep_ref[xd - OFF]
        if xd < LAYERS:
            sums_ref[xd, 0:SY, :] += before_ref[SY * xd : SY * (xd + 1), :]
        if xd >= SX - LAYERS:
            at = SY * (xd - SX + LAYERS)
            sums_ref[xd, 0:SY, :] += after_ref[at : at + SY, :]
    lane = lane_index(PITCH)
    pos_x = lax.axis_index(AXES[0]) * CX - WIDE + three(lane, SZ, 0, PACK, 2 * PACK)
    pos_y = lax.axis_index(AXES[1]) * CY - WIDE + lax.broadcasted_iota(jnp.int32, (PITCH, 128), 0)
    pos_z = lax.axis_index(AXES[2]) * CZ - WIDE + lane - three(lane, SZ, 0, SZ, 2 * SZ)
    inside_yz = (
        (lane < 3 * SZ) & (pos_y >= 0) & (pos_y < count_y * CY) & (pos_z >= 0) & (pos_z < count_z * CZ)
    )
    for j in range(PACK):
        first, second, third = sums_ref[j], sums_ref[j + PACK], sums_ref[j + 2 * PACK]
        mass = three(lane, SZ, first, shift_lanes(second, SZ), shift_lanes(third, 2 * SZ))
        damage = three(lane, SZ, shift_lanes(first, -SZ), second, shift_lanes(third, SZ))
        drive = three(lane, SZ, shift_lanes(first, -2 * SZ), shift_lanes(second, -SZ), third)
        mask = (inside_yz & (pos_x + j >= 0) & (pos_x + j < count_x * CX)).astype(F32)
        inverse = mask / jnp.maximum(mass, mass_floor)
        drive = (2.0 * relax_rate) * (drive * inverse)
        keep_ref[j] = (1.0 - relax_rate * (1.0 + 6.0 * length_sq)) * mask - drive
        add_ref[j] = drive
        spread_ref[j] = (relax_rate * length_sq) * mask
        one_ref[j] = damage * inverse
        inverse_ref[j] = inverse
    source, target = one_ref, two_ref
    for _ in range(SUBSTEPS):
        for j in range(PACK):
            centre = source[j]
            lower = source[j - 1] if j > 0 else shift_lanes(source[PACK - 1], SZ)
            upper = source[j + 1] if j < PACK - 1 else shift_lanes(source[0], -SZ)
            around = (
                (lower + upper)
                + (pltpu.roll(centre, 1, 0) + pltpu.roll(centre, PITCH - 1, 0))
                + (shift_lanes(centre, 1) + shift_lanes(centre, -1))
            )
            target[j] = (centre * keep_ref[j] + add_ref[j]) + spread_ref[j] * around
        source, target = target, source
    for x in range(CX):
        xd = x + WIDE
        value = shift_lanes(source[xd % PACK], -SZ * (xd // PACK) - WIDE)
        damage_ref[x] = value[WIDE : WIDE + CY, 0:CZ]
    move = pltpu.make_async_copy(damage_ref, damage_hbm, sem)
    move.start()
    fv_ref[...] = jnp.zeros_like(fv_ref)
    fd_ref[...] = jnp.zeros_like(fd_ref)
    vel_at = SY * LAYERS
    lane = lane_index(EY)
    for x in range(EX):
        vel = vel_ref[x, OFF : OFF + EY, :]
        if x < 2:
            vel = vel + before_ref[vel_at + EY * x : vel_at + EY * (x + 1), :]
        if x >= EX - 2:
            at = vel_at + EY * (x - EX + 2)
            vel = vel + after_ref[at : at + EY, :]
        slot, group = (x + OFF) % PACK, (x + OFF) // PACK
        inverse = inverse_ref[slot, OFF : OFF + EY, :]
        vel = three(lane, ZROWS, *(shift_lanes(vel, (ZROWS - SZ) * ch - OFF) for ch in range(3)))
        inverse = three(lane, ZROWS, *(shift_lanes(inverse, ZROWS * ch - SZ * group - OFF) for ch in range(3)))
        fv_ref[EY * x : EY * (x + 1), :] = vel * inverse
        fd_ref[EY * x : EY * (x + 1), :] = shift_lanes(source[slot], -SZ * group - OFF)[OFF : OFF + EY, :]
    nodes = jnp.concatenate([fv_ref[...].T[0 : 3 * ZROWS], fd_ref[...].T[0:ZROWS]], axis=0)
    for corner in range(4):
        shift = (corner >> 1) * EY + (corner & 1)
        value = nodes if shift == 0 else pltpu.roll(nodes, 256 - shift, 1)
        high = value.astype(BF16)
        low = (value - high.astype(F32)).astype(BF16)
        start = 8 * ZROWS * corner
        nodes_ref[start : start + 4 * ZROWS, :] = high
        nodes_ref[start + 4 * ZROWS : start + 8 * ZROWS, :] = low
    for index in range(TAIL // CHUNK):
        gather_update((COUNT - TAIL) // CHUNK + index, nodes_ref, part_ref, base_ref, w_ref, g_ref, rows_ref, index, True)
    for at in range(len(SENT)):
        first = MOST * MOST * (at // MOST) + at % MOST
        tail_ref[MOST * at : MOST * (at + 1), :] = rows_ref[pl.ds(first, MOST, stride=MOST), :]
    move.wait()


def head_kernel(
    counts_ref, prior_ref, nodes_ref, tail_ref, part_ref, base_ref, w_ref, g_ref, out_hbm, head_ref, left_ref, zero_ref, sems
):
    prior = prior_ref[0, 3 * SZ].astype(jnp.int32)
    left = MOST - counts_ref[0]
    zero_ref[...] = jnp.zeros_like(zero_ref)
    blanks = []
    for i in range(MOST):
        to = pl.ds(pl.multiple_of((NBIN + MOST - 1 - i) * BIN, BIN), BIN)
        blanks.append((i < MOST - prior, pltpu.make_async_copy(zero_ref, out_hbm.at[:, to], sems.at[2 + i])))
    for wanted, move in blanks:
        pl.when(wanted)(move.start)
    unpack(tail_ref, left_ref, left)
    to = pl.ds(pl.multiple_of((prior + NBIN - MOST) * BIN, BIN), TAIL)
    own = pltpu.make_async_copy(left_ref, out_hbm.at[:, to], sems.at[0])
    own.start()
    for index in range((COUNT - TAIL) // CHUNK):
        gather_update(index, nodes_ref, part_ref, base_ref, w_ref, g_ref, head_ref, index, False)
    to = pl.ds(pl.multiple_of(prior * BIN, BIN), COUNT - TAIL)
    stay = pltpu.make_async_copy(head_ref, out_hbm.at[:, to], sems.at[1])
    stay.start()
    for wanted, move in blanks:
        pl.when(wanted)(move.wait)
    own.wait()
    stay.wait()


def arrive_kernel(turn, prior_ref, packed_ref, partial_hbm, out_hbm, recv_ref, sems):
    is_far = lax.rem(lax.axis_index(AXES[2]), FAR) == 0

    @pl.when(jnp.logical_not(is_far) if turn else is_far)
    def _():
        prior = prior_ref[0, 3 * SZ].astype(jnp.int32)
        unpack(packed_ref, recv_ref)
        moves = []
        for slot in range(MOST):
            source = pl.ds(pl.multiple_of(jnp.minimum(MOST - prior + slot, MOST - 1) * BIN, BIN), BIN)
            target = out_hbm.at[:, slot * BIN : (slot + 1) * BIN]
            moves.append((slot < prior, pltpu.make_async_copy(recv_ref.at[:, source], target, sems.at[slot])))
        for wanted, move in moves:
            pl.when(wanted)(move.start)
        for wanted, move in moves:
            pl.when(wanted)(move.wait)


def shape(*dims, kind=F32):
    return jax.ShapeDtypeStruct(dims, kind)


SMEM = pltpu.SMEM
HBM = pltpu.HBM


def call(kernel, out_shape, spaces, args, out_spaces=None, scratch=(), flops=0, aliases=None, limit=None):
    leaves = jax.tree.leaves(out_shape)
    out_spaces = out_spaces or [VMEM] * len(leaves)
    out_specs = [pl.BlockSpec(memory_space=s) for s in out_spaces]
    return pl.pallas_call(
        kernel,
        out_shape=out_shape,
        in_specs=[pl.BlockSpec(memory_space=s) for s in spaces],
        out_specs=tuple(out_specs) if isinstance(out_shape, tuple) else out_specs[0],
        scratch_shapes=list(scratch),
        input_output_aliases=aliases or {},
        compiler_params=pltpu.CompilerParams(vmem_limit_bytes=(limit or 48 * 1024) * 1024),
        cost_estimate=pl.CostEstimate(flops=flops, bytes_accessed=2000000, transcendentals=0),
    )(*args)


def swap_pairs(odd, even, axis, extra=()):
    count = lax.axis_size(axis)
    odd_pairs = [(i, i + 1) for i in range(1, count - 1, 2)]
    even_pairs = [(i, i + 1) for i in range(0, count - 1, 2)]
    from_odd = lax.ppermute(odd, axis, odd_pairs + [(j, i) for i, j in odd_pairs] + list(extra))
    return from_odd, lax.ppermute(even, axis, even_pairs + [(j, i) for i, j in even_pairs])


def per_device(particles, stencil_base, weights, gradients, counts):
    sizes = tuple(lax.axis_size(a) for a in AXES)
    inputs = (particles, stencil_base, weights, gradients)
    deep, vel, odd, even = call(
        scatter_kernel,
        (VMEM((GROWS, 128), F32), VMEM((GROWS, 128), F32), VMEM((GROUP, 128), F32), VMEM((GROUP, 128), F32)),
        [SMEM] + [HBM] * 4,
        (counts,) + inputs,
        scratch=[
            VMEM((FIELDS, COUNT), F32),
            VMEM((3, COUNT), jnp.int32),
            VMEM((8, COUNT), F32),
            VMEM((3, 8, COUNT), F32),
            VMEM((4, 2 * HALF, 256), F32),
            VMEM((256, 256), F32),
            VMEM((2, 6, 8, COUNT), F32),
            VMEM((8 * HALF, 2 * COUNT), BF16),
            VMEM((AROWS, COUNT), BF16),
            pltpu.SemaphoreType.DMA((4,)),
        ],
        limit=SCATTER_KIB,
    )
    count_z = sizes[2]
    from_odd, from_even = swap_pairs(odd, even, "gz", [(count_z - 1, 0)])
    message = LAYERS * EX + 2 * EX
    pairs = sizes[1] - 1
    deep, vel, prior, *messages = call(
        lambda *refs: join_z_kernel(pairs, *refs),
        (shape(GROWS, 128), shape(GROWS, 128), shape(8, 128)) + (shape(message, 128),) * pairs,
        [VMEM] * 4,
        (deep, vel, from_odd, from_even),
    )
    received = [lax.ppermute(messages[i], "gy", [(i, i + 1), (i + 1, i)]) for i in range(pairs)]
    wide_message = LAYERS * SY + 2 * EY
    deep, vel, odd, even = call(
        lambda *refs: join_y_kernel(pairs, *refs),
        (shape(EX, PITCH, 128), shape(EX, PITCH, 128), shape(wide_message, 128), shape(wide_message, 128)),
        [VMEM] * (2 + pairs),
        (deep, vel, *received),
        scratch=[VMEM((message, 128), F32)] * 2,
    )
    from_odd, from_even = swap_pairs(odd, even, "gx")

    ring = [(i, (i + 1) % count_z) for i in range(count_z)]
    far = [edge for edge in ring if edge[1] % FAR == 0]
    near = [edge for edge in ring if edge[1] % FAR != 0]
    results = ()
    for turn in range(2):
        results = call(
            lambda *refs, turn=turn: relax_kernel(turn, sizes, *refs),
            (shape(CX, CY, CZ), VMEM((32 * ZROWS, 256), BF16), VMEM((len(SENT) * MOST, BIN), F32)),
            [VMEM] * 8 + [HBM, VMEM, VMEM][: len(results)],
            (deep, vel, from_odd, from_even) + inputs + tuple(results),
            out_spaces=[HBM, VMEM, VMEM],
            scratch=[VMEM((SX, PITCH, 128), F32)]
            + [VMEM((PACK, PITCH, 128), F32)] * 6
            + [VMEM((256, 128), F32)] * 2
            + [VMEM((CX, CY, CZ), F32), VMEM((3 * MOST * MOST, BIN), F32)]
            + [VMEM((wide_message, 128), F32)] * 2
            + [pltpu.SemaphoreType.DMA],
            aliases={8: 0, 9: 1} if turn else {},
        )
        if turn == 0:
            recv_far = lax.ppermute(results[2], "gz", far)
    damage, nodes, tail = results
    recv_near = lax.ppermute(tail, "gz", near)
    own = call(
        head_kernel,
        shape(FIELDS, SLOTS),
        [SMEM] + [VMEM] * 7,
        (counts, prior, nodes, tail) + inputs,
        out_spaces=[HBM],
        scratch=[
            VMEM((FIELDS, COUNT - TAIL), F32),
            VMEM((FIELDS, TAIL), F32),
            VMEM((FIELDS, BIN), F32),
            pltpu.SemaphoreType.DMA((2 + MOST,)),
        ],
        flops=2 * 1280 * 256 * 1024,
    )
    migrated = own
    for turn, recv in enumerate((recv_far, recv_near)):
        migrated = call(
            lambda *refs, turn=turn: arrive_kernel(turn, *refs),
            shape(FIELDS, SLOTS),
            [VMEM, VMEM, HBM],
            (prior, recv, migrated),
            out_spaces=[HBM],
            scratch=[VMEM((FIELDS, TAIL), F32), pltpu.SemaphoreType.DMA((MOST,))],
            aliases={2: 0},
        )
    return (migrated, damage)


def solution(mesh):
    return jax.shard_map(
        per_device,
        mesh=mesh,
        in_specs=(
            P(None, ("gx", "gy", "gz")),
            P(None, ("gx", "gy", "gz")),
            P(None, ("gx", "gy", "gz")),
            P(None, None, ("gx", "gy", "gz")),
            P(("gx", "gy", "gz")),
        ),
        out_specs=(P(None, ("gx", "gy", "gz")), P("gx", "gy", "gz")),
        check_vma=False,
    )
```

```python
import jax
import jax.numpy as jnp
from jax import lax
from jax.experimental import pallas as pl
from jax.experimental.pallas import tpu as pltpu
from jax.sharding import PartitionSpec as P

CX = 8
CY = 16
CZ = 32
NBIN = 16
BIN = 128
SUBSTEPS = 4
FIELDS = 28
MOST = 8
COUNT = NBIN * BIN
TAIL = MOST * BIN
SLOTS = (NBIN + MOST) * BIN

time_step = 0.1
relax_rate = 0.2
length_sq = 0.6
shear_mod = 1.0
bulk_coef = 1.5
mass_floor = 0.5

EX = CX + 2
EY = CY + 2
EZ = CZ + 2
WIDE = SUBSTEPS + 1
LAYERS = WIDE + 1
SX = CX + 2 * WIDE
SY = CY + 2 * WIDE
SZ = CZ + 2 * WIDE
OFF = WIDE - 1
PITCH = 32
AROWS = 176
GROWS = 200
GROUP = 40
REACH = tuple(max(i - 1, 0) for i in range(LAYERS))
ROWS_AT = tuple(sum(SY - 2 * r for r in REACH[:i]) for i in range(LAYERS + 1))
HALF = 104
PACK = SX // 3
ZROWS = 40
CHUNK = 256
FAR = 4
SENT = tuple(range(14)) + tuple(range(23, FIELDS))
AXES = ("gx", "gy", "gz")
F32 = jnp.float32
BF16 = jnp.bfloat16
SCATTER_KIB = 56000
VMEM = pltpu.VMEM


def shift_lanes(value, by):
    by = by % 128
    return value if by == 0 else pltpu.roll(value, by, 1)


def channel_lane(lane):
    return jnp.where(
        lane < SZ, lane, jnp.where(lane < 2 * SZ, lane - SZ, jnp.where(lane < 3 * SZ, lane - 2 * SZ, 1000))
    )


def three(lane, width, a, b, c):
    return jnp.where(lane < width, a, jnp.where(lane < 2 * width, b, c))


def lane_index(rows):
    return lax.broadcasted_iota(jnp.int32, (rows, 128), 1)


def onehot_rows(base_ref, lanes):
    xy = base_ref[0:1, lanes] * EY + base_ref[1:2, lanes]
    rows = lax.broadcasted_iota(jnp.int32, (AROWS, CHUNK), 0)
    return jnp.where(rows == xy, 1.0, 0.0).astype(BF16)


def scatter_kernel(
    counts_ref,
    part_hbm,
    base_hbm,
    w_hbm,
    g_hbm,
    deep_ref,
    vel_ref,
    odd_ref,
    even_ref,
    part_ref,
    base_ref,
    w_ref,
    g_ref,
    acc_ref,
    wide_ref,
    term_ref,
    rows_ref,
    onehot_ref,
    sems,
):
    moves = [
        pltpu.make_async_copy(source, target, sems.at[i])
        for i, (source, target) in enumerate(
            ((base_hbm, base_ref), (part_hbm, part_ref), (w_hbm, w_ref), (g_hbm, g_ref))
        )
    ]
    for move in moves:
        move.start()
    acc_ref[...] = jnp.zeros_like(acc_ref)
    wide_ref[...] = jnp.zeros_like(wide_ref)
    moves[0].wait()
    for index in range(COUNT // CHUNK):
        lanes = slice(index * CHUNK, (index + 1) * CHUNK)
        onehot_ref[:, lanes] = onehot_rows(base_ref, lanes)
    for move in moves[1:]:
        move.wait()
    for index in range(COUNT // CHUNK):
        lanes = slice(index * CHUNK, (index + 1) * CHUNK)
        minus_vol = -time_step * part_ref[1:2, lanes]
        share = part_ref[0:1, lanes] * w_ref[:, lanes]
        slope = [g_ref[j, :, lanes] for j in range(3)]
        terms = [share, share * part_ref[23:24, lanes], share * part_ref[24:25, lanes]]
        for i in range(3):
            row = 14 + 3 * i
            pull = (
                part_ref[row : row + 1, lanes] * slope[0]
                + part_ref[row + 1 : row + 2, lanes] * slope[1]
                + part_ref[row + 2 : row + 3, lanes] * slope[2]
            )
            terms.append(share * part_ref[2 + i : 3 + i, lanes] + minus_vol * pull)
        for ch, term in enumerate(terms):
            high = term.astype(BF16).astype(F32)
            term_ref[0, ch, :, lanes] = high
            term_ref[1, ch, :, lanes] = term - high
    nt = (((1,), (1,)), ((), ()))
    for corner in range(4):
        k = 2 * corner
        for index in range(COUNT // CHUNK):
            lanes = slice(index * CHUNK, (index + 1) * CHUNK)
            sub = lax.broadcasted_iota(jnp.int32, (8, CHUNK), 0) - base_ref[2:3, lanes]
            for part in range(2):
                tiles = {}
                for tile in range(HALF // 8):
                    first = [(ch, EZ * ch - 8 * tile) for ch in range(3) if EZ * ch < 8 * tile + 8 and EZ * (ch + 1) > 8 * tile]
                    for half in range(2):
                        value = jnp.zeros((8, CHUNK), F32)
                        for ch, at in first:
                            value = jnp.where(sub == at, term_ref[part, 3 * half + ch, k : k + 1, lanes], value)
                            value = jnp.where(sub == at + 1, term_ref[part, 3 * half + ch, k + 1 : k + 2, lanes], value)
                        tiles[half * (HALF // 8) + tile] = value
                to = slice(part * COUNT + index * CHUNK, part * COUNT + (index + 1) * CHUNK)
                for pair in range(HALF // 8):
                    row = 2 * HALF * corner + 16 * pair
                    rows_ref[row : row + 16, to] = jnp.concatenate([tiles[2 * pair], tiles[2 * pair + 1]], axis=0).astype(BF16)
        rows = slice(2 * HALF * corner, 2 * HALF * (corner + 1))
        piece = lax.dot_general(rows_ref[rows, 0:COUNT], onehot_ref[...], nt, preferred_element_type=F32)
        piece = piece + lax.dot_general(rows_ref[rows, COUNT:], onehot_ref[...], nt, preferred_element_type=F32)
        acc_ref[corner, :, 0:AROWS] = piece
    total = acc_ref[0]
    for corner in range(1, 4):
        total = total + pltpu.roll(acc_ref[corner], (corner >> 1) * EY + (corner & 1), 1)
    for half in range(2):
        for ch in range(3):
            row = half * HALF + EZ * ch
            to = half * 128 + SZ * ch + OFF
            wide_ref[to : to + EZ, :] = total[row : row + EZ]
    deep_ref[...] = wide_ref[0:128, :].T[0:GROWS]
    vel_ref[...] = wide_ref[128:256, :].T[0:GROWS]
    lane = lane_index(GROUP)
    place = channel_lane(lane)
    low_msg = jnp.zeros((GROUP, 128), F32)
    high_msg = jnp.zeros((GROUP, 128), F32)
    for j in range(5):
        rows = slice(GROUP * j, GROUP * (j + 1))
        deep = deep_ref[rows, :]
        vel = vel_ref[rows, :]
        inside = (place >= 8 * j) & (place < 8 * j + LAYERS)
        low_msg = jnp.where(inside, shift_lanes(deep, 8 * j - OFF), low_msg)
        high_msg = jnp.where(inside, shift_lanes(deep, 8 * j - CZ), high_msg)
        inside = (place >= 8 * j + LAYERS) & (place < 8 * j + LAYERS + 2)
        low_msg = jnp.where(inside, shift_lanes(vel, 8 * j + LAYERS - OFF), low_msg)
        high_msg = jnp.where(inside, shift_lanes(vel, 8 * j + LAYERS - OFF - CZ), high_msg)
    high_msg = jnp.where(lane >= 3 * SZ, counts_ref[0].astype(F32), high_msg)
    is_even = lax.rem(lax.axis_index(AXES[2]), 2) == 0
    odd_ref[...] = jnp.where(is_even, low_msg, high_msg)
    even_ref[...] = jnp.where(is_even, high_msg, low_msg)


def join_z_kernel(pairs, deep_ref, vel_ref, odd_ref, even_ref, deep_out, vel_out, prior_ref, *messages):
    place = channel_lane(lane_index(GROUP))
    is_even = lax.rem(lax.axis_index(AXES[2]), 2) == 0
    before = jnp.where(is_even, odd_ref[...], even_ref[...])
    after = jnp.where(is_even, even_ref[...], odd_ref[...])
    prior_ref[...] = before[0:8]
    before = jnp.where(lax.axis_index(AXES[2]) > 0, before, 0.0)
    deep_low, deep_high = place < LAYERS, (place >= SZ - LAYERS) & (place < SZ)
    vel_low = (place >= OFF) & (place < OFF + 2)
    vel_high = (place >= OFF + CZ) & (place < OFF + CZ + 2)
    for j in range(5):
        rows = slice(GROUP * j, GROUP * (j + 1))
        deep = jnp.where(
            deep_low,
            shift_lanes(before, -8 * j),
            jnp.where(deep_high, shift_lanes(after, SZ - LAYERS - 8 * j), 0.0),
        )
        vel = jnp.where(
            vel_low,
            shift_lanes(before, OFF - 8 * j - LAYERS),
            jnp.where(vel_high, shift_lanes(after, OFF + CZ - 8 * j - LAYERS), 0.0),
        )
        deep_out[rows, :] = deep_ref[rows, :] + deep
        vel_out[rows, :] = vel_ref[rows, :] + vel
    for i in range(pairs):
        is_lower = lax.axis_index(AXES[1]) == i
        for x in range(EX):
            row = EY * x
            messages[i][LAYERS * x : LAYERS * (x + 1), :] = jnp.where(
                is_lower, deep_out[row + EY - LAYERS : row + EY, :], deep_out[row : row + LAYERS, :]
            )
            at = LAYERS * EX + 2 * x
            messages[i][at : at + 2, :] = jnp.where(
                is_lower, vel_out[row + EY - 2 : row + EY, :], vel_out[row : row + 2, :]
            )


def join_y_kernel(pairs, deep_ref, vel_ref, *refs):
    received, (deep_out, vel_out, odd_ref, even_ref, before_ref, after_ref) = refs[:pairs], refs[pairs:]
    before = jnp.zeros_like(before_ref)
    after = jnp.zeros_like(after_ref)
    for i in range(pairs):
        before = jnp.where(lax.axis_index(AXES[1]) == i + 1, received[i][...], before)
        after = jnp.where(lax.axis_index(AXES[1]) == i, received[i][...], after)
    before_ref[...] = before
    after_ref[...] = after
    deep_out[...] = jnp.zeros_like(deep_out)
    vel_out[...] = jnp.zeros_like(vel_out)
    for x in range(EX):
        row = EY * x
        deep_out[x, OFF : OFF + EY, :] = deep_ref[row : row + EY, :]
        deep_out[x, 0:LAYERS, :] += before_ref[LAYERS * x : LAYERS * (x + 1), :]
        deep_out[x, OFF + CY : OFF + CY + LAYERS, :] += after_ref[LAYERS * x : LAYERS * (x + 1), :]
        at = LAYERS * EX + 2 * x
        vel_out[x, OFF : OFF + EY, :] = vel_ref[row : row + EY, :]
        vel_out[x, OFF : OFF + 2, :] += before_ref[at : at + 2, :]
        vel_out[x, OFF + CY : OFF + CY + 2, :] += after_ref[at : at + 2, :]
    is_even = lax.rem(lax.axis_index(AXES[0]), 2) == 0

    def put(rows, low, high):
        odd_ref[rows, :] = jnp.where(is_even, low, high)
        even_ref[rows, :] = jnp.where(is_even, high, low)

    for x in range(LAYERS):
        rows = slice(REACH[x], SY - REACH[x])
        put(slice(ROWS_AT[x], ROWS_AT[x + 1]), deep_out[x, rows, :], deep_out[EX - 1 - x, rows, :])
    for x in range(2):
        at = ROWS_AT[LAYERS] + EY * x
        put(slice(at, at + EY), vel_out[x, OFF : OFF + EY, :], vel_out[EX - 2 + x, OFF : OFF + EY, :])


def determinant(m):
    return (
        m[0][0] * (m[1][1] * m[2][2] - m[1][2] * m[2][1])
        - m[0][1] * (m[1][0] * m[2][2] - m[1][2] * m[2][0])
        + m[0][2] * (m[1][0] * m[2][1] - m[1][1] * m[2][0])
    )


def left_product(m, i, j):
    return m[i][0] * m[j][0] + m[i][1] * m[j][1] + m[i][2] * m[j][2]


def stress_rows(mapped, damaged):
    degrade = (1.0 - damaged) ** 2
    pressure = bulk_coef * (determinant(mapped) - 1.0)
    rows = {}
    for i in range(3):
        for j in range(i, 3):
            term = shear_mod * (left_product(mapped, i, j) - (1.0 if i == j else 0.0))
            if i == j:
                term = term + pressure
            rows[14 + 3 * i + j] = rows[14 + 3 * j + i] = degrade * term
    return rows


def unpack(packed_ref, out_ref, left=None):
    rows = {f: packed_ref[MOST * at : MOST * (at + 1), :] for at, f in enumerate(SENT)}
    rows.update(stress_rows([[rows[5 + 3 * i + j] for j in range(3)] for i in range(3)], rows[23]))
    for f in range(FIELDS):
        value = rows[f]
        if left is not None:
            value = jnp.where(lax.broadcasted_iota(jnp.int32, (MOST, BIN), 0) < left, value, 0.0)
        for t in range(MOST):
            out_ref[f : f + 1, t * BIN : (t + 1) * BIN] = value[t : t + 1]


def gather_update(index, nodes_ref, part_ref, base_ref, w_ref, g_ref, out_ref, out_index, packed):
    lanes = slice(index * CHUNK, (index + 1) * CHUNK)
    to = slice(out_index * CHUNK, (out_index + 1) * CHUNK)
    onehot = onehot_rows(base_ref, lanes)
    base_z = base_ref[2:3, lanes]
    rows = lax.broadcasted_iota(jnp.int32, (ZROWS, CHUNK), 0) - base_z
    at = rows == 0
    after = rows == 1

    def pick(mask, value):
        kept = jnp.where(mask, value, 0.0)
        total = kept[0:8]
        for t in range(1, ZROWS // 8):
            total = total + kept[8 * t : 8 * t + 8]
        return total

    moved = [jnp.zeros((8, CHUNK), F32) for _ in range(3)]
    velgrad = [[jnp.zeros((8, CHUNK), F32) for _ in range(3)] for _ in range(3)]
    damage_node = jnp.zeros((8, CHUNK), F32)
    rows_ab = 4 * ZROWS
    for corner in range(4):
        start = 2 * rows_ab * corner
        near = jnp.dot(nodes_ref[start : start + rows_ab, 0:AROWS], onehot, preferred_element_type=F32) + jnp.dot(
            nodes_ref[start + rows_ab : start + 2 * rows_ab, 0:AROWS], onehot, preferred_element_type=F32
        )
        for c, mask in enumerate((at, after)):
            k = 2 * corner + c
            weight = w_ref[k : k + 1, lanes]
            slope = [g_ref[j, k : k + 1, lanes] for j in range(3)]
            for i in range(3):
                value = pick(mask, near[ZROWS * i : ZROWS * (i + 1)])
                moved[i] = moved[i] + value * weight
                for j in range(3):
                    velgrad[i][j] = velgrad[i][j] + value * slope[j]
            damage_node = damage_node + pick(mask, near[3 * ZROWS : 4 * ZROWS]) * weight
    moved = [jnp.sum(v, axis=0, keepdims=True) for v in moved]
    velgrad = [[jnp.sum(v, axis=0, keepdims=True) for v in row] for row in velgrad]
    damage_node = jnp.sum(damage_node, axis=0, keepdims=True)

    def field(i):
        return part_ref[i : i + 1, lanes]

    deform = [[field(5 + 3 * i + j) for j in range(3)] for i in range(3)]
    stretch = [[(1.0 if i == j else 0.0) + time_step * velgrad[i][j] for j in range(3)] for i in range(3)]
    mapped = [
        [
            stretch[i][0] * deform[0][j] + stretch[i][1] * deform[1][j] + stretch[i][2] * deform[2][j]
            for j in range(3)
        ]
        for i in range(3)
    ]
    damaged = jnp.maximum(field(23), damage_node)
    jacobian = determinant(mapped)
    trace = left_product(mapped, 0, 0) + left_product(mapped, 1, 1) + left_product(mapped, 2, 2)
    energy = 0.5 * shear_mod * (trace - 3.0) + 0.5 * bulk_coef * (jacobian - 1.0) ** 2
    rows = {f: field(f) for f in range(2)}
    for i in range(3):
        rows[2 + i] = moved[i]
        rows[25 + i] = field(25 + i) + time_step * moved[i]
        for j in range(3):
            rows[5 + 3 * i + j] = mapped[i][j]
    rows[23] = damaged
    rows[24] = jnp.maximum(field(24), energy)
    if packed:
        for at, f in enumerate(SENT):
            for t in range(CHUNK // BIN):
                row = MOST * (MOST * (at // MOST) + out_index * (CHUNK // BIN) + t) + at % MOST
                out_ref[row : row + 1, :] = rows[f][:, t * BIN : (t + 1) * BIN]
    else:
        rows.update(stress_rows(mapped, damaged))
        for f in range(FIELDS):
            out_ref[f : f + 1, to] = rows[f]


def relax_kernel(turn, axis_sizes, *refs):
    tail_before = refs[10]
    refs = refs if turn == 0 else refs[:8] + refs[11:]
    is_far = lax.rem(lax.axis_index(AXES[2]), FAR) == 0

    @pl.when(is_far if turn else jnp.logical_not(is_far))
    def _():
        relax_body(axis_sizes, *refs)

    if turn:

        @pl.when(jnp.logical_not(is_far))
        def _():
            refs[10][...] = tail_before[...]


def relax_body(
    axis_sizes,
    deep_ref,
    vel_ref,
    odd_ref,
    even_ref,
    part_ref,
    base_ref,
    w_ref,
    g_ref,
    damage_hbm,
    nodes_ref,
    tail_ref,
    sums_ref,
    one_ref,
    two_ref,
    keep_ref,
    add_ref,
    spread_ref,
    inverse_ref,
    fv_ref,
    fd_ref,
    damage_ref,
    rows_ref,
    before_ref,
    after_ref,
    sem,
):
    is_even = lax.rem(lax.axis_index(AXES[0]), 2) == 0
    before_ref[...] = jnp.where(is_even, odd_ref[...], even_ref[...])
    after_ref[...] = jnp.where(is_even, even_ref[...], odd_ref[...])
    count_x, count_y, count_z = axis_sizes
    sums_ref[...] = jnp.zeros_like(sums_ref)
    for xd in range(SX):
        if OFF <= xd < OFF + EX:
            sums_ref[xd] = deep_ref[xd - OFF]
        if xd < LAYERS:
            i = LAYERS - 1 - xd
            sums_ref[xd, REACH[i] : SY - REACH[i], :] += before_ref[ROWS_AT[i] : ROWS_AT[i + 1], :]
        if xd >= SX - LAYERS:
            i = xd - SX + LAYERS
            sums_ref[xd, REACH[i] : SY - REACH[i], :] += after_ref[ROWS_AT[i] : ROWS_AT[i + 1], :]
    lane = lane_index(PITCH)
    pos_x = lax.axis_index(AXES[0]) * CX - WIDE + three(lane, SZ, 0, PACK, 2 * PACK)
    pos_y = lax.axis_index(AXES[1]) * CY - WIDE + lax.broadcasted_iota(jnp.int32, (PITCH, 128), 0)
    pos_z = lax.axis_index(AXES[2]) * CZ - WIDE + lane - three(lane, SZ, 0, SZ, 2 * SZ)
    inside_yz = (
        (lane < 3 * SZ) & (pos_y >= 0) & (pos_y < count_y * CY) & (pos_z >= 0) & (pos_z < count_z * CZ)
    )
    for j in range(PACK):
        first, second, third = sums_ref[j], sums_ref[j + PACK], sums_ref[j + 2 * PACK]
        mass = three(lane, SZ, first, shift_lanes(second, SZ), shift_lanes(third, 2 * SZ))
        damage = three(lane, SZ, shift_lanes(first, -SZ), second, shift_lanes(third, SZ))
        drive = three(lane, SZ, shift_lanes(first, -2 * SZ), shift_lanes(second, -SZ), third)
        mask = (inside_yz & (pos_x + j >= 0) & (pos_x + j < count_x * CX)).astype(F32)
        inverse = mask / jnp.maximum(mass, mass_floor)
        drive = (2.0 * relax_rate) * (drive * inverse)
        keep_ref[j] = (1.0 - relax_rate * (1.0 + 6.0 * length_sq)) * mask - drive
        add_ref[j] = drive
        spread_ref[j] = (relax_rate * length_sq) * mask
        one_ref[j] = damage * inverse
        inverse_ref[j] = inverse
    source, target = one_ref, two_ref
    for _ in range(SUBSTEPS):
        for j in range(PACK):
            centre = source[j]
            lower = source[j - 1] if j > 0 else shift_lanes(source[PACK - 1], SZ)
            upper = source[j + 1] if j < PACK - 1 else shift_lanes(source[0], -SZ)
            around = (
                (lower + upper)
                + (pltpu.roll(centre, 1, 0) + pltpu.roll(centre, PITCH - 1, 0))
                + (shift_lanes(centre, 1) + shift_lanes(centre, -1))
            )
            target[j] = (centre * keep_ref[j] + add_ref[j]) + spread_ref[j] * around
        source, target = target, source
    for x in range(CX):
        xd = x + WIDE
        value = shift_lanes(source[xd % PACK], -SZ * (xd // PACK) - WIDE)
        damage_ref[x] = value[WIDE : WIDE + CY, 0:CZ]
    move = pltpu.make_async_copy(damage_ref, damage_hbm, sem)
    move.start()
    fv_ref[...] = jnp.zeros_like(fv_ref)
    fd_ref[...] = jnp.zeros_like(fd_ref)
    vel_at = ROWS_AT[LAYERS]
    lane = lane_index(EY)
    for x in range(EX):
        vel = vel_ref[x, OFF : OFF + EY, :]
        if x < 2:
            vel = vel + before_ref[vel_at + EY * x : vel_at + EY * (x + 1), :]
        if x >= EX - 2:
            at = vel_at + EY * (x - EX + 2)
            vel = vel + after_ref[at : at + EY, :]
        slot, group = (x + OFF) % PACK, (x + OFF) // PACK
        inverse = inverse_ref[slot, OFF : OFF + EY, :]
        vel = three(lane, ZROWS, *(shift_lanes(vel, (ZROWS - SZ) * ch - OFF) for ch in range(3)))
        inverse = three(lane, ZROWS, *(shift_lanes(inverse, ZROWS * ch - SZ * group - OFF) for ch in range(3)))
        fv_ref[EY * x : EY * (x + 1), :] = vel * inverse
        fd_ref[EY * x : EY * (x + 1), :] = shift_lanes(source[slot], -SZ * group - OFF)[OFF : OFF + EY, :]
    nodes = jnp.concatenate([fv_ref[...].T[0 : 3 * ZROWS], fd_ref[...].T[0:ZROWS]], axis=0)
    for corner in range(4):
        shift = (corner >> 1) * EY + (corner & 1)
        value = nodes if shift == 0 else pltpu.roll(nodes, 256 - shift, 1)
        high = value.astype(BF16)
        low = (value - high.astype(F32)).astype(BF16)
        start = 8 * ZROWS * corner
        nodes_ref[start : start + 4 * ZROWS, :] = high
        nodes_ref[start + 4 * ZROWS : start + 8 * ZROWS, :] = low
    for index in range(TAIL // CHUNK):
        gather_update((COUNT - TAIL) // CHUNK + index, nodes_ref, part_ref, base_ref, w_ref, g_ref, rows_ref, index, True)
    for at in range(len(SENT)):
        first = MOST * MOST * (at // MOST) + at % MOST
        tail_ref[MOST * at : MOST * (at + 1), :] = rows_ref[pl.ds(first, MOST, stride=MOST), :]
    move.wait()


def head_kernel(
    counts_ref, prior_ref, nodes_ref, tail_ref, part_ref, base_ref, w_ref, g_ref, out_hbm, head_ref, left_ref, zero_ref, sems
):
    prior = prior_ref[0, 3 * SZ].astype(jnp.int32)
    left = MOST - counts_ref[0]
    zero_ref[...] = jnp.zeros_like(zero_ref)
    blanks = []
    for i in range(MOST):
        to = pl.ds(pl.multiple_of((NBIN + MOST - 1 - i) * BIN, BIN), BIN)
        blanks.append((i < MOST - prior, pltpu.make_async_copy(zero_ref, out_hbm.at[:, to], sems.at[2 + i])))
    for wanted, move in blanks:
        pl.when(wanted)(move.start)
    unpack(tail_ref, left_ref, left)
    to = pl.ds(pl.multiple_of((prior + NBIN - MOST) * BIN, BIN), TAIL)
    own = pltpu.make_async_copy(left_ref, out_hbm.at[:, to], sems.at[0])
    own.start()
    for index in range((COUNT - TAIL) // CHUNK):
        gather_update(index, nodes_ref, part_ref, base_ref, w_ref, g_ref, head_ref, index, False)
    to = pl.ds(pl.multiple_of(prior * BIN, BIN), COUNT - TAIL)
    stay = pltpu.make_async_copy(head_ref, out_hbm.at[:, to], sems.at[1])
    stay.start()
    for wanted, move in blanks:
        pl.when(wanted)(move.wait)
    own.wait()
    stay.wait()


def arrive_kernel(turn, prior_ref, packed_ref, partial_hbm, out_hbm, recv_ref, sems):
    is_far = lax.rem(lax.axis_index(AXES[2]), FAR) == 0

    @pl.when(jnp.logical_not(is_far) if turn else is_far)
    def _():
        prior = prior_ref[0, 3 * SZ].astype(jnp.int32)
        unpack(packed_ref, recv_ref)
        moves = []
        for slot in range(MOST):
            source = pl.ds(pl.multiple_of(jnp.minimum(MOST - prior + slot, MOST - 1) * BIN, BIN), BIN)
            target = out_hbm.at[:, slot * BIN : (slot + 1) * BIN]
            moves.append((slot < prior, pltpu.make_async_copy(recv_ref.at[:, source], target, sems.at[slot])))
        for wanted, move in moves:
            pl.when(wanted)(move.start)
        for wanted, move in moves:
            pl.when(wanted)(move.wait)


def shape(*dims, kind=F32):
    return jax.ShapeDtypeStruct(dims, kind)


SMEM = pltpu.SMEM
HBM = pltpu.HBM


def call(kernel, out_shape, spaces, args, out_spaces=None, scratch=(), flops=0, aliases=None, limit=None):
    leaves = jax.tree.leaves(out_shape)
    out_spaces = out_spaces or [VMEM] * len(leaves)
    out_specs = [pl.BlockSpec(memory_space=s) for s in out_spaces]
    return pl.pallas_call(
        kernel,
        out_shape=out_shape,
        in_specs=[pl.BlockSpec(memory_space=s) for s in spaces],
        out_specs=tuple(out_specs) if isinstance(out_shape, tuple) else out_specs[0],
        scratch_shapes=list(scratch),
        input_output_aliases=aliases or {},
        compiler_params=pltpu.CompilerParams(vmem_limit_bytes=(limit or 48 * 1024) * 1024),
        cost_estimate=pl.CostEstimate(flops=flops, bytes_accessed=2000000, transcendentals=0),
    )(*args)


def swap_pairs(odd, even, axis, extra=()):
    count = lax.axis_size(axis)
    odd_pairs = [(i, i + 1) for i in range(1, count - 1, 2)]
    even_pairs = [(i, i + 1) for i in range(0, count - 1, 2)]
    from_odd = lax.ppermute(odd, axis, odd_pairs + [(j, i) for i, j in odd_pairs] + list(extra))
    return from_odd, lax.ppermute(even, axis, even_pairs + [(j, i) for i, j in even_pairs])


def per_device(particles, stencil_base, weights, gradients, counts):
    sizes = tuple(lax.axis_size(a) for a in AXES)
    inputs = (particles, stencil_base, weights, gradients)
    deep, vel, odd, even = call(
        scatter_kernel,
        (VMEM((GROWS, 128), F32), VMEM((GROWS, 128), F32), VMEM((GROUP, 128), F32), VMEM((GROUP, 128), F32)),
        [SMEM] + [HBM] * 4,
        (counts,) + inputs,
        scratch=[
            VMEM((FIELDS, COUNT), F32),
            VMEM((3, COUNT), jnp.int32),
            VMEM((8, COUNT), F32),
            VMEM((3, 8, COUNT), F32),
            VMEM((4, 2 * HALF, 256), F32),
            VMEM((256, 256), F32),
            VMEM((2, 6, 8, COUNT), F32),
            VMEM((8 * HALF, 2 * COUNT), BF16),
            VMEM((AROWS, COUNT), BF16),
            pltpu.SemaphoreType.DMA((4,)),
        ],
        limit=SCATTER_KIB,
    )
    count_z = sizes[2]
    from_odd, from_even = swap_pairs(odd, even, "gz", [(count_z - 1, 0)])
    message = LAYERS * EX + 2 * EX
    pairs = sizes[1] - 1
    deep, vel, prior, *messages = call(
        lambda *refs: join_z_kernel(pairs, *refs),
        (shape(GROWS, 128), shape(GROWS, 128), shape(8, 128)) + (shape(message, 128),) * pairs,
        [VMEM] * 4,
        (deep, vel, from_odd, from_even),
    )
    received = [lax.ppermute(messages[i], "gy", [(i, i + 1), (i + 1, i)]) for i in range(pairs)]
    wide_message = ROWS_AT[LAYERS] + 2 * EY
    deep, vel, odd, even = call(
        lambda *refs: join_y_kernel(pairs, *refs),
        (shape(EX, PITCH, 128), shape(EX, PITCH, 128), shape(wide_message, 128), shape(wide_message, 128)),
        [VMEM] * (2 + pairs),
        (deep, vel, *received),
        scratch=[VMEM((message, 128), F32)] * 2,
    )
    from_odd, from_even = swap_pairs(odd, even, "gx")

    ring = [(i, (i + 1) % count_z) for i in range(count_z)]
    far = [edge for edge in ring if edge[1] % FAR == 0]
    near = [edge for edge in ring if edge[1] % FAR != 0]
    results = ()
    for turn in range(2):
        results = call(
            lambda *refs, turn=turn: relax_kernel(turn, sizes, *refs),
            (shape(CX, CY, CZ), VMEM((32 * ZROWS, 256), BF16), VMEM((len(SENT) * MOST, BIN), F32)),
            [VMEM] * 8 + [HBM, VMEM, VMEM][: len(results)],
            (deep, vel, from_odd, from_even) + inputs + tuple(results),
            out_spaces=[HBM, VMEM, VMEM],
            scratch=[VMEM((SX, PITCH, 128), F32)]
            + [VMEM((PACK, PITCH, 128), F32)] * 6
            + [VMEM((256, 128), F32)] * 2
            + [VMEM((CX, CY, CZ), F32), VMEM((3 * MOST * MOST, BIN), F32)]
            + [VMEM((wide_message, 128), F32)] * 2
            + [pltpu.SemaphoreType.DMA],
            aliases={8: 0, 9: 1} if turn else {},
        )
        if turn == 0:
            recv_far = lax.ppermute(results[2], "gz", far)
    damage, nodes, tail = results
    recv_near = lax.ppermute(tail, "gz", near)
    own = call(
        head_kernel,
        shape(FIELDS, SLOTS),
        [SMEM] + [VMEM] * 7,
        (counts, prior, nodes, tail) + inputs,
        out_spaces=[HBM],
        scratch=[
            VMEM((FIELDS, COUNT - TAIL), F32),
            VMEM((FIELDS, TAIL), F32),
            VMEM((FIELDS, BIN), F32),
            pltpu.SemaphoreType.DMA((2 + MOST,)),
        ],
        flops=2 * 1280 * 256 * 1024,
    )
    migrated = own
    for turn, recv in enumerate((recv_far, recv_near)):
        migrated = call(
            lambda *refs, turn=turn: arrive_kernel(turn, *refs),
            shape(FIELDS, SLOTS),
            [VMEM, VMEM, HBM],
            (prior, recv, migrated),
            out_spaces=[HBM],
            scratch=[VMEM((FIELDS, TAIL), F32), pltpu.SemaphoreType.DMA((MOST,))],
            aliases={2: 0},
        )
    return (migrated, damage)


def solution(mesh):
    return jax.shard_map(
        per_device,
        mesh=mesh,
        in_specs=(
            P(None, ("gx", "gy", "gz")),
            P(None, ("gx", "gy", "gz")),
            P(None, ("gx", "gy", "gz")),
            P(None, None, ("gx", "gy", "gz")),
            P(("gx", "gy", "gz")),
        ),
        out_specs=(P(None, ("gx", "gy", "gz")), P("gx", "gy", "gz")),
        check_vma=False,
    )
```
